128 devices in a mesh: dp: 16 (over z, y), tensor: 8 (over x, core).
Axes of the slice: x: 4, y: 4, z: 4, core: 2. Of those that a mesh axis runs over, the one named last changes fastest.
Arguments:
- acts: bfloat16 [24576, 6144], P('dp', 'tensor'), may hold values from -600 to 600, as said below
- grads_out: bfloat16 [24576, 24576], P('dp', 'tensor'), may hold values from -600 to 600, as said below
- sketch_in: bfloat16 [6144, 256], P('tensor'), may hold values from -0.078125 to 0.078125
- sketch_out: bfloat16 [24576, 256], P('tensor'), may hold values from -0.0390625 to 0.0390625
- weight_grad: float32 [6144, 24576], P('dp', 'tensor'), may hold values from -6 to 6
Outputs:
- precond: float32 [6144, 24576], P('dp', 'tensor')
The draws below stay inside these ranges and needn't reach their ends.
Inputs may be any that keep to these rules, and one draw needn't show every extreme that they name: acts: rows and columns of varying scale. grads_out: rows and columns of varying scale.
All inputs are finite; a program needn't handle non-finite values.
Results may differ from the reference program's by a relative error of at most 0.0015.
Values sent between devices are 32-bit elements; how exact they have to be, the bound alone decides.
No kernel may reach another device: no remote copies, remote signals or barrier semaphores. Data moves between devices by JAX's collectives and lax.ppermute only.
A program may use at most 128 MiB of HBM per device.

```python
import jax
import jax.numpy as jnp
from jax import lax

D = 6144
FF = 24576
R = 256
TOKENS = 24576


def shape_field(key, noise, rise_rows, rise_cols):
    rows, cols = noise.shape
    keys = jax.random.split(key, 2)
    row_scale = jnp.exp(jax.random.uniform(keys[0], (rows, 1), jnp.float32, -1.2, 1.1))
    col_scale = jnp.exp(jax.random.uniform(keys[1], (1, cols), jnp.float32, -1.2, 1.1))
    row_place = jnp.arange(rows, dtype=jnp.float32)[:, None] / rows
    col_place = jnp.arange(cols, dtype=jnp.float32)[None, :] / cols
    field = noise
    return field * row_scale * col_scale * jnp.sqrt(1.0 + rise_rows * row_place) * jnp.sqrt(1.0 + rise_cols * col_place)


def draw_acts(key, part):
    key = jax.random.fold_in(key, 11)
    noise_key, key = jax.random.split(key)
    noise = jnp.clip(jax.random.normal(noise_key, (TOKENS, D), jnp.float32), -5.0, 5.0)
    return shape_field(key, noise, 2.0, 2.0).astype(jnp.bfloat16)


def draw_grads_out(key, part):
    key = jax.random.fold_in(key, 23)
    noise_key, key = jax.random.split(key)
    noise = jnp.clip(jax.random.normal(noise_key, (TOKENS, FF), jnp.float32), -5.0, 5.0)
    return shape_field(key, noise, 2.0, 2.0).astype(jnp.bfloat16)


def level_of(key, extent, cuts, least, high):
    def one(dim, parts):
        heights = jax.random.uniform(jax.random.fold_in(jax.random.fold_in(key, 6), dim), (parts,), jnp.float32, least / len(cuts), high / len(cuts))
        return jnp.repeat(jnp.exp(heights), extent[dim] // parts).reshape((-1,) + (1,) * (len(extent) - dim - 1))

    loudness = one(*cuts[0])
    for cut in cuts[1:]:
        loudness = loudness * one(*cut)
    return loudness


def bell_draw(own_key, shape, deviation, limit, cuts=(), kind=jnp.bfloat16):
    entries = deviation * jax.random.normal(own_key, shape, jnp.float32)
    if cuts:
        entries = entries * level_of(own_key, shape, cuts, -0.22, 0.18)
    return jnp.clip(entries, -limit, limit).astype(kind)


def setup_inputs(seed: int = 0) -> dict:
    arg_keys = jax.random.split(jax.random.key(seed), 6)
    return {
        "acts": draw_acts(jax.random.fold_in(arg_keys[5], 71), 0),
        "grads_out": draw_grads_out(jax.random.fold_in(arg_keys[5], 71), 0),
        "sketch_in": bell_draw(arg_keys[2], (D, R), D ** -0.5, 0.078125, ((0, 8),)),
        "sketch_out": bell_draw(arg_keys[3], (FF, R), FF ** -0.5, 0.0390625, ((0, 8),)),
        "weight_grad": bell_draw(arg_keys[4], (D, FF), 1.0, 6.0, ((0, 16), (1, 8)), jnp.float32),
    }


DAMPING = 0.1

def transpose_dot(left, right):
    return lax.dot_general(left.astype(jnp.float32), right.astype(jnp.float32), (((0,), (0,)), ((), ())), preferred_element_type=jnp.float32)

def precise_dot(left, right):
    return jnp.dot(left, right, precision=lax.Precision.HIGHEST)

def reference(acts, grads_out, sketch_in, sketch_out, weight_grad):
    full_act = jnp.dot(acts.astype(jnp.float32), sketch_in.astype(jnp.float32), preferred_element_type=jnp.float32)
    full_grad = jnp.dot(grads_out.astype(jnp.float32), sketch_out.astype(jnp.float32), preferred_element_type=jnp.float32)
    sketch_act = full_act.astype(jnp.bfloat16)
    sketch_grad = full_grad.astype(jnp.bfloat16)
    trace_act = jnp.sum(jnp.square(acts.astype(jnp.float32)))
    trace_grad = jnp.sum(jnp.square(grads_out.astype(jnp.float32)))
    damp_act = DAMPING * trace_act / (TOKENS * D)
    damp_grad = DAMPING * trace_grad / (TOKENS * FF)
    range_act = transpose_dot(acts, sketch_act) / TOKENS
    range_grad = transpose_dot(grads_out, sketch_grad) / TOKENS
    core_act = precise_dot(full_act.T, full_act) / TOKENS
    core_grad = precise_dot(full_grad.T, full_grad) / TOKENS
    inner_act = damp_act * core_act + precise_dot(range_act.T, range_act)
    inner_grad = damp_grad * core_grad + precise_dot(range_grad.T, range_grad)
    right_sums = precise_dot(weight_grad, range_grad)
    solved_grad = jax.scipy.linalg.cho_solve((jnp.linalg.cholesky(inner_grad), True), right_sums.T)
    halfway = (weight_grad - precise_dot(solved_grad.T, range_grad.T)) / damp_grad
    left_sums = precise_dot(range_act.T, halfway)
    solved_act = jax.scipy.linalg.cho_solve((jnp.linalg.cholesky(inner_act), True), left_sums)
    return (halfway - precise_dot(range_act, solved_act)) / damp_act
```

```python
import jax
import jax.numpy as jnp
from jax import lax
from jax.sharding import PartitionSpec as P

D = 6144
FF = 24576
R = 256

DAMPING = 0.1


def ring(kind, step):
    if kind == "y":
        return [(i, i // 4 * 4 + (i % 4 + step) % 4) for i in range(16)]
    if kind == "z":
        return [(i, (i // 4 + step) % 4 * 4 + i % 4) for i in range(16)]
    return [(i, (i // 2 + step) % 4 * 2 + i % 2) for i in range(8)]


def send(value, kind, step):
    return lax.ppermute(value, "tensor" if kind == "x" else "dp", ring(kind, step))


def swap_cores(value):
    return lax.ppermute(value, "tensor", [(i, i ^ 1) for i in range(8)])


def place(kind):
    if kind == "y":
        return lax.axis_index("dp") % 4
    if kind == "z":
        return lax.axis_index("dp") // 4
    return lax.axis_index("tensor") // 2


def rows(value, index, count):
    return lax.dynamic_slice_in_dim(value, index * count, count, 0)


def scatter_four(value, kind):
    here, count = place(kind), value.shape[0] // 4
    two, one, three = (
        send(rows(value, (here + step) % 4, count), kind, step) for step in (2, 1, 3)
    )
    return (rows(value, here, count) + two) + (one + three)


def gather_four(value, kind):
    here, count = place(kind), value.shape[0]
    parts = {step: send(value, kind, step) for step in (2, 1, 3)}
    whole = jnp.zeros((4 * count,) + value.shape[1:], value.dtype)
    whole = lax.dynamic_update_slice_in_dim(whole, value, here * count, 0)
    for step in (1, 3, 2):
        whole = lax.dynamic_update_slice_in_dim(
            whole, parts[step], (here - step) % 4 * count, 0
        )
    return whole


def sum_four(value, kind):
    two, one, three = (send(value, kind, step) for step in (2, 1, 3))
    return (value + two) + (one + three)


def scatter_dp(first, second):
    first, second = scatter_four(first, "y"), scatter_four(second, "z")
    return scatter_four(first, "z"), scatter_four(second, "y")


def gather_dp(first, second):
    first, second = gather_four(first, "z"), gather_four(second, "y")
    return gather_four(first, "y"), gather_four(second, "z")


def sum_dp(value):
    return sum_four(sum_four(value, "y"), "z")


def tensor_chunk():
    index = lax.axis_index("tensor")
    return index % 2 * 4 + index // 2


def scatter_tensor(value):
    core, half = lax.axis_index("tensor") % 2, value.shape[0] // 2
    other = swap_cores(rows(value, 1 - core, half))
    return scatter_four(rows(value, core, half) + other, "x")


def gather_tensor(value):
    core = lax.axis_index("tensor") % 2
    value = gather_four(value, "x")
    other = swap_cores(value)
    low = jnp.where(core == 0, value, other)
    high = jnp.where(core == 0, other, value)
    return jnp.concatenate([low, high])


def contract(left, right, dims, precision=lax.Precision.HIGH):
    return lax.dot_general(
        left, right, (dims, ((), ())), precision=precision, preferred_element_type=jnp.float32
    )


def inverse_factor(inner):
    factor = jnp.linalg.cholesky(inner)
    return lax.linalg.triangular_solve(
        factor, jnp.eye(R, dtype=jnp.float32), left_side=True, lower=True
    )


def body(acts, grads_out, sketch_in, sketch_out, weight_grad):
    tokens_all = acts.shape[0] * lax.axis_size("dp")
    chunk = tensor_chunk()
    width = R // 8

    full_grad = gather_tensor(
        scatter_tensor(jnp.dot(grads_out, sketch_out, preferred_element_type=jnp.float32))
    )
    full_act = gather_tensor(
        scatter_tensor(jnp.dot(acts, sketch_in, preferred_element_type=jnp.float32))
    )
    square_grad = jnp.sum(jnp.square(grads_out.astype(jnp.float32)))
    square_act = jnp.sum(jnp.square(acts.astype(jnp.float32)))
    core_grad = contract(full_grad, full_grad, ((0,), (0,))) / tokens_all
    core_act = contract(full_act, full_act, ((0,), (0,))) / tokens_all

    part = contract(full_grad.astype(jnp.bfloat16), grads_out, ((0,), (0,)), None) / tokens_all
    extra = jnp.concatenate(
        [
            rows(core_grad, chunk, width).T,
            jnp.full((R, 1), square_grad),
            jnp.zeros((R, 128 - width - 1), jnp.float32),
        ],
        axis=1,
    )
    part = jnp.concatenate([part, extra], axis=1)
    range_grad = jnp.concatenate(gather_dp(*scatter_dp(part[: R // 2], part[R // 2 :])))
    extra = range_grad[:, 3072:]
    range_grad = range_grad[:, :3072]

    part = contract(acts, full_act.astype(jnp.bfloat16), ((0,), (0,)), None) / tokens_all
    part = part.reshape(4, 4, 2, 24, R)
    first, second = scatter_dp(
        part[:, :, 0].transpose(1, 0, 2, 3).reshape(384, R), part[:, :, 1].reshape(384, R)
    )
    piece = jnp.concatenate([first, second])
    moves = []
    for d in range(16):
        for t in range(8):
            k = d % 8
            moves.append((d * 8 + t, (2 * t + d // 8) * 8 + 2 * (k % 4) + k // 4))
    piece = lax.ppermute(piece, ("dp", "tensor"), moves)
    rows_act = gather_tensor(piece)

    part = contract(rows_act, weight_grad, ((0,), (0,)))
    left_sums = jnp.concatenate(gather_dp(*scatter_dp(part[: R // 2], part[R // 2 :])))

    gram = contract(rows_act, rows_act, ((0,), (0,)))
    small = jnp.concatenate(
        [
            rows(gram, chunk, width),
            rows(core_act, chunk, width),
            jnp.full((8, R), square_act),
        ]
    )
    small = gather_tensor(sum_dp(small)).reshape(8, 72, R)
    gram_act = small[:, :32].reshape(R, R)
    core_act = small[:, 32:64].reshape(R, R)
    damp_act = DAMPING * jnp.sum(small[:, 64, 0]) / (tokens_all * D)
    inverse_act = inverse_factor(damp_act * core_act + gram_act)

    right = contract(weight_grad, range_grad, ((1,), (1,)))
    gram = contract(range_grad, range_grad, ((1,), (1,)))
    part = jnp.concatenate([right.reshape(8, 48, R), gram.reshape(8, 32, R)], axis=1)
    part = scatter_tensor(part.reshape(640, R))
    part = jnp.concatenate(
        [part, extra[:, :width].T, jnp.full((8, R), extra[0, width])]
    )
    part = gather_tensor(part).reshape(8, 120, R)
    right_sums = part[:, :48].reshape(384, R)
    gram_grad = part[:, 48:80].reshape(R, R)
    core_grad = part[:, 80:112].reshape(R, R)
    damp_grad = DAMPING * jnp.sum(part[:, 112, 0]) / (tokens_all * FF)
    inverse_grad = inverse_factor(damp_grad * core_grad + gram_grad)

    both = contract(rows_act, right_sums, ((0,), (0,)))
    both = gather_tensor(sum_dp(rows(both, chunk, width)))

    solved_act = contract(
        contract(rows_act, inverse_act, ((1,), (1,))), inverse_act, ((1,), (0,))
    )
    right_sums = right_sums - contract(solved_act, both, ((1,), (0,)))
    solved_grad = contract(
        contract(right_sums, inverse_grad, ((1,), (1,))), inverse_grad, ((1,), (0,))
    )
    out = weight_grad - contract(solved_grad, range_grad, ((1,), (0,)))
    out = out - contract(solved_act, left_sums, ((1,), (0,)))
    return out / (damp_act * damp_grad)


def solution(mesh):
    return jax.shard_map(
        body,
        mesh=mesh,
        in_specs=(
            P("dp", "tensor"),
            P("dp", "tensor"),
            P("tensor", None),
            P("tensor", None),
            P("dp", "tensor"),
        ),
        out_specs=P("dp", "tensor"),
        check_vma=False,
    )
```

```python
import functools

import jax
import jax.numpy as jnp
from jax import lax
from jax.experimental import pallas as pl
from jax.experimental.pallas import tpu as pltpu
from jax.sharding import PartitionSpec as P

D = 6144
FF = 24576
R = 256
TILE = 512
BLOCK = 64
VMEM_LIMIT = 48 * 1024 * 1024

DAMPING = 0.1


def ring(kind, step):
    if kind == "y":
        return [(i, i // 4 * 4 + (i % 4 + step) % 4) for i in range(16)]
    if kind == "z":
        return [(i, (i // 4 + step) % 4 * 4 + i % 4) for i in range(16)]
    return [(i, (i // 2 + step) % 4 * 2 + i % 2) for i in range(8)]


def send(value, kind, step):
    return lax.ppermute(value, "tensor" if kind == "x" else "dp", ring(kind, step))


def swap_cores(value):
    return lax.ppermute(value, "tensor", [(i, i ^ 1) for i in range(8)])


def place(kind):
    if kind == "y":
        return lax.axis_index("dp") % 4
    if kind == "z":
        return lax.axis_index("dp") // 4
    return lax.axis_index("tensor") // 2


def rows(value, index, count):
    return lax.dynamic_slice_in_dim(value, index * count, count, 0)


def scatter_four(value, kind):
    here, count = place(kind), value.shape[0] // 4
    two, one, three = (
        send(rows(value, (here + step) % 4, count), kind, step) for step in (2, 1, 3)
    )
    return (rows(value, here, count) + two) + (one + three)


def blocks_four(value, kind):
    two, one, three = (send(value, kind, step) for step in (2, 1, 3))
    return value, one, two, three


def gather_four(value, kind):
    here, count = place(kind), value.shape[0]
    parts = blocks_four(value, kind)
    whole = jnp.zeros((4 * count,) + value.shape[1:], value.dtype)
    for step in range(4):
        whole = lax.dynamic_update_slice_in_dim(
            whole, parts[step], (here - step) % 4 * count, 0
        )
    return whole


def sum_four(value, kind):
    own, one, two, three = blocks_four(value, kind)
    return (own + two) + (one + three)


def scatter_dp(value):
    half = value.shape[0] // 2
    first, second = scatter_four(value[:half], "y"), scatter_four(value[half:], "z")
    return scatter_four(first, "z"), scatter_four(second, "y")


def gather_dp(first, second):
    first, second = gather_four(first, "z"), gather_four(second, "y")
    return blocks_four(first, "y") + blocks_four(second, "z")


def block_offsets():
    here = [place("y") - step for step in range(4)] + [place("z") - step for step in range(4)]
    first = [(p % 4) * (R // 8) for p in here[:4]]
    second = [R // 2 + (p % 4) * (R // 8) for p in here[4:]]
    return jnp.stack(first + second).astype(jnp.int32)


def sum_dp(value):
    return sum_four(sum_four(value, "y"), "z")


def tensor_chunk():
    index = lax.axis_index("tensor")
    return index % 2 * 4 + index // 2


def scatter_tensor(value):
    core, half = lax.axis_index("tensor") % 2, value.shape[0] // 2
    other = swap_cores(rows(value, 1 - core, half))
    return scatter_four(rows(value, core, half) + other, "x")


def gather_tensor(value):
    core = lax.axis_index("tensor") % 2
    value = gather_four(value, "x")
    other = swap_cores(value)
    low = jnp.where(core == 0, value, other)
    high = jnp.where(core == 0, other, value)
    return jnp.concatenate([low, high])


def contract(left, right, dims, precision=lax.Precision.HIGH):
    return lax.dot_general(
        left, right, (dims, ((), ())), precision=precision, preferred_element_type=jnp.float32
    )


def split(value):
    high = value.astype(jnp.bfloat16)
    return high, (value - high.astype(jnp.float32)).astype(jnp.bfloat16)


def product(left, right, dims):
    dot = functools.partial(
        lax.dot_general, dimension_numbers=(dims, ((), ())), preferred_element_type=jnp.float32
    )
    (lh, ll), (rh, rl) = left, right
    return dot(lh, rh) + (dot(lh, rl) + dot(ll, rh))


def call(kernel, out_shape, **options):
    return pl.pallas_call(
        kernel,
        out_shape=out_shape,
        compiler_params=pltpu.CompilerParams(vmem_limit_bytes=VMEM_LIMIT),
        **options,
    )


def array(*shape):
    return jax.ShapeDtypeStruct(shape, jnp.float32)


def sketch_kernel(value, sketch, out, squares, total):
    step = pl.program_id(0)

    @pl.when(step == 0)
    def _():
        total[...] = jnp.zeros_like(total)

    tile = value[...]
    out[...] = jnp.dot(tile, sketch[...], preferred_element_type=jnp.float32)
    tile = tile.astype(jnp.float32)
    total[...] += jnp.sum(jnp.square(tile).reshape(-1, 8, tile.shape[1]), axis=0)

    @pl.when(step == pl.num_programs(0) - 1)
    def _():
        squares[...] = jnp.broadcast_to(jnp.sum(total[...], keepdims=True), (8, 128))


def sketch_of(value, sketch):
    count, columns = value.shape
    return call(
        sketch_kernel,
        [array(count, R), array(8, 128)],
        grid=(count // 256,),
        in_specs=[
            pl.BlockSpec((256, columns), lambda i: (i, 0)),
            pl.BlockSpec((columns, R), lambda i: (0, 0)),
        ],
        out_specs=[
            pl.BlockSpec((256, R), lambda i: (i, 0)),
            pl.BlockSpec((8, 128), lambda i: (0, 0)),
        ],
        scratch_shapes=[pltpu.VMEM((8, columns), jnp.float32)],
        name="sketch",
    )(value, sketch)


LAST = ((1,), (1,))
INNER = ((1,), (0,))


def range_grad_kernel(tokens_all, chunk, sketch, grads, square_grad, square_act, out, flipped):
    step = pl.program_id(0)
    columns = grads.shape[1]

    @pl.when(step == 0)
    def _():
        flipped[...] = sketch[...].T

    part = jnp.dot(
        flipped[...].astype(jnp.bfloat16), grads[...], preferred_element_type=jnp.float32
    )
    out[:, pl.ds(pl.multiple_of(step * columns, 128), columns)] = part / tokens_all

    @pl.when(step == pl.num_programs(0) - 1)
    def _():
        some = flipped[pl.ds(pl.multiple_of(chunk[0] * 32, 32), 32), :]
        core = product(split(flipped[...]), split(some), LAST) / tokens_all
        lane = lax.broadcasted_iota(jnp.int32, (R, 96), 1)
        traces = jnp.where(lane == 0, square_grad[0:1, 0:1], 0.0)
        traces = jnp.where(lane == 1, square_act[0:1, 0:1], traces)
        whole = out.shape[1] - 128
        out[:, whole:] = jnp.concatenate([core, traces], axis=1)


def range_grad_of(chunk, sketch, grads, square_grad, square_act, tokens_all):
    count, columns = grads.shape
    grid_spec = pltpu.PrefetchScalarGridSpec(
        num_scalar_prefetch=1,
        grid=(columns // TILE,),
        in_specs=[
            pl.BlockSpec((count, R), lambda j, c: (0, 0)),
            pl.BlockSpec((count, TILE), lambda j, c: (0, j)),
            pl.BlockSpec((8, 128), lambda j, c: (0, 0)),
            pl.BlockSpec((8, 128), lambda j, c: (0, 0)),
        ],
        out_specs=pl.BlockSpec((R, columns + 128), lambda j, c: (0, 0)),
        scratch_shapes=[pltpu.VMEM((R, count), jnp.float32)],
    )
    return call(
        functools.partial(range_grad_kernel, tokens_all),
        array(R, columns + 128),
        grid_spec=grid_spec,
        name="range_grad",
    )(chunk, sketch, grads, square_grad, square_act)


def range_act_kernel(tokens_all, chunk, sketch, acts, after, out, core):
    flipped = sketch[...].T
    part = jnp.dot(flipped.astype(jnp.bfloat16), acts[...], preferred_element_type=jnp.float32)
    out[...] = part.T / tokens_all
    pieces = split(flipped)
    core[...] = product(pieces, pieces, LAST) / tokens_all


def range_act_of(chunk, sketch, acts, after, tokens_all):
    whole = pl.BlockSpec(memory_space=pltpu.VMEM)
    return call(
        functools.partial(range_act_kernel, tokens_all),
        [array(acts.shape[1], R), array(R, R)],
        in_specs=[
            pl.BlockSpec(memory_space=pltpu.SMEM),
            whole,
            whole,
            pl.BlockSpec(memory_space=pl.ANY),
        ],
        out_specs=[whole, whole],
        name="range_act",
    )(chunk, sketch, acts, after)


def left_kernel(chunk, rows_act, weight, out, gram, slice_out, high, low):
    @pl.when(pl.program_id(0) == 0)
    def _():
        flipped = rows_act[...].T
        high[...], low[...] = split(flipped)
        gram_all = product(split(flipped), split(flipped), LAST)
        gram[...] = gram_all
        slice_out[...] = flipped

    out[...] = product((high[...], low[...]), split(weight[...]), INNER)


def left_products(chunk, rows_act, weight):
    count, columns = weight.shape
    grid_spec = pltpu.PrefetchScalarGridSpec(
        num_scalar_prefetch=1,
        grid=(columns // TILE,),
        in_specs=[
            pl.BlockSpec((count, R), lambda j, c: (0, 0)),
            pl.BlockSpec((count, TILE), lambda j, c: (0, j)),
        ],
        out_specs=[
            pl.BlockSpec((R, TILE), lambda j, c: (0, j)),
            pl.BlockSpec((R, R), lambda j, c: (0, 0)),
            pl.BlockSpec((R, count), lambda j, c: (0, 0)),
        ],
        scratch_shapes=[pltpu.VMEM((R, count), jnp.bfloat16)] * 2,
    )
    return call(
        left_kernel,
        [array(R, columns), array(R, R), array(R, count)],
        grid_spec=grid_spec,
        name="left_products",
    )(chunk, rows_act, weight)


def right_kernel(offsets, *refs):
    blocks, extras = refs[:8], refs[8:16]
    weight, whole, extra, sums = refs[16:]

    @pl.when(pl.program_id(0) == 0)
    def _():
        sums[...] = jnp.zeros_like(sums)
        for i, ref in enumerate(extras):
            extra[pl.ds(pl.multiple_of(offsets[i], 32), 32), :] = ref[...]

    for i, ref in enumerate(blocks):
        whole[pl.ds(pl.multiple_of(offsets[i], 32), 32), :] = ref[...]
    ranges = split(whole[...])
    right = product(split(weight[...]), ranges, LAST)
    gram = product(ranges, ranges, LAST)
    for i in range(8):
        sums[i * 80 : i * 80 + 48, :] += right[i * 48 : i * 48 + 48]
        sums[i * 80 + 48 : i * 80 + 80, :] += gram[i * 32 : i * 32 + 32]


def right_products(offsets, blocks, weight):
    count, columns = weight.shape
    grid_spec = pltpu.PrefetchScalarGridSpec(
        num_scalar_prefetch=1,
        grid=(columns // TILE,),
        in_specs=[pl.BlockSpec((32, TILE), lambda j, o: (0, j))] * 8
        + [pl.BlockSpec((32, 128), lambda j, o: (0, columns // 128))] * 8
        + [pl.BlockSpec((count, TILE), lambda j, o: (0, j))],
        out_specs=[
            pl.BlockSpec((R, TILE), lambda j, o: (0, j)),
            pl.BlockSpec((R, 128), lambda j, o: (0, 0)),
            pl.BlockSpec((640, R), lambda j, o: (0, 0)),
        ],
    )
    return call(
        right_kernel,
        [array(R, columns), array(R, 128), array(640, R)],
        grid_spec=grid_spec,
        name="right_products",
    )(offsets, *blocks, *blocks, weight)


def exact(left, right, dims):
    return lax.dot_general(
        left,
        right,
        (dims, ((), ())),
        precision=lax.Precision.HIGHEST,
        preferred_element_type=jnp.float32,
    )


def spread(value):
    return jnp.broadcast_to(value, (8, 2 * BLOCK))


def eliminate(matrices):
    sub = lax.broadcasted_iota(jnp.int32, (8, 2 * BLOCK), 0)
    count = BLOCK // 8
    groups = [[m[8 * i : 8 * i + 8] for i in range(count)] for m in matrices]
    for at in range(count):
        k = 8 * at
        for group in groups:
            tile = group[at]
            lines = [spread(tile[j : j + 1]) for j in range(8)]
            pivot = {
                (j, l): spread(lines[j][:, k + l : k + l + 1])
                for j in range(8)
                for l in range(j, 8)
            }
            scaled, factor = [], {}
            for j in range(8):
                inverse = 1.0 / pivot[j, j]
                scaled.append(lines[j] * inverse)
                for l in range(j + 1, 8):
                    factor[j, l] = pivot[j, l] * inverse
                    for m in range(l, 8):
                        pivot[l, m] = pivot[l, m] - factor[j, l] * pivot[j, m]
                    lines[l] = lines[l] - factor[j, l] * lines[j]
            for i in range(at + 1, count):
                value, sums, columns = group[i], None, []
                for j in range(8):
                    column = spread(value[:, k + j : k + j + 1])
                    for q in range(j):
                        column = column - columns[q] * factor[q, j]
                    columns.append(column)
                    term = column * scaled[j]
                    sums = term if sums is None else sums + term
                group[i] = value - sums
            for j in range(8):
                tile = jnp.where(sub == j, lines[j] * lax.rsqrt(pivot[j, j]), tile)
            group[at] = tile
    return [jnp.concatenate(group, axis=0) for group in groups]


def lower_inverses(work, outs):
    row = lax.broadcasted_iota(jnp.int32, (BLOCK, BLOCK), 0)
    column = lax.broadcasted_iota(jnp.int32, (BLOCK, BLOCK), 1)
    identity = jnp.where(row == column, 1.0, 0.0)
    for low in range(0, R, BLOCK):
        high = low + BLOCK
        done = eliminate(
            [jnp.concatenate([w[low:high, low:high], identity], axis=1) for w in work]
        )
        for w, corner, out in zip(work, done, outs):
            corner = jnp.where(row >= column, corner[:, BLOCK:], 0.0)
            line = exact(corner, w[low:high, :], INNER)
            out[low:high, :] = line[:, R:]
            if high < R:
                w[high:, :] -= exact(line[:, high:R], line, ((0,), (0,)))


def solve_kernel(counts, right, small, rows_act, solved_act, solved_grad, scale, *scratch):
    work, inverses = scratch[:2], scratch[2:4]
    sums, both = scratch[4:]
    trace_grad, trace_act = jnp.zeros((1, 1)), jnp.zeros((1, 1))
    for i in range(8):
        trace_grad += right[i * 120 + 112 : i * 120 + 113, 32:33]
        trace_act += right[i * 120 + 112 : i * 120 + 113, 33:34]
    damp_grad = DAMPING * trace_grad / counts[0]
    damp_act = DAMPING * trace_act / counts[1]
    scale[...] = jnp.broadcast_to(1.0 / (damp_act * damp_grad), (8, 128))
    row = lax.broadcasted_iota(jnp.int32, (R, R), 0)
    column = lax.broadcasted_iota(jnp.int32, (R, R), 1)
    identity = jnp.where(row == column, 1.0, 0.0)
    for w in work:
        w[:, R:] = identity
    for i in range(8):
        at, here = slice(i * 32, i * 32 + 32), i * 96
        both[at, :] = small[here : here + 32, :]
        work[0][at, :R] = damp_act * small[here + 64 : here + 96, :] + small[here + 32 : here + 64, :]
        here = i * 120
        work[1][at, :R] = damp_grad * right[here + 80 : here + 112, :] + right[here + 48 : here + 80, :]
        sums[i * 48 : i * 48 + 48, :] = right[here : here + 48, :]
    lower_inverses(work, inverses)

    def applied(value, inverse):
        pieces = split(inverse)
        value = product(split(value), pieces, LAST)
        return product(split(value), pieces, INNER)

    left = applied(rows_act[...], inverses[0][...])
    solved_act[...] = left
    rest = sums[...] - product(split(left), split(both[...]), INNER)
    solved_grad[...] = applied(rest, inverses[1][...])


def solve(right, small, rows_act, counts):
    whole = pl.BlockSpec(memory_space=pltpu.VMEM)
    count = rows_act.shape[0]
    return call(
        functools.partial(solve_kernel, counts),
        [array(count, R), array(count, R), array(8, 128)],
        in_specs=[whole] * 3,
        out_specs=[whole] * 3,
        scratch_shapes=[pltpu.VMEM((R, 2 * R), jnp.float32)] * 2
        + [pltpu.VMEM((R, R), jnp.float32)] * 2
        + [pltpu.VMEM((count, R), jnp.float32), pltpu.VMEM((R, R), jnp.float32)],
        name="solve",
    )(right, small, rows_act)


def last_kernel(offsets, *refs):
    blocks = refs[:8]
    weight, range_grad, solved_act, solved_grad, scale, out, whole = refs[8:]
    for i, ref in enumerate(blocks):
        whole[pl.ds(pl.multiple_of(offsets[i], 32), 32), :] = ref[...]
    left = product(split(solved_act[...]), split(whole[...]), INNER)
    right = product(split(solved_grad[...]), split(range_grad[...]), INNER)
    out[...] = (weight[...] - left - right) * scale[0:1, 0:1]


def last_update(offsets, blocks, weight, range_grad, solved_act, solved_grad, scale):
    count, columns = weight.shape
    grid_spec = pltpu.PrefetchScalarGridSpec(
        num_scalar_prefetch=1,
        grid=(columns // TILE,),
        in_specs=[pl.BlockSpec((32, TILE), lambda j, o: (0, j))] * 8
        + [
            pl.BlockSpec((count, TILE), lambda j, o: (0, j)),
            pl.BlockSpec((R, TILE), lambda j, o: (0, j)),
            pl.BlockSpec((count, R), lambda j, o: (0, 0)),
            pl.BlockSpec((count, R), lambda j, o: (0, 0)),
            pl.BlockSpec((8, 128), lambda j, o: (0, 0)),
        ],
        out_specs=pl.BlockSpec((count, TILE), lambda j, o: (0, j)),
        scratch_shapes=[pltpu.VMEM((R, TILE), jnp.float32)],
    )
    return call(
        last_kernel, array(count, columns), grid_spec=grid_spec, name="last_update"
    )(offsets, *blocks, weight, range_grad, solved_act, solved_grad, scale)


def body(acts, grads_out, sketch_in, sketch_out, weight_grad):
    tokens_all = acts.shape[0] * lax.axis_size("dp")
    chunk, offsets = tensor_chunk(), block_offsets()
    chunk_ref = chunk.astype(jnp.int32).reshape(1)
    width = R // 8

    part, square_act = sketch_of(acts, sketch_in)
    full_act = lax.psum(part, "tensor")
    part, square_grad = sketch_of(grads_out, sketch_out)
    full_grad = gather_tensor(scatter_tensor(part))

    part = range_grad_of(chunk_ref, full_grad, grads_out, square_grad, square_act, tokens_all)
    first, second = scatter_dp(part)
    blocks = gather_dp(first, second)
    range_grad, extra, part = right_products(offsets, blocks, weight_grad)

    part = scatter_tensor(part)
    part = jnp.concatenate(
        [part, extra[:, :width].T, jnp.pad(extra[:8], ((0, 0), (0, R - 128)))]
    )
    right = gather_tensor(part)
    right_sums = right.reshape(8, 120, R)[:, :48].reshape(-1, R)

    part, core_act = range_act_of(chunk_ref, full_act, acts, first, tokens_all)
    part = lax.all_to_all(part, "dp", 0, 0, tiled=True)
    piece = jnp.sum(part.reshape(16, 48, R), axis=0)
    moves = []
    for d in range(16):
        for t in range(8):
            k = d % 8
            moves.append((d * 8 + t, (2 * t + d // 8) * 8 + 2 * (k % 4) + k // 4))
    piece = lax.ppermute(piece, ("dp", "tensor"), moves)
    rows_act = gather_tensor(piece)

    part, gram_act, flipped = left_products(chunk_ref, rows_act, weight_grad)
    left_blocks = gather_dp(*scatter_dp(part))

    both = contract(rows(flipped, chunk, width), right_sums, INNER)
    small = [both, rows(gram_act, chunk, width), rows(core_act, chunk, width)]
    small = gather_tensor(sum_dp(jnp.concatenate(small)))

    counts = (float(tokens_all * FF), float(tokens_all * D))
    solved_act, solved_grad, scale = solve(right, small, rows_act, counts)
    return last_update(
        offsets, left_blocks, weight_grad, range_grad, solved_act, solved_grad, scale
    )


def solution(mesh):
    return jax.shard_map(
        body,
        mesh=mesh,
        in_specs=(
            P("dp", "tensor"),
            P("dp", "tensor"),
            P("tensor", None),
            P("tensor", None),
            P("dp", "tensor"),
        ),
        out_specs=P("dp", "tensor"),
        check_vma=False,
    )
```

```python
import functools

import jax
import jax.numpy as jnp
from jax import lax
from jax.experimental import pallas as pl
from jax.experimental.pallas import tpu as pltpu
from jax.sharding import PartitionSpec as P

D = 6144
FF = 24576
R = 256
TILE = 512
BLOCK = 64
VMEM_LIMIT = 48 * 1024 * 1024

DAMPING = 0.1


def ring(kind, step):
    if kind == "y":
        return [(i, i // 4 * 4 + (i % 4 + step) % 4) for i in range(16)]
    if kind == "z":
        return [(i, (i // 4 + step) % 4 * 4 + i % 4) for i in range(16)]
    return [(i, (i // 2 + step) % 4 * 2 + i % 2) for i in range(8)]


def send(value, kind, step):
    return lax.ppermute(value, "tensor" if kind == "x" else "dp", ring(kind, step))


def swap_cores(value):
    return lax.ppermute(value, "tensor", [(i, i ^ 1) for i in range(8)])


def place(kind):
    if kind == "y":
        return lax.axis_index("dp") % 4
    if kind == "z":
        return lax.axis_index("dp") // 4
    return lax.axis_index("tensor") // 2


def rows(value, index, count):
    return lax.dynamic_slice_in_dim(value, index * count, count, 0)


def scatter_four(value, kind):
    here, count = place(kind), value.shape[0] // 4
    two, one, three = (
        send(rows(value, (here + step) % 4, count), kind, step) for step in (2, 1, 3)
    )
    return (rows(value, here, count) + two) + (one + three)


def gather_four(value, kind):
    here, count = place(kind), value.shape[0]
    two, one, three = (send(value, kind, step) for step in (2, 1, 3))
    whole = jnp.zeros((4 * count,) + value.shape[1:], value.dtype)
    for step, part in enumerate((value, one, two, three)):
        whole = lax.dynamic_update_slice_in_dim(whole, part, (here - step) % 4 * count, 0)
    return whole


def scatter_dp(value):
    half = value.shape[0] // 2
    first, second = scatter_four(value[:half], "y"), scatter_four(value[half:], "z")
    return jnp.concatenate([scatter_four(first, "z"), scatter_four(second, "y")])


def store_groups(out, columns, value):
    for group in range(R // 8):
        d = group // 2
        to = 16 + d if group % 2 else d % 4 * 4 + d // 4
        out[8 * to : 8 * to + 8, columns] = value[8 * group : 8 * group + 8]


def tensor_chunk():
    index = lax.axis_index("tensor")
    return index % 2 * 4 + index // 2


def scatter_tensor(value):
    core, half = lax.axis_index("tensor") % 2, value.shape[0] // 2
    other = swap_cores(rows(value, 1 - core, half))
    return scatter_four(rows(value, core, half) + other, "x")


def gather_tensor(value):
    core = lax.axis_index("tensor") % 2
    value = gather_four(value, "x")
    other = swap_cores(value)
    low = jnp.where(core == 0, value, other)
    high = jnp.where(core == 0, other, value)
    return jnp.concatenate([low, high])


def split(value):
    high = value.astype(jnp.bfloat16)
    return high, (value - high.astype(jnp.float32)).astype(jnp.bfloat16)


def product(left, right, dims):
    dot = functools.partial(
        lax.dot_general, dimension_numbers=(dims, ((), ())), preferred_element_type=jnp.float32
    )
    (lh, ll), (rh, rl) = left, right
    return dot(lh, rh) + (dot(lh, rl) + dot(ll, rh))


def call(kernel, out_shape, **options):
    return pl.pallas_call(
        kernel,
        out_shape=out_shape,
        compiler_params=pltpu.CompilerParams(vmem_limit_bytes=VMEM_LIMIT),
        **options,
    )


def array(*shape):
    return jax.ShapeDtypeStruct(shape, jnp.float32)


def sketch_kernel(value, sketch, after, out, squares, total):
    step = pl.program_id(0)

    @pl.when(step == 0)
    def _():
        total[...] = jnp.zeros_like(total)

    tile = value[...]
    out[...] = jnp.dot(tile, sketch[...], preferred_element_type=jnp.float32)
    tile = tile.astype(jnp.float32)
    total[...] += jnp.sum(jnp.square(tile).reshape(-1, 8, tile.shape[1]), axis=0)

    @pl.when(step == pl.num_programs(0) - 1)
    def _():
        squares[...] = jnp.broadcast_to(jnp.sum(total[...], keepdims=True), (8, 128))


def sketch_of(value, sketch, after):
    count, columns = value.shape
    return call(
        sketch_kernel,
        [array(count, R), array(8, 128)],
        grid=(count // 256,),
        in_specs=[
            pl.BlockSpec((256, columns), lambda i: (i, 0)),
            pl.BlockSpec((columns, R), lambda i: (0, 0)),
            pl.BlockSpec(memory_space=pl.ANY),
        ],
        out_specs=[
            pl.BlockSpec((256, R), lambda i: (i, 0)),
            pl.BlockSpec((8, 128), lambda i: (0, 0)),
        ],
        scratch_shapes=[pltpu.VMEM((8, columns), jnp.float32)],
        name="sketch",
    )(value, sketch, after)


LAST = ((1,), (1,))
INNER = ((1,), (0,))


def range_grad_kernel(tokens_all, chunk, sketch, grads, square_grad, square_act, out, flipped):
    step = pl.program_id(0)
    columns = grads.shape[1]

    @pl.when(step == 0)
    def _():
        flipped[...] = sketch[...].T

    part = jnp.dot(
        flipped[...].astype(jnp.bfloat16), grads[...], preferred_element_type=jnp.float32
    )
    store_groups(out, pl.ds(pl.multiple_of(step * columns, 128), columns), part / tokens_all)

    @pl.when(step == pl.num_programs(0) - 1)
    def _():
        some = flipped[pl.ds(pl.multiple_of(chunk[0] * 32, 32), 32), :]
        core = product(split(flipped[...]), split(some), LAST) / tokens_all
        lane = lax.broadcasted_iota(jnp.int32, (R, 96), 1)
        traces = jnp.where(lane == 0, square_grad[0:1, 0:1], 0.0)
        traces = jnp.where(lane == 1, square_act[0:1, 0:1], traces)
        whole = out.shape[1] - 128
        store_groups(out, pl.ds(whole, 128), jnp.concatenate([core, traces], axis=1))


def range_grad_of(chunk, sketch, grads, square_grad, square_act, tokens_all):
    count, columns = grads.shape
    grid_spec = pltpu.PrefetchScalarGridSpec(
        num_scalar_prefetch=1,
        grid=(columns // TILE,),
        in_specs=[
            pl.BlockSpec((count, R), lambda j, c: (0, 0)),
            pl.BlockSpec((count, TILE), lambda j, c: (0, j)),
            pl.BlockSpec((8, 128), lambda j, c: (0, 0)),
            pl.BlockSpec((8, 128), lambda j, c: (0, 0)),
        ],
        out_specs=pl.BlockSpec((R, columns + 128), lambda j, c: (0, 0)),
        scratch_shapes=[pltpu.VMEM((R, count), jnp.float32)],
    )
    return call(
        functools.partial(range_grad_kernel, tokens_all),
        array(R, columns + 128),
        grid_spec=grid_spec,
        name="range_grad",
    )(chunk, sketch, grads, square_grad, square_act)


def range_act_kernel(tokens_all, chunk, sketch, acts, after, out, core, flipped):
    flipped[...] = sketch[...].T
    part = jnp.dot(
        flipped[...].astype(jnp.bfloat16), acts[...], preferred_element_type=jnp.float32
    )
    out[...] = part.T / tokens_all
    some = flipped[pl.ds(pl.multiple_of(chunk[0] * 32, 32), 32), :]
    core[:, :32] = product(split(flipped[...]), split(some), LAST) / tokens_all
    core[:, 32:] = jnp.zeros((R, 96), jnp.float32)


def range_act_of(chunk, sketch, acts, after, tokens_all):
    whole = pl.BlockSpec(memory_space=pltpu.VMEM)
    return call(
        functools.partial(range_act_kernel, tokens_all),
        [array(acts.shape[1], R), array(R, 128)],
        in_specs=[
            pl.BlockSpec(memory_space=pltpu.SMEM),
            whole,
            whole,
            pl.BlockSpec(memory_space=pl.ANY),
        ],
        out_specs=[whole, whole],
        scratch_shapes=[pltpu.VMEM((R, acts.shape[0]), jnp.float32)],
        name="range_act",
    )(chunk, sketch, acts, after)


def left_kernel(chunk, rows_act, core, weight, out, flipped, high, low):
    step = pl.program_id(0)
    columns = weight.shape[1]

    @pl.when(step == 0)
    def _():
        flipped[...] = rows_act[...].T
        high[...], low[...] = split(flipped[...])
        some = flipped[pl.ds(pl.multiple_of(chunk[0] * 32, 32), 32), :]
        gram = product((high[...], low[...]), split(some), LAST)
        rest = jnp.concatenate([gram, core[:, :96]], axis=1)
        store_groups(out, pl.ds(out.shape[1] - 128, 128), rest)

    part = product((high[...], low[...]), split(weight[...]), INNER)
    store_groups(out, pl.ds(pl.multiple_of(step * columns, 128), columns), part)


def left_products(chunk, rows_act, core, weight):
    count, columns = weight.shape
    grid_spec = pltpu.PrefetchScalarGridSpec(
        num_scalar_prefetch=1,
        grid=(columns // TILE,),
        in_specs=[
            pl.BlockSpec((count, R), lambda j, c: (0, 0)),
            pl.BlockSpec((R, 128), lambda j, c: (0, 0)),
            pl.BlockSpec((count, TILE), lambda j, c: (0, j)),
        ],
        out_specs=pl.BlockSpec((R, columns + 128), lambda j, c: (0, 0)),
        scratch_shapes=[
            pltpu.VMEM((R, count), jnp.float32),
            pltpu.VMEM((R, count), jnp.bfloat16),
            pltpu.VMEM((R, count), jnp.bfloat16),
        ],
    )
    return call(
        left_kernel, array(R, columns + 128), grid_spec=grid_spec, name="left_products"
    )(chunk, rows_act, core, weight)


def right_kernel(whole, weight, left, sums):
    @pl.when(pl.program_id(0) == 0)
    def _():
        sums[...] = jnp.zeros_like(sums)

    ranges = split(whole[...])
    right = product(split(weight[...]), ranges, LAST)
    gram = product(ranges, ranges, LAST)
    both = product(split(left[...]), ranges, LAST)
    for i in range(8):
        at = i * 88
        sums[at : at + 48, :] += right[i * 48 : i * 48 + 48]
        sums[at + 48 : at + 80, :] += gram[i * 32 : i * 32 + 32]
        sums[at + 80 : at + 82, :] += both[i * 2 : i * 2 + 2]


def right_products(whole, weight, left):
    count, columns = weight.shape
    return call(
        right_kernel,
        array(704, R),
        grid=(columns // TILE,),
        in_specs=[
            pl.BlockSpec((R, TILE), lambda j: (0, j)),
            pl.BlockSpec((count, TILE), lambda j: (0, j)),
            pl.BlockSpec((16, TILE), lambda j: (0, j)),
        ],
        out_specs=pl.BlockSpec((704, R), lambda j: (0, 0)),
        name="right_products",
    )(whole, weight, left)


def pack_kernel(right, out):
    parts = [right[i * 136 + 120 : i * 136 + 136, :] for i in range(8)]
    gram = jnp.concatenate([p[:, :32] for p in parts], axis=1)
    core = jnp.concatenate([p[:, 32:64] for p in parts], axis=1)
    for d in range(16):
        at = 48 * d
        for i in range(8):
            out[at + 2 * i : at + 2 * i + 2, :] = right[i * 136 + 80 : i * 136 + 82, :]
        out[at + 16 : at + 32, :] = gram
        out[at + 32 : at + 48, :] = core


def pack(right):
    whole = pl.BlockSpec(memory_space=pltpu.VMEM)
    return call(
        pack_kernel, array(768, R), in_specs=[whole], out_specs=whole, name="pack"
    )(right)


def exact(left, right, dims):
    return lax.dot_general(
        left,
        right,
        (dims, ((), ())),
        precision=lax.Precision.HIGHEST,
        preferred_element_type=jnp.float32,
    )


def spread(value):
    return jnp.broadcast_to(value, (8, 2 * BLOCK))


def eliminate(matrices):
    sub = lax.broadcasted_iota(jnp.int32, (8, 2 * BLOCK), 0)
    count = BLOCK // 8
    groups = [[m[8 * i : 8 * i + 8] for i in range(count)] for m in matrices]
    for at in range(count):
        k = 8 * at
        for group in groups:
            tile = group[at]
            lines = [spread(tile[j : j + 1]) for j in range(8)]
            pivot = {
                (j, l): spread(lines[j][:, k + l : k + l + 1])
                for j in range(8)
                for l in range(j, 8)
            }
            scaled, factor = [], {}
            for j in range(8):
                inverse = 1.0 / pivot[j, j]
                scaled.append(lines[j] * inverse)
                for l in range(j + 1, 8):
                    factor[j, l] = pivot[j, l] * inverse
                    for m in range(l, 8):
                        pivot[l, m] = pivot[l, m] - factor[j, l] * pivot[j, m]
                    lines[l] = lines[l] - factor[j, l] * lines[j]
            for i in range(at + 1, count):
                value, sums, columns = group[i], None, []
                for j in range(8):
                    column = spread(value[:, k + j : k + j + 1])
                    for q in range(j):
                        column = column - columns[q] * factor[q, j]
                    columns.append(column)
                    term = column * scaled[j]
                    sums = term if sums is None else sums + term
                group[i] = value - sums
            for j in range(8):
                tile = jnp.where(sub == j, lines[j] * lax.rsqrt(pivot[j, j]), tile)
            group[at] = tile
    return [jnp.concatenate(group, axis=0) for group in groups]


def lower_inverses(work, outs):
    row = lax.broadcasted_iota(jnp.int32, (BLOCK, BLOCK), 0)
    column = lax.broadcasted_iota(jnp.int32, (BLOCK, BLOCK), 1)
    identity = jnp.where(row == column, 1.0, 0.0)
    for low in range(0, R, BLOCK):
        high = low + BLOCK
        done = eliminate(
            [jnp.concatenate([w[low:high, low:high], identity], axis=1) for w in work]
        )
        for w, corner, out in zip(work, done, outs):
            corner = jnp.where(row >= column, corner[:, BLOCK:], 0.0)
            line = exact(corner, w[low:high, :], INNER)
            out[low:high, :] = line[:, R:]
            if high < R:
                w[high:, :] -= exact(line[:, high:R], line, ((0,), (0,)))


def solve_kernel(counts, right, small, rows_act, solved_act, solved_grad, scale, *scratch):
    work, inverses = scratch[:2], scratch[2:4]
    sums, both = scratch[4:]
    trace_grad, trace_act = jnp.zeros((1, 1)), jnp.zeros((1, 1))
    for i in range(8):
        at = i * 136 + 120
        trace_grad += right[at : at + 1, 160:161]
        trace_act += right[at : at + 1, 161:162]
    damp_grad = DAMPING * trace_grad / counts[0]
    damp_act = DAMPING * trace_act / counts[1]
    scale[...] = jnp.broadcast_to(1.0 / (damp_act * damp_grad), (8, 128))
    row = lax.broadcasted_iota(jnp.int32, (R, R), 0)
    column = lax.broadcasted_iota(jnp.int32, (R, R), 1)
    identity = jnp.where(row == column, 1.0, 0.0)
    for w in work:
        w[:, R:] = identity
    for i in range(8):
        at, here = slice(i * 32, i * 32 + 32), i * 136
        work[1][at, :R] = damp_grad * right[here + 88 : here + 120, :] + right[here + 48 : here + 80, :]
        sums[i * 48 : i * 48 + 48, :] = right[here : here + 48, :]
    for d in range(16):
        at, here = slice(d * 16, d * 16 + 16), d * 48
        both[at, :] = small[here : here + 16, :]
        work[0][at, :R] = damp_act * small[here + 32 : here + 48, :] + small[here + 16 : here + 32, :]
    lower_inverses(work, inverses)

    def applied(value, inverse):
        pieces = split(inverse)
        value = product(split(value), pieces, LAST)
        return product(split(value), pieces, INNER)

    left = applied(rows_act[...], inverses[0][...])
    solved_act[...] = left
    rest = sums[...] - product(split(left), split(both[...]), INNER)
    solved_grad[...] = applied(rest, inverses[1][...])


def solve(right, small, rows_act, counts):
    whole = pl.BlockSpec(memory_space=pltpu.VMEM)
    count = rows_act.shape[0]
    return call(
        functools.partial(solve_kernel, counts),
        [array(count, R), array(count, R), array(8, 128)],
        in_specs=[whole] * 3,
        out_specs=[whole] * 3,
        scratch_shapes=[pltpu.VMEM((R, 2 * R), jnp.float32)] * 2
        + [pltpu.VMEM((R, R), jnp.float32)] * 2
        + [pltpu.VMEM((count, R), jnp.float32), pltpu.VMEM((R, R), jnp.float32)],
        name="solve",
    )(right, small, rows_act)


def last_kernel(left_sums, weight, range_grad, solved_act, solved_grad, scale, out):
    left = product(split(solved_act[...]), split(left_sums[...]), INNER)
    right = product(split(solved_grad[...]), split(range_grad[...]), INNER)
    out[...] = (weight[...] - left - right) * scale[0:1, 0:1]


def last_update(left_sums, weight, range_grad, solved_act, solved_grad, scale):
    count, columns = weight.shape
    return call(
        last_kernel,
        array(count, columns),
        grid=(columns // TILE,),
        in_specs=[
            pl.BlockSpec((R, TILE), lambda j: (0, j)),
            pl.BlockSpec((count, TILE), lambda j: (0, j)),
            pl.BlockSpec((R, TILE), lambda j: (0, j)),
            pl.BlockSpec((count, R), lambda j: (0, 0)),
            pl.BlockSpec((count, R), lambda j: (0, 0)),
            pl.BlockSpec((8, 128), lambda j: (0, 0)),
        ],
        out_specs=pl.BlockSpec((count, TILE), lambda j: (0, j)),
        name="last_update",
    )(left_sums, weight, range_grad, solved_act, solved_grad, scale)


def body(acts, grads_out, sketch_in, sketch_out, weight_grad):
    tokens_all = acts.shape[0] * lax.axis_size("dp")
    columns = weight_grad.shape[1]
    chunk = tensor_chunk().astype(jnp.int32).reshape(1)
    width = R // 8

    part, square_act = sketch_of(acts, sketch_in, sketch_in)
    full_act = lax.psum(part, "tensor")
    part, square_grad = sketch_of(grads_out, sketch_out, square_act)
    full_grad = gather_tensor(scatter_tensor(part))

    part = range_grad_of(chunk, full_grad, grads_out, square_grad, square_act, tokens_all)
    piece = scatter_dp(part)
    range_grad = lax.all_gather(piece, "dp", axis=0, tiled=True)

    part, core = range_act_of(chunk, full_act, acts, part, tokens_all)
    part = lax.all_to_all(part, "dp", 0, 0, tiled=True)
    piece = jnp.sum(part.reshape(16, 48, R), axis=0)
    moves = []
    for d in range(16):
        for t in range(8):
            k = d % 8
            moves.append((d * 8 + t, (2 * t + d // 8) * 8 + 2 * (k % 4) + k // 4))
    piece = lax.ppermute(piece, ("dp", "tensor"), moves)
    rows_act = gather_tensor(piece)

    piece = scatter_dp(left_products(chunk, rows_act, core, weight_grad))
    left_sums = lax.all_gather(piece, "dp", axis=0, tiled=True)

    part = scatter_tensor(right_products(range_grad, weight_grad, piece))
    extra = range_grad[:, columns:]
    rest = jnp.concatenate([piece[:, columns:], extra[:16]], axis=1)
    right = gather_tensor(jnp.concatenate([part, extra[:, :width].T, rest]))
    small = lax.all_to_all(pack(right), "dp", 0, 0, tiled=True)

    counts = (float(tokens_all * FF), float(tokens_all * D))
    solved_act, solved_grad, scale = solve(right, small, rows_act, counts)
    return last_update(left_sums, weight_grad, range_grad, solved_act, solved_grad, scale)


def solution(mesh):
    return jax.shard_map(
        body,
        mesh=mesh,
        in_specs=(
            P("dp", "tensor"),
            P("dp", "tensor"),
            P("tensor", None),
            P("tensor", None),
            P("dp", "tensor"),
        ),
        out_specs=P("dp", "tensor"),
        check_vma=False,
    )
```

```python
import functools

import jax
import jax.numpy as jnp
from jax import lax
from jax.experimental import pallas as pl
from jax.experimental.pallas import tpu as pltpu
from jax.sharding import PartitionSpec as P

D = 6144
FF = 24576
R = 256
TILE = 512
BLOCK = 64
VMEM_LIMIT = 48 * 1024 * 1024

DAMPING = 0.1


def ring(kind, step):
    if kind == "y":
        return [(i, i // 4 * 4 + (i % 4 + step) % 4) for i in range(16)]
    if kind == "z":
        return [(i, (i // 4 + step) % 4 * 4 + i % 4) for i in range(16)]
    return [(i, (i // 2 + step) % 4 * 2 + i % 2) for i in range(8)]


def send(value, kind, step):
    return lax.ppermute(value, "tensor" if kind == "x" else "dp", ring(kind, step))


def swap_cores(value):
    return lax.ppermute(value, "tensor", [(i, i ^ 1) for i in range(8)])


def place(kind):
    if kind == "y":
        return lax.axis_index("dp") % 4
    if kind == "z":
        return lax.axis_index("dp") // 4
    return lax.axis_index("tensor") // 2


def rows(value, index, count):
    return lax.dynamic_slice_in_dim(value, index * count, count, 0)


def scatter_four(value, kind):
    here, count = place(kind), value.shape[0] // 4
    two, one, three = (
        send(rows(value, (here + step) % 4, count), kind, step) for step in (2, 1, 3)
    )
    return (rows(value, here, count) + two) + (one + three)


def gather_four(value, kind):
    here, count = place(kind), value.shape[0]
    two, one, three = (send(value, kind, step) for step in (2, 1, 3))
    whole = jnp.zeros((4 * count,) + value.shape[1:], value.dtype)
    for step, part in enumerate((value, one, two, three)):
        whole = lax.dynamic_update_slice_in_dim(whole, part, (here - step) % 4 * count, 0)
    return whole


def scatter_dp(value):
    half = value.shape[0] // 2
    first, second = scatter_four(value[:half], "y"), scatter_four(value[half:], "z")
    return jnp.concatenate([scatter_four(first, "z"), scatter_four(second, "y")])


def store_groups(out, columns, value):
    for group in range(R // 8):
        d = group // 2
        to = 16 + d if group % 2 else d % 4 * 4 + d // 4
        out[8 * to : 8 * to + 8, columns] = value[8 * group : 8 * group + 8]


def tensor_chunk():
    index = lax.axis_index("tensor")
    return index % 2 * 4 + index // 2


def scatter_tensor(value):
    core, half = lax.axis_index("tensor") % 2, value.shape[0] // 2
    other = swap_cores(rows(value, 1 - core, half))
    return scatter_four(rows(value, core, half) + other, "x")


def gather_tensor(value):
    core = lax.axis_index("tensor") % 2
    value = gather_four(value, "x")
    other = swap_cores(value)
    low = jnp.where(core == 0, value, other)
    high = jnp.where(core == 0, other, value)
    return jnp.concatenate([low, high])


def split(value):
    high = value.astype(jnp.bfloat16)
    return high, (value - high.astype(jnp.float32)).astype(jnp.bfloat16)


def product(left, right, dims):
    (lh, ll), (rh, rl) = left, right
    (along_left,), (along_right,) = dims
    return lax.dot_general(
        jnp.concatenate([lh, lh, ll], axis=along_left),
        jnp.concatenate([rh, rl, rh], axis=along_right),
        (dims, ((), ())),
        preferred_element_type=jnp.float32,
    )


def call(kernel, out_shape, **options):
    return pl.pallas_call(
        kernel,
        out_shape=out_shape,
        compiler_params=pltpu.CompilerParams(vmem_limit_bytes=VMEM_LIMIT),
        **options,
    )


def array(*shape):
    return jax.ShapeDtypeStruct(shape, jnp.float32)


def sketch_kernel(grads, acts, sketch_out, sketch_in, out, squares, total_grad, total_act):
    step = pl.program_id(0)
    some = zip((grads, acts), (sketch_out, sketch_in), (total_grad, total_act))
    for i, (value, sketch, total) in enumerate(some):

        @pl.when(step == 0)
        def _():
            total[...] = jnp.zeros_like(total)

        tile = value[...]
        out[:, i * R : i * R + R] = jnp.dot(
            tile, sketch[...], preferred_element_type=jnp.float32
        )
        tile = tile.astype(jnp.float32)
        total[...] += jnp.sum(jnp.square(tile).reshape(-1, 8, tile.shape[1]), axis=0)

        @pl.when(step == pl.num_programs(0) - 1)
        def _():
            whole = jnp.sum(total[...], keepdims=True)
            squares[8 * i : 8 * i + 8, :] = jnp.broadcast_to(whole, (8, 128))


def sketches(grads, acts, sketch_out, sketch_in):
    count = grads.shape[0]
    step = 512
    tile = lambda columns: pl.BlockSpec((step, columns), lambda i: (i, 0))
    whole = lambda value: pl.BlockSpec(value.shape, lambda i: (0, 0))
    return call(
        sketch_kernel,
        [array(count, 2 * R), array(16, 128)],
        grid=(count // step,),
        in_specs=[
            tile(grads.shape[1]),
            tile(acts.shape[1]),
            whole(sketch_out),
            whole(sketch_in),
        ],
        out_specs=[tile(2 * R), pl.BlockSpec((16, 128), lambda i: (0, 0))],
        scratch_shapes=[
            pltpu.VMEM((8, grads.shape[1]), jnp.float32),
            pltpu.VMEM((8, acts.shape[1]), jnp.float32),
        ],
        name="sketches",
    )(grads, acts, sketch_out, sketch_in)


LAST = ((1,), (1,))
INNER = ((1,), (0,))


def range_grad_kernel(tokens_all, chunk, sketch, grads, squares, out, flipped, rounded):
    step = pl.program_id(0)
    columns = grads.shape[1]

    @pl.when(step == 0)
    def _():
        flipped[...] = sketch[...].T
        rounded[...] = flipped[...].astype(jnp.bfloat16)

    part = jnp.dot(rounded[...], grads[...], preferred_element_type=jnp.float32)
    store_groups(out, pl.ds(pl.multiple_of(step * columns, 128), columns), part / tokens_all)

    @pl.when(step == pl.num_programs(0) - 1)
    def _():
        some = flipped[pl.ds(pl.multiple_of(chunk[0] * 32, 32), 32), :]
        core = product(split(flipped[...]), split(some), LAST) / tokens_all
        lane = lax.broadcasted_iota(jnp.int32, (R, 96), 1)
        traces = jnp.where(lane == 0, squares[0:1, 0:1], 0.0)
        traces = jnp.where(lane == 1, squares[8:9, 0:1], traces)
        whole = out.shape[1] - 128
        store_groups(out, pl.ds(whole, 128), jnp.concatenate([core, traces], axis=1))


def range_grad_of(chunk, sketch, grads, squares, tokens_all):
    count, columns = grads.shape
    grid_spec = pltpu.PrefetchScalarGridSpec(
        num_scalar_prefetch=1,
        grid=(columns // TILE,),
        in_specs=[
            pl.BlockSpec((count, R), lambda j, c: (0, 0)),
            pl.BlockSpec((count, TILE), lambda j, c: (0, j)),
            pl.BlockSpec((16, 128), lambda j, c: (0, 0)),
        ],
        out_specs=pl.BlockSpec((R, columns + 128), lambda j, c: (0, 0)),
        scratch_shapes=[
            pltpu.VMEM((R, count), jnp.float32),
            pltpu.VMEM((R, count), jnp.bfloat16),
        ],
    )
    return call(
        functools.partial(range_grad_kernel, tokens_all),
        array(R, columns + 128),
        grid_spec=grid_spec,
        name="range_grad",
    )(chunk, sketch, grads, squares)


def range_act_kernel(tokens_all, chunk, sketch, acts, out, core, flipped):
    flipped[...] = sketch[...].T
    part = jnp.dot(
        flipped[...].astype(jnp.bfloat16), acts[...], preferred_element_type=jnp.float32
    )
    out[...] = part.T / tokens_all
    some = flipped[pl.ds(pl.multiple_of(chunk[0] * 32, 32), 32), :]
    core[:, :32] = product(split(flipped[...]), split(some), LAST) / tokens_all
    core[:, 32:] = jnp.zeros((R, 96), jnp.float32)


def range_act_of(chunk, sketch, acts, tokens_all):
    count, columns = acts.shape
    grid_spec = pltpu.PrefetchScalarGridSpec(
        num_scalar_prefetch=1,
        grid=(1,),
        in_specs=[
            pl.BlockSpec((count, R), lambda j, c: (0, 1)),
            pl.BlockSpec((count, columns), lambda j, c: (0, 0)),
        ],
        out_specs=[
            pl.BlockSpec((columns, R), lambda j, c: (0, 0)),
            pl.BlockSpec((R, 128), lambda j, c: (0, 0)),
        ],
        scratch_shapes=[pltpu.VMEM((R, count), jnp.float32)],
    )
    return call(
        functools.partial(range_act_kernel, tokens_all),
        [array(columns, R), array(R, 128)],
        grid_spec=grid_spec,
        name="range_act",
    )(chunk, sketch, acts)


def left_kernel(chunk, rows_act, core, weight, out, flipped, high, low):
    step = pl.program_id(0)
    columns = weight.shape[1]

    @pl.when(step == 0)
    def _():
        flipped[...] = rows_act[...].T
        high[...], low[...] = split(flipped[...])
        some = flipped[pl.ds(pl.multiple_of(chunk[0] * 32, 32), 32), :]
        gram = product((high[...], low[...]), split(some), LAST)
        rest = jnp.concatenate([gram, core[:, :96]], axis=1)
        store_groups(out, pl.ds(out.shape[1] - 128, 128), rest)

    part = product((high[...], low[...]), split(weight[...]), INNER)
    store_groups(out, pl.ds(pl.multiple_of(step * columns, 128), columns), part)


def left_products(chunk, rows_act, core, weight):
    count, columns = weight.shape
    grid_spec = pltpu.PrefetchScalarGridSpec(
        num_scalar_prefetch=1,
        grid=(columns // TILE,),
        in_specs=[
            pl.BlockSpec((count, R), lambda j, c: (0, 0)),
            pl.BlockSpec((R, 128), lambda j, c: (0, 0)),
            pl.BlockSpec((count, TILE), lambda j, c: (0, j)),
        ],
        out_specs=pl.BlockSpec((R, columns + 128), lambda j, c: (0, 0)),
        scratch_shapes=[
            pltpu.VMEM((R, count), jnp.float32),
            pltpu.VMEM((R, count), jnp.bfloat16),
            pltpu.VMEM((R, count), jnp.bfloat16),
        ],
    )
    return call(
        left_kernel, array(R, columns + 128), grid_spec=grid_spec, name="left_products"
    )(chunk, rows_act, core, weight)


def right_kernel(whole, weight, left, sums):
    @pl.when(pl.program_id(0) == 0)
    def _():
        sums[...] = jnp.zeros_like(sums)

    ranges = split(whole[...])
    right = product(split(weight[...]), ranges, LAST)
    gram = product(ranges, ranges, LAST)
    both = product(split(left[...]), ranges, LAST)
    for i in range(8):
        at = i * 88
        sums[at : at + 48, :] += right[i * 48 : i * 48 + 48]
        sums[at + 48 : at + 80, :] += gram[i * 32 : i * 32 + 32]
        sums[at + 80 : at + 82, :] += both[i * 2 : i * 2 + 2]


def right_products(whole, weight, left):
    count, columns = weight.shape
    return call(
        right_kernel,
        array(704, R),
        grid=(columns // TILE,),
        in_specs=[
            pl.BlockSpec((R, TILE), lambda j: (0, j)),
            pl.BlockSpec((count, TILE), lambda j: (0, j)),
            pl.BlockSpec((16, TILE), lambda j: (0, j)),
        ],
        out_specs=pl.BlockSpec((704, R), lambda j: (0, 0)),
        name="right_products",
    )(whole, weight, left)


def pack_kernel(right, out):
    parts = [right[i * 136 + 120 : i * 136 + 136, :] for i in range(8)]
    gram = jnp.concatenate([p[:, :32] for p in parts], axis=1)
    core = jnp.concatenate([p[:, 32:64] for p in parts], axis=1)
    for d in range(16):
        at = 48 * d
        for i in range(8):
            out[at + 2 * i : at + 2 * i + 2, :] = right[i * 136 + 80 : i * 136 + 82, :]
        out[at + 16 : at + 32, :] = gram
        out[at + 32 : at + 48, :] = core


def pack(right):
    whole = pl.BlockSpec(memory_space=pltpu.VMEM)
    return call(
        pack_kernel, array(768, R), in_specs=[whole], out_specs=whole, name="pack"
    )(right)


def exact(left, right, dims):
    return lax.dot_general(
        left,
        right,
        (dims, ((), ())),
        precision=lax.Precision.HIGHEST,
        preferred_element_type=jnp.float32,
    )


def spread(value):
    return jnp.broadcast_to(value, (8, 2 * BLOCK))


def eliminate(matrices):
    sub = lax.broadcasted_iota(jnp.int32, (8, 2 * BLOCK), 0)
    count = BLOCK // 8
    groups = [[m[8 * i : 8 * i + 8] for i in range(count)] for m in matrices]
    for at in range(count):
        k = 8 * at
        for group in groups:
            tile = group[at]
            lines = [spread(tile[j : j + 1]) for j in range(8)]
            pivot = {
                (j, l): spread(lines[j][:, k + l : k + l + 1])
                for j in range(8)
                for l in range(j, 8)
            }
            scaled, factor = [], {}
            for j in range(8):
                inverse = 1.0 / pivot[j, j]
                scaled.append(lines[j] * inverse)
                for l in range(j + 1, 8):
                    factor[j, l] = pivot[j, l] * inverse
                    for m in range(l, 8):
                        pivot[l, m] = pivot[l, m] - factor[j, l] * pivot[j, m]
                    lines[l] = lines[l] - factor[j, l] * lines[j]
            for i in range(at + 1, count):
                value, sums, columns = group[i], None, []
                for j in range(8):
                    column = spread(value[:, k + j : k + j + 1])
                    for q in range(j):
                        column = column - columns[q] * factor[q, j]
                    columns.append(column)
                    term = column * scaled[j]
                    sums = term if sums is None else sums + term
                group[i] = value - sums
            for j in range(8):
                tile = jnp.where(sub == j, lines[j] * lax.rsqrt(pivot[j, j]), tile)
            group[at] = tile
    return [jnp.concatenate(group, axis=0) for group in groups]


def lower_inverses(work, outs):
    row = lax.broadcasted_iota(jnp.int32, (BLOCK, BLOCK), 0)
    column = lax.broadcasted_iota(jnp.int32, (BLOCK, BLOCK), 1)
    identity = jnp.where(row == column, 1.0, 0.0)
    for low in range(0, R, BLOCK):
        high = low + BLOCK
        done = eliminate(
            [jnp.concatenate([w[low:high, low:high], identity], axis=1) for w in work]
        )
        for w, corner, out in zip(work, done, outs):
            corner = jnp.where(row >= column, corner[:, BLOCK:], 0.0)
            line = exact(corner, w[low:high, :], INNER)
            out[low:high, :] = line[:, R:]
            if high < R:
                w[high:, :] -= exact(line[:, high:R], line, ((0,), (0,)))


def solve_kernel(counts, right, small, rows_act, solved_act, solved_grad, scale, *scratch):
    work, inverses = scratch[:2], scratch[2:4]
    sums, both = scratch[4:]
    trace_grad, trace_act = jnp.zeros((1, 1)), jnp.zeros((1, 1))
    for i in range(8):
        at = i * 136 + 120
        trace_grad += right[at : at + 1, 160:161]
        trace_act += right[at : at + 1, 161:162]
    damp_grad = DAMPING * trace_grad / counts[0]
    damp_act = DAMPING * trace_act / counts[1]
    scale[...] = jnp.broadcast_to(1.0 / (damp_act * damp_grad), (8, 128))
    row = lax.broadcasted_iota(jnp.int32, (R, R), 0)
    column = lax.broadcasted_iota(jnp.int32, (R, R), 1)
    identity = jnp.where(row == column, 1.0, 0.0)
    for w in work:
        w[:, R:] = identity
    for i in range(8):
        at, here = slice(i * 32, i * 32 + 32), i * 136
        work[1][at, :R] = damp_grad * right[here + 88 : here + 120, :] + right[here + 48 : here + 80, :]
        sums[i * 48 : i * 48 + 48, :] = right[here : here + 48, :]
    for d in range(16):
        at, here = slice(d * 16, d * 16 + 16), d * 48
        both[at, :] = small[here : here + 16, :]
        work[0][at, :R] = damp_act * small[here + 32 : here + 48, :] + small[here + 16 : here + 32, :]
    lower_inverses(work, inverses)

    def applied(value, inverse):
        pieces = split(inverse)
        value = product(split(value), pieces, LAST)
        return product(split(value), pieces, INNER)

    left = applied(rows_act[...], inverses[0][...])
    solved_act[...] = left
    rest = sums[...] - product(split(left), split(both[...]), INNER)
    solved_grad[...] = applied(rest, inverses[1][...])


def solve(right, small, rows_act, counts):
    whole = pl.BlockSpec(memory_space=pltpu.VMEM)
    count = rows_act.shape[0]
    return call(
        functools.partial(solve_kernel, counts),
        [array(count, R), array(count, R), array(8, 128)],
        in_specs=[whole] * 3,
        out_specs=[whole] * 3,
        scratch_shapes=[pltpu.VMEM((R, 2 * R), jnp.float32)] * 2
        + [pltpu.VMEM((R, R), jnp.float32)] * 2
        + [pltpu.VMEM((count, R), jnp.float32), pltpu.VMEM((R, R), jnp.float32)],
        name="solve",
    )(right, small, rows_act)


def last_kernel(left_sums, weight, range_grad, solved_act, solved_grad, scale, out):
    left = product(split(solved_act[...]), split(left_sums[...]), INNER)
    right = product(split(solved_grad[...]), split(range_grad[...]), INNER)
    out[...] = (weight[...] - left - right) * scale[0:1, 0:1]


def last_update(left_sums, weight, range_grad, solved_act, solved_grad, scale):
    count, columns = weight.shape
    return call(
        last_kernel,
        array(count, columns),
        grid=(columns // TILE,),
        in_specs=[
            pl.BlockSpec((R, TILE), lambda j: (0, j)),
            pl.BlockSpec((count, TILE), lambda j: (0, j)),
            pl.BlockSpec((R, TILE), lambda j: (0, j)),
            pl.BlockSpec((count, R), lambda j: (0, 0)),
            pl.BlockSpec((count, R), lambda j: (0, 0)),
            pl.BlockSpec((8, 128), lambda j: (0, 0)),
        ],
        out_specs=pl.BlockSpec((count, TILE), lambda j: (0, j)),
        name="last_update",
    )(left_sums, weight, range_grad, solved_act, solved_grad, scale)


def body(acts, grads_out, sketch_in, sketch_out, weight_grad):
    tokens_all = acts.shape[0] * lax.axis_size("dp")
    columns = weight_grad.shape[1]
    chunk = tensor_chunk().astype(jnp.int32).reshape(1)
    width = R // 8

    part, squares = sketches(grads_out, acts, sketch_out, sketch_in)
    full = gather_tensor(scatter_tensor(part))

    part, core = range_act_of(chunk, full, acts, tokens_all)
    part = lax.all_to_all(part, "dp", 0, 0, tiled=True)
    piece = jnp.sum(part.reshape(16, 48, R), axis=0)
    moves = []
    for d in range(16):
        for t in range(8):
            k = d % 8
            moves.append((d * 8 + t, (2 * t + d // 8) * 8 + 2 * (k % 4) + k // 4))
    piece = lax.ppermute(piece, ("dp", "tensor"), moves)
    rows_act = gather_tensor(piece)

    part = range_grad_of(chunk, full, grads_out, squares, tokens_all)
    piece = scatter_dp(part)
    range_grad = lax.all_gather(piece, "dp", axis=0, tiled=True)

    piece = scatter_dp(left_products(chunk, rows_act, core, weight_grad))
    left_sums = lax.all_gather(piece, "dp", axis=0, tiled=True)

    part = scatter_tensor(right_products(range_grad, weight_grad, piece))
    extra = range_grad[:, columns:]
    rest = jnp.concatenate([piece[:, columns:], extra[:16]], axis=1)
    right = gather_tensor(jnp.concatenate([part, extra[:, :width].T, rest]))
    small = lax.all_to_all(pack(right), "dp", 0, 0, tiled=True)

    counts = (float(tokens_all * FF), float(tokens_all * D))
    solved_act, solved_grad, scale = solve(right, small, rows_act, counts)
    return last_update(left_sums, weight_grad, range_grad, solved_act, solved_grad, scale)


def solution(mesh):
    return jax.shard_map(
        body,
        mesh=mesh,
        in_specs=(
            P("dp", "tensor"),
            P("dp", "tensor"),
            P("tensor", None),
            P("tensor", None),
            P("dp", "tensor"),
        ),
        out_specs=P("dp", "tensor"),
        check_vma=False,
    )
```

```python
import functools

import jax
import jax.numpy as jnp
from jax import lax
from jax.experimental import pallas as pl
from jax.experimental.pallas import tpu as pltpu
from jax.sharding import PartitionSpec as P

D = 6144
FF = 24576
R = 256
TILE = 512
BLOCK = 64
VMEM_LIMIT = 60 * 1024 * 1024

DAMPING = 0.1


def ring(kind, step):
    if kind == "y":
        return [(i, i // 4 * 4 + (i % 4 + step) % 4) for i in range(16)]
    if kind == "z":
        return [(i, (i // 4 + step) % 4 * 4 + i % 4) for i in range(16)]
    return [(i, (i // 2 + step) % 4 * 2 + i % 2) for i in range(8)]


def send(value, kind, step):
    return lax.ppermute(value, "tensor" if kind == "x" else "dp", ring(kind, step))


def swap_cores(value):
    return lax.ppermute(value, "tensor", [(i, i ^ 1) for i in range(8)])


def place(kind):
    if kind == "y":
        return lax.axis_index("dp") % 4
    if kind == "z":
        return lax.axis_index("dp") // 4
    return lax.axis_index("tensor") // 2


def rows(value, index, count):
    return lax.dynamic_slice_in_dim(value, index * count, count, 0)


def scatter_four(value, kind):
    here, count = place(kind), value.shape[0] // 4
    two, one, three = (
        send(rows(value, (here + step) % 4, count), kind, step) for step in (2, 1, 3)
    )
    return (rows(value, here, count) + two) + (one + three)


def gather_four(value, kind):
    here, count = place(kind), value.shape[0]
    two, one, three = (send(value, kind, step) for step in (2, 1, 3))
    whole = jnp.zeros((4 * count,) + value.shape[1:], value.dtype)
    for step, part in enumerate((value, one, two, three)):
        whole = lax.dynamic_update_slice_in_dim(whole, part, (here - step) % 4 * count, 0)
    return whole


def scatter_dp(first, second):
    first, second = scatter_four(first, "y"), scatter_four(second, "z")
    return jnp.concatenate([scatter_four(first, "z"), scatter_four(second, "y")])


def scatter_dp_after(first, second, after):
    halves = []
    for value, kind in ((first, "y"), (second, "z")):
        here, count = place(kind), value.shape[0] // 4
        parts = [
            send(rows(value, (here + step) % 4, count), kind, step) for step in (2, 1, 3)
        ]
        halves.append(sum_blocks(here, value, parts, after))
    return jnp.concatenate([scatter_four(halves[0], "z"), scatter_four(halves[1], "y")])


def sum_kernel(here, value, two, one, three, after, out):
    out[...] = (value[...] + two[...]) + (one[...] + three[...])


def sum_blocks(here, value, parts, after):
    count, columns = parts[0].shape
    whole = pl.BlockSpec((count, columns), lambda i, h: (0, 0))
    grid_spec = pltpu.PrefetchScalarGridSpec(
        num_scalar_prefetch=1,
        grid=(1,),
        in_specs=[pl.BlockSpec((count, columns), lambda i, h: (h[0], 0))]
        + [whole] * 3
        + [pl.BlockSpec(memory_space=pl.ANY)],
        out_specs=whole,
    )
    return call(sum_kernel, array(count, columns), grid_spec=grid_spec, name="sum_blocks")(
        here.astype(jnp.int32).reshape(1), value, *parts, after
    )


def store_groups(first, second, columns, value):
    for d in range(16):
        to = d % 4 * 4 + d // 4
        first[8 * to : 8 * to + 8, columns] = value[16 * d : 16 * d + 8]
        second[8 * d : 8 * d + 8, columns] = value[16 * d + 8 : 16 * d + 16]


def tensor_chunk():
    index = lax.axis_index("tensor")
    return index % 2 * 4 + index // 2


def scatter_tensor(value):
    core, half = lax.axis_index("tensor") % 2, value.shape[0] // 2
    other = swap_cores(rows(value, 1 - core, half))
    return scatter_four(rows(value, core, half) + other, "x")


def gather_tensor(value):
    core = lax.axis_index("tensor") % 2
    value = gather_four(value, "x")
    other = swap_cores(value)
    low = jnp.where(core == 0, value, other)
    high = jnp.where(core == 0, other, value)
    return jnp.concatenate([low, high])


def split(value):
    high = value.astype(jnp.bfloat16)
    return high, (value - high.astype(jnp.float32)).astype(jnp.bfloat16)


def product(left, right, dims):
    (lh, ll), (rh, rl) = left, right
    (along_left,), (along_right,) = dims
    return lax.dot_general(
        jnp.concatenate([lh, lh, ll], axis=along_left),
        jnp.concatenate([rh, rl, rh], axis=along_right),
        (dims, ((), ())),
        preferred_element_type=jnp.float32,
    )


def call(kernel, out_shape, **options):
    return pl.pallas_call(
        kernel,
        out_shape=out_shape,
        compiler_params=pltpu.CompilerParams(vmem_limit_bytes=VMEM_LIMIT),
        **options,
    )


def array(*shape):
    return jax.ShapeDtypeStruct(shape, jnp.float32)


def sketch_kernel(core, grads, acts, sketch_out, sketch_in, out, squares, total_grad, total_act):
    step = pl.program_id(0)
    some = zip((grads, acts), (sketch_out, sketch_in), (total_grad, total_act))
    for i, (value, sketch, total) in enumerate(some):

        @pl.when(step == 0)
        def _():
            total[...] = jnp.zeros_like(total)

        tile = value[...]
        out[:, i * R : i * R + R] = jnp.dot(
            tile, sketch[...], preferred_element_type=jnp.float32
        )
        tile = tile.astype(jnp.float32)
        total[...] += jnp.sum(jnp.square(tile).reshape(-1, 8, tile.shape[1]), axis=0)

        @pl.when(step == pl.num_programs(0) - 1)
        def _():
            whole = jnp.sum(total[...], keepdims=True)
            squares[8 * i : 8 * i + 8, :] = jnp.broadcast_to(whole, (8, 128))


def sketches(half, grads, acts, sketch_out, sketch_in):
    count = grads.shape[0] // 2
    step = 384
    steps = count // step
    tile = lambda columns: pl.BlockSpec((step, columns), lambda i, h: (h[0] * steps + i, 0))
    whole = lambda value: pl.BlockSpec(value.shape, lambda i, h: (0, 0))
    grid_spec = pltpu.PrefetchScalarGridSpec(
        num_scalar_prefetch=1,
        grid=(steps,),
        in_specs=[
            tile(grads.shape[1]),
            tile(acts.shape[1]),
            whole(sketch_out),
            whole(sketch_in),
        ],
        out_specs=[
            pl.BlockSpec((step, 2 * R), lambda i, h: (i, 0)),
            pl.BlockSpec((16, 128), lambda i, h: (0, 0)),
        ],
        scratch_shapes=[
            pltpu.VMEM((8, grads.shape[1]), jnp.float32),
            pltpu.VMEM((8, acts.shape[1]), jnp.float32),
        ],
    )
    return call(
        sketch_kernel,
        [array(count, 2 * R), array(16, 128)],
        grid_spec=grid_spec,
        name="sketches",
    )(half.astype(jnp.int32).reshape(1), grads, acts, sketch_out, sketch_in)


LAST = ((1,), (1,))
INNER = ((1,), (0,))


def flip_halves(core, own, other, flipped):
    half = own.shape[0]
    flipped[:, pl.ds(pl.multiple_of(core * half, 128), half)] = own[...].T
    flipped[:, pl.ds(pl.multiple_of((1 - core) * half, 128), half)] = other[...].T


def range_grad_kernel(
    tokens_all, place_ref, own, other, grads, sq_one, sq_two, act, first, second, piece, flipped, rounded
):
    step = pl.program_id(0)
    columns = grads.shape[1]

    @pl.when(step == 0)
    def _():
        flip_halves(place_ref[1], own, other, flipped)
        rounded[...] = flipped[...].astype(jnp.bfloat16)
        total = act[0:48, :]
        for d in range(1, 16):
            total += act[48 * d : 48 * d + 48, :]
        piece[...] = total

    part = jnp.dot(rounded[...], grads[...], preferred_element_type=jnp.float32)
    to = pl.ds(pl.multiple_of(step * columns, 128), columns)
    store_groups(first, second, to, part / tokens_all)

    @pl.when(step == pl.num_programs(0) - 1)
    def _():
        some = flipped[pl.ds(pl.multiple_of(place_ref[0] * 32, 32), 32), :]
        core = product(split(flipped[...]), split(some), LAST) / tokens_all
        lane = lax.broadcasted_iota(jnp.int32, (R, 96), 1)
        squares = sq_one[...] + sq_two[...]
        traces = jnp.where(lane == 0, squares[0:1, 0:1], 0.0)
        traces = jnp.where(lane == 1, squares[8:9, 0:1], traces)
        rest = jnp.concatenate([core, traces], axis=1)
        store_groups(first, second, pl.ds(first.shape[1] - 128, 128), rest)


def range_grad_of(places, own, other, grads, sq_one, sq_two, act, tokens_all):
    count, columns = grads.shape
    whole = lambda shape: pl.BlockSpec(shape, lambda j, c: (0, 0))
    grid_spec = pltpu.PrefetchScalarGridSpec(
        num_scalar_prefetch=1,
        grid=(columns // TILE,),
        in_specs=[
            whole((count // 2, R)),
            whole((count // 2, R)),
            pl.BlockSpec((count, TILE), lambda j, c: (0, j)),
            whole((16, 128)),
            whole((16, 128)),
            whole((768, R)),
        ],
        out_specs=[whole((R // 2, columns + 128))] * 2 + [whole((48, R))],
        scratch_shapes=[
            pltpu.VMEM((R, count), jnp.float32),
            pltpu.VMEM((R, count), jnp.bfloat16),
        ],
    )
    return call(
        functools.partial(range_grad_kernel, tokens_all),
        [array(R // 2, columns + 128)] * 2 + [array(48, R)],
        grid_spec=grid_spec,
        name="range_grad",
    )(places, own, other, grads, sq_one, sq_two, act)


def range_act_kernel(tokens_all, place_ref, own, other, acts, out, core, flipped):
    flip_halves(place_ref[1], own, other, flipped)
    part = jnp.dot(
        flipped[...].astype(jnp.bfloat16), acts[...], preferred_element_type=jnp.float32
    )
    out[...] = part.T / tokens_all
    some = flipped[pl.ds(pl.multiple_of(place_ref[0] * 32, 32), 32), :]
    core[:, :32] = product(split(flipped[...]), split(some), LAST) / tokens_all
    core[:, 32:] = jnp.zeros((R, 96), jnp.float32)


def range_act_of(places, own, other, acts, tokens_all):
    count, columns = acts.shape
    whole = lambda shape, j=0: pl.BlockSpec(shape, lambda i, c: (0, j))
    grid_spec = pltpu.PrefetchScalarGridSpec(
        num_scalar_prefetch=1,
        grid=(1,),
        in_specs=[whole((count // 2, R), 1), whole((count // 2, R), 1), whole((count, columns))],
        out_specs=[whole((columns, R)), whole((R, 128))],
        scratch_shapes=[pltpu.VMEM((R, count), jnp.float32)],
    )
    return call(
        functools.partial(range_act_kernel, tokens_all),
        [array(columns, R), array(R, 128)],
        grid_spec=grid_spec,
        name="range_act",
    )(places, own, other, acts)


def left_kernel(place_ref, rows_act, core, weight, first, second, flipped, high, low):
    step = pl.program_id(0)
    columns = weight.shape[1]

    @pl.when(step == 0)
    def _():
        flipped[...] = rows_act[...].T
        high[...], low[...] = split(flipped[...])
        some = flipped[pl.ds(pl.multiple_of(place_ref[0] * 32, 32), 32), :]
        gram = product((high[...], low[...]), split(some), LAST)
        rest = jnp.concatenate([gram, core[:, :96]], axis=1)
        store_groups(first, second, pl.ds(first.shape[1] - 128, 128), rest)

    part = product((high[...], low[...]), split(weight[...]), INNER)
    store_groups(first, second, pl.ds(pl.multiple_of(step * columns, 128), columns), part)


def left_products(places, rows_act, core, weight):
    count, columns = weight.shape
    whole = lambda shape: pl.BlockSpec(shape, lambda j, c: (0, 0))
    grid_spec = pltpu.PrefetchScalarGridSpec(
        num_scalar_prefetch=1,
        grid=(columns // TILE,),
        in_specs=[
            whole((count, R)),
            whole((R, 128)),
            pl.BlockSpec((count, TILE), lambda j, c: (0, j)),
        ],
        out_specs=[whole((R // 2, columns + 128))] * 2,
        scratch_shapes=[
            pltpu.VMEM((R, count), jnp.float32),
            pltpu.VMEM((R, count), jnp.bfloat16),
            pltpu.VMEM((R, count), jnp.bfloat16),
        ],
    )
    return call(
        left_kernel,
        [array(R // 2, columns + 128)] * 2,
        grid_spec=grid_spec,
        name="left_products",
    )(places, rows_act, core, weight)


def right_kernel(whole, weight, left, sums):
    @pl.when(pl.program_id(0) == 0)
    def _():
        sums[...] = jnp.zeros_like(sums)

    ranges = split(whole[...])
    right = product(split(weight[...]), ranges, LAST)
    gram = product(ranges, ranges, LAST)
    both = product(split(left[...]), ranges, LAST)
    for i in range(8):
        at = i * 88
        sums[at : at + 48, :] += right[i * 48 : i * 48 + 48]
        sums[at + 48 : at + 80, :] += gram[i * 32 : i * 32 + 32]
        sums[at + 80 : at + 82, :] += both[i * 2 : i * 2 + 2]


def right_products(whole, weight, left):
    count, columns = weight.shape
    return call(
        right_kernel,
        array(704, R),
        grid=(columns // TILE,),
        in_specs=[
            pl.BlockSpec((R, TILE), lambda j: (0, j)),
            pl.BlockSpec((count, TILE), lambda j: (0, j)),
            pl.BlockSpec((16, TILE), lambda j: (0, j)),
        ],
        out_specs=pl.BlockSpec((704, R), lambda j: (0, 0)),
        name="right_products",
    )(whole, weight, left)


def pack_small_kernel(parts, out):
    parts = [parts[i * 16 : i * 16 + 16, :] for i in range(8)]
    gram = jnp.concatenate([p[:, :32] for p in parts], axis=1)
    core = jnp.concatenate([p[:, 32:64] for p in parts], axis=1)
    for d in range(16):
        out[32 * d : 32 * d + 16, :] = gram
        out[32 * d + 16 : 32 * d + 32, :] = core


def pack_both_kernel(right, out):
    for d in range(16):
        for i in range(8):
            at = 16 * d + 2 * i
            out[at : at + 2, :] = right[i * 128 + 80 : i * 128 + 82, :]


def pack(kernel, value, count, name):
    whole = pl.BlockSpec(memory_space=pltpu.VMEM)
    return call(kernel, array(count, R), in_specs=[whole], out_specs=whole, name=name)(value)


def exact(left, right, dims):
    return lax.dot_general(
        left,
        right,
        (dims, ((), ())),
        precision=lax.Precision.HIGHEST,
        preferred_element_type=jnp.float32,
    )


def spread(value):
    return jnp.broadcast_to(value, (8, 2 * BLOCK))


def eliminate(matrices):
    sub = lax.broadcasted_iota(jnp.int32, (8, 2 * BLOCK), 0)
    count = BLOCK // 8
    groups = [[m[8 * i : 8 * i + 8] for i in range(count)] for m in matrices]
    for at in range(count):
        k = 8 * at
        for group in groups:
            tile = group[at]
            lines = [spread(tile[j : j + 1]) for j in range(8)]
            pivot = {
                (j, l): spread(lines[j][:, k + l : k + l + 1])
                for j in range(8)
                for l in range(j, 8)
            }
            scaled, factor = [], {}
            for j in range(8):
                inverse = 1.0 / pivot[j, j]
                scaled.append(lines[j] * inverse)
                for l in range(j + 1, 8):
                    factor[j, l] = pivot[j, l] * inverse
                    for m in range(l, 8):
                        pivot[l, m] = pivot[l, m] - factor[j, l] * pivot[j, m]
                    lines[l] = lines[l] - factor[j, l] * lines[j]
            for i in range(at + 1, count):
                value, sums, columns = group[i], None, []
                for j in range(8):
                    column = spread(value[:, k + j : k + j + 1])
                    for q in range(j):
                        column = column - columns[q] * factor[q, j]
                    columns.append(column)
                    term = column * scaled[j]
                    sums = term if sums is None else sums + term
                group[i] = value - sums
            for j in range(8):
                tile = jnp.where(sub == j, lines[j] * lax.rsqrt(pivot[j, j]), tile)
            group[at] = tile
    return [jnp.concatenate(group, axis=0) for group in groups]


def lower_inverses(work, outs):
    row = lax.broadcasted_iota(jnp.int32, (BLOCK, BLOCK), 0)
    column = lax.broadcasted_iota(jnp.int32, (BLOCK, BLOCK), 1)
    identity = jnp.where(row == column, 1.0, 0.0)
    for low in range(0, R, BLOCK):
        high = low + BLOCK
        done = eliminate(
            [jnp.concatenate([w[low:high, low:high], identity], axis=1) for w in work]
        )
        for w, corner, out in zip(work, done, outs):
            corner = jnp.where(row >= column, corner[:, BLOCK:], 0.0)
            line = exact(corner, w[low:high, :], INNER)
            out[low:high, :] = line[:, R:]
            if high < R:
                w[high:, :] -= exact(line[:, high:R], line, ((0,), (0,)))


def factor_kernel(counts, right, small, inverse_act, inverse_grad, scale, *work):
    trace_grad, trace_act = jnp.zeros((1, 1)), jnp.zeros((1, 1))
    for i in range(8):
        at = i * 128 + 120
        trace_grad += right[at : at + 1, 32:33]
        trace_act += right[at : at + 1, 33:34]
    damp_grad = DAMPING * trace_grad / counts[0]
    damp_act = DAMPING * trace_act / counts[1]
    scale[...] = jnp.broadcast_to(1.0 / (damp_act * damp_grad), (8, 128))
    row = lax.broadcasted_iota(jnp.int32, (R, R), 0)
    column = lax.broadcasted_iota(jnp.int32, (R, R), 1)
    identity = jnp.where(row == column, 1.0, 0.0)
    for w in work:
        w[:, R:] = identity
    for i in range(8):
        at, here = slice(i * 32, i * 32 + 32), i * 128
        work[1][at, :R] = damp_grad * right[here + 88 : here + 120, :] + right[here + 48 : here + 80, :]
    for d in range(16):
        at, here = slice(d * 16, d * 16 + 16), d * 32
        work[0][at, :R] = damp_act * small[here + 16 : here + 32, :] + small[here : here + 16, :]
    lower_inverses(work, (inverse_act, inverse_grad))


def factors(right, small, counts):
    whole = pl.BlockSpec(memory_space=pltpu.VMEM)
    return call(
        functools.partial(factor_kernel, counts),
        [array(R, R), array(R, R), array(8, 128)],
        in_specs=[whole] * 2,
        out_specs=[whole] * 3,
        scratch_shapes=[pltpu.VMEM((R, 2 * R), jnp.float32)] * 2,
        name="factors",
    )(right, small)


def applied(value, inverse):
    pieces = split(inverse)
    value = product(split(value), pieces, LAST)
    return product(split(value), pieces, INNER)


def last_kernel(
    left_sums, weight, range_grad, right, both, rows_act, inverse_act, inverse_grad, scale, out, sums, *pieces
):
    @pl.when(pl.program_id(0) == 0)
    def _():
        for i in range(8):
            sums[i * 48 : i * 48 + 48, :] = right[i * 128 : i * 128 + 48, :]
        solved = applied(rows_act[...], inverse_act[...])
        pieces[0][...], pieces[1][...] = split(solved)
        rest = sums[...] - product(split(solved), split(both[...]), INNER)
        pieces[2][...], pieces[3][...] = split(applied(rest, inverse_grad[...]))

    left = product((pieces[0][...], pieces[1][...]), split(left_sums[...]), INNER)
    range_pieces = split(range_grad[...])
    update = left + product((pieces[2][...], pieces[3][...]), range_pieces, INNER)
    out[...] = (weight[...] - update) * scale[0:1, 0:1]


def last_update(left_sums, weight, range_grad, *rest):
    count, columns = weight.shape
    return call(
        last_kernel,
        array(count, columns),
        grid=(columns // TILE,),
        in_specs=[
            pl.BlockSpec((R, TILE), lambda j: (0, j)),
            pl.BlockSpec((count, TILE), lambda j: (0, j)),
            pl.BlockSpec((R, TILE), lambda j: (0, j)),
        ]
        + [pl.BlockSpec(value.shape, lambda j: (0, 0)) for value in rest],
        out_specs=pl.BlockSpec((count, TILE), lambda j: (0, j)),
        scratch_shapes=[pltpu.VMEM((count, R), jnp.float32)]
        + [pltpu.VMEM((count, R), jnp.bfloat16)] * 4,
        name="last_update",
    )(left_sums, weight, range_grad, *rest)


def hand_over_dp(value):
    return lax.all_to_all(value, "dp", 0, 0, tiled=True)


def body(acts, grads_out, sketch_in, sketch_out, weight_grad):
    tokens_all = acts.shape[0] * lax.axis_size("dp")
    columns = weight_grad.shape[1]
    core_id = lax.axis_index("tensor") % 2
    places = jnp.stack([tensor_chunk(), core_id]).astype(jnp.int32)
    width = R // 8

    part, sq_one = sketches(1 - core_id, grads_out, acts, sketch_out, sketch_in)
    other = swap_cores(part)
    part, sq_two = sketches(core_id, grads_out, acts, sketch_out, sketch_in)
    own = gather_four(scatter_four(part + other, "x"), "x")
    other = swap_cores(own)

    part, core = range_act_of(places, own, other, acts, tokens_all)
    part = hand_over_dp(part)
    first, second, piece = range_grad_of(
        places, own, other, grads_out, sq_one, sq_two, part, tokens_all
    )

    moves = []
    for d in range(16):
        for t in range(8):
            k = d % 8
            moves.append((d * 8 + t, (2 * t + d // 8) * 8 + 2 * (k % 4) + k // 4))
    piece = lax.ppermute(piece, ("dp", "tensor"), moves)
    rows_act = gather_tensor(piece)

    piece = scatter_dp_after(first, second, rows_act)
    range_grad = lax.all_gather(piece, "dp", axis=0, tiled=True)

    piece = scatter_dp(*left_products(places, rows_act, core, weight_grad))
    left_sums = lax.all_gather(piece, "dp", axis=0, tiled=True)
    small = gather_tensor(piece[:, columns:])
    small = hand_over_dp(pack(pack_small_kernel, small, 512, "pack_small"))

    part = scatter_tensor(right_products(range_grad, weight_grad, piece))
    extra = range_grad[:, columns:]
    rest = jnp.pad(extra[:8], ((0, 0), (0, R - 128)))
    right = gather_tensor(jnp.concatenate([part, extra[:, :width].T, rest]))
    both = hand_over_dp(pack(pack_both_kernel, right, R, "pack_both"))

    counts = (float(tokens_all * FF), float(tokens_all * D))
    inverse_act, inverse_grad, scale = factors(right, small, counts)
    return last_update(
        left_sums, weight_grad, range_grad, right, both, rows_act, inverse_act, inverse_grad, scale
    )


def solution(mesh):
    return jax.shard_map(
        body,
        mesh=mesh,
        in_specs=(
            P("dp", "tensor"),
            P("dp", "tensor"),
            P("tensor", None),
            P("tensor", None),
            P("dp", "tensor"),
        ),
        out_specs=P("dp", "tensor"),
        check_vma=False,
    )
```

```python
import functools

import jax
import jax.numpy as jnp
from jax import lax
from jax.experimental import pallas as pl
from jax.experimental.pallas import tpu as pltpu
from jax.sharding import PartitionSpec as P

D = 6144
FF = 24576
R = 256
TILE = 512
BLOCK = 64
VMEM_LIMIT = 48 * 1024 * 1024

DAMPING = 0.1


def ring(kind, step):
    if kind == "y":
        return [(i, i // 4 * 4 + (i % 4 + step) % 4) for i in range(16)]
    if kind == "z":
        return [(i, (i // 4 + step) % 4 * 4 + i % 4) for i in range(16)]
    return [(i, (i // 2 + step) % 4 * 2 + i % 2) for i in range(8)]


def send(value, kind, step):
    return lax.ppermute(value, "tensor" if kind == "x" else "dp", ring(kind, step))


def swap_cores(value):
    return lax.ppermute(value, "tensor", [(i, i ^ 1) for i in range(8)])


def place(kind):
    if kind == "y":
        return lax.axis_index("dp") % 4
    if kind == "z":
        return lax.axis_index("dp") // 4
    return lax.axis_index("tensor") // 2


def rows(value, index, count):
    return lax.dynamic_slice_in_dim(value, index * count, count, 0)


def scatter_four(value, kind):
    here, count = place(kind), value.shape[0] // 4
    two, one, three = (
        send(rows(value, (here + step) % 4, count), kind, step) for step in (2, 1, 3)
    )
    return (rows(value, here, count) + two) + (one + three)


def gather_four(value, kind):
    here, count = place(kind), value.shape[0]
    two, one, three = (send(value, kind, step) for step in (2, 1, 3))
    whole = jnp.zeros((4 * count,) + value.shape[1:], value.dtype)
    for step, part in enumerate((value, one, two, three)):
        whole = lax.dynamic_update_slice_in_dim(whole, part, (here - step) % 4 * count, 0)
    return whole


def scatter_dp(first, second):
    first, second = scatter_four(first, "y"), scatter_four(second, "z")
    return jnp.concatenate([scatter_four(first, "z"), scatter_four(second, "y")])


def store_groups(first, second, columns, value):
    for d in range(16):
        to = d % 4 * 4 + d // 4
        first[8 * to : 8 * to + 8, columns] = value[16 * d : 16 * d + 8]
        second[8 * d : 8 * d + 8, columns] = value[16 * d + 8 : 16 * d + 16]


def tensor_chunk():
    index = lax.axis_index("tensor")
    return index % 2 * 4 + index // 2


def scatter_tensor(value):
    core, half = lax.axis_index("tensor") % 2, value.shape[0] // 2
    other = swap_cores(rows(value, 1 - core, half))
    return scatter_four(rows(value, core, half) + other, "x")


def gather_tensor(value):
    core = lax.axis_index("tensor") % 2
    value = gather_four(value, "x")
    other = swap_cores(value)
    low = jnp.where(core == 0, value, other)
    high = jnp.where(core == 0, other, value)
    return jnp.concatenate([low, high])


def split(value):
    high = value.astype(jnp.bfloat16)
    return high, (value - high.astype(jnp.float32)).astype(jnp.bfloat16)


def product(left, right, dims):
    (lh, ll), (rh, rl) = left, right
    (along_left,), (along_right,) = dims
    return lax.dot_general(
        jnp.concatenate([lh, lh, ll], axis=along_left),
        jnp.concatenate([rh, rl, rh], axis=along_right),
        (dims, ((), ())),
        preferred_element_type=jnp.float32,
    )


def call(kernel, out_shape, **options):
    return pl.pallas_call(
        kernel,
        out_shape=out_shape,
        compiler_params=pltpu.CompilerParams(vmem_limit_bytes=VMEM_LIMIT),
        **options,
    )


def array(*shape):
    return jax.ShapeDtypeStruct(shape, jnp.float32)


def sketch_kernel(core, grads, acts, sketch_out, sketch_in, out, squares, total_grad, total_act):
    step = pl.program_id(0)
    some = zip((grads, acts), (sketch_out, sketch_in), (total_grad, total_act))
    for i, (value, sketch, total) in enumerate(some):

        @pl.when(step == 0)
        def _():
            total[...] = jnp.zeros_like(total)

        tile = value[...]
        out[:, i * R : i * R + R] = jnp.dot(
            tile, sketch[...], preferred_element_type=jnp.float32
        )
        tile = tile.astype(jnp.float32)
        total[...] += jnp.sum(jnp.square(tile).reshape(-1, 8, tile.shape[1]), axis=0)

        @pl.when(step == pl.num_programs(0) - 1)
        def _():
            whole = jnp.sum(total[...], keepdims=True)
            squares[8 * i : 8 * i + 8, :] = jnp.broadcast_to(whole, (8, 128))


def sketches(half, grads, acts, sketch_out, sketch_in):
    count = grads.shape[0] // 2
    step = 384
    steps = count // step
    tile = lambda columns: pl.BlockSpec((step, columns), lambda i, h: (h[0] * steps + i, 0))
    whole = lambda value: pl.BlockSpec(value.shape, lambda i, h: (0, 0))
    grid_spec = pltpu.PrefetchScalarGridSpec(
        num_scalar_prefetch=1,
        grid=(steps,),
        in_specs=[
            tile(grads.shape[1]),
            tile(acts.shape[1]),
            whole(sketch_out),
            whole(sketch_in),
        ],
        out_specs=[
            pl.BlockSpec((step, 2 * R), lambda i, h: (i, 0)),
            pl.BlockSpec((16, 128), lambda i, h: (0, 0)),
        ],
        scratch_shapes=[
            pltpu.VMEM((8, grads.shape[1]), jnp.float32),
            pltpu.VMEM((8, acts.shape[1]), jnp.float32),
        ],
    )
    return call(
        sketch_kernel,
        [array(count, 2 * R), array(16, 128)],
        grid_spec=grid_spec,
        name="sketches",
    )(half.astype(jnp.int32).reshape(1), grads, acts, sketch_out, sketch_in)


LAST = ((1,), (1,))
INNER = ((1,), (0,))


def flip_halves(core, own, other, flipped):
    half = own.shape[0]
    flipped[:, pl.ds(pl.multiple_of(core * half, 128), half)] = own[...].T
    flipped[:, pl.ds(pl.multiple_of((1 - core) * half, 128), half)] = other[...].T


def ranges_kernel(
    tokens_all, places, own, other, grads, acts, sq_one, sq_two, first, second, flipped, rounded, range_act
):
    step = pl.program_id(0)
    columns = grads.shape[1]
    whole = pl.num_programs(0) * columns

    @pl.when(step == 0)
    def _():
        half = own.shape[0]
        flipped[:, pl.ds(pl.multiple_of(places[1] * half, 128), half)] = own[...].T
        flipped[:, pl.ds(pl.multiple_of((1 - places[1]) * half, 128), half)] = other[...].T
        rounded[...] = flipped[...].astype(jnp.bfloat16)

    part = jnp.dot(rounded[:R, :], grads[...], preferred_element_type=jnp.float32)
    to = pl.ds(pl.multiple_of(step * columns, 128), columns)
    store_groups(first, second, to, part / tokens_all)

    @pl.when(step == pl.num_programs(0) - 1)
    def _():
        cores = []
        for low in (0, R):
            some = flipped[pl.ds(pl.multiple_of(low + places[0] * 32, 32), 32), :]
            core = product(split(flipped[low : low + R, :]), split(some), LAST)
            cores.append(core / tokens_all)
        lane = lax.broadcasted_iota(jnp.int32, (R, 64), 1)
        squares = sq_one[...] + sq_two[...]
        traces = jnp.where(lane == 0, squares[0:1, 0:1], 0.0)
        traces = jnp.where(lane == 1, squares[8:9, 0:1], traces)
        rest = jnp.concatenate(cores + [traces], axis=1)
        store_groups(first, second, pl.ds(whole, 128), rest)
        part = jnp.dot(rounded[R:, :], acts[...], preferred_element_type=jnp.float32)
        range_act[...] = part.T / tokens_all
        for d in range(16):
            for i in range(3):
                to = pl.ds(whole + 128 + i * R, R)
                at, here = d % 4 * 4 + d // 4, 48 * d + 16 * i
                first[8 * at : 8 * at + 8, to] = range_act[here : here + 8, :]
                second[8 * d : 8 * d + 8, to] = range_act[here + 8 : here + 16, :]


def ranges(places, own, other, grads, acts, sq_one, sq_two, tokens_all):
    count, columns = grads.shape
    fixed = lambda shape: pl.BlockSpec(shape, lambda j, c: (0, 0))
    total = columns + 128 + 3 * R
    grid_spec = pltpu.PrefetchScalarGridSpec(
        num_scalar_prefetch=1,
        grid=(columns // TILE,),
        in_specs=[
            fixed(own.shape),
            fixed(other.shape),
            pl.BlockSpec((count, TILE), lambda j, c: (0, j)),
            fixed(acts.shape),
            fixed((16, 128)),
            fixed((16, 128)),
        ],
        out_specs=[fixed((R // 2, total))] * 2,
        scratch_shapes=[
            pltpu.VMEM((2 * R, count), jnp.float32),
            pltpu.VMEM((2 * R, count), jnp.bfloat16),
            pltpu.VMEM((acts.shape[1], R), jnp.float32),
        ],
    )
    return call(
        functools.partial(ranges_kernel, tokens_all),
        [array(R // 2, total)] * 2,
        grid_spec=grid_spec,
        name="ranges",
    )(places, own, other, grads, acts, sq_one, sq_two)


def left_kernel(rows_act, weight, first, second, high, low):
    step = pl.program_id(0)
    columns = weight.shape[1]

    @pl.when(step == 0)
    def _():
        high[...], low[...] = split(rows_act[...].T)

    part = product((high[...], low[...]), split(weight[...]), INNER)
    store_groups(first, second, pl.ds(pl.multiple_of(step * columns, 128), columns), part)


def left_products(rows_act, weight):
    count, columns = weight.shape
    return call(
        left_kernel,
        [array(R // 2, columns)] * 2,
        grid=(columns // TILE,),
        in_specs=[
            pl.BlockSpec((count, R), lambda j: (0, 0)),
            pl.BlockSpec((count, TILE), lambda j: (0, j)),
        ],
        out_specs=[pl.BlockSpec((R // 2, columns), lambda j: (0, 0))] * 2,
        scratch_shapes=[pltpu.VMEM((R, count), jnp.bfloat16)] * 2,
        name="left_products",
    )(rows_act, weight)


def right_kernel(whole, one, two, three, weight, left, sums):
    @pl.when(pl.program_id(0) == 0)
    def _():
        sums[...] = jnp.zeros_like(sums)
        pieces = split(jnp.concatenate([one[...], two[...], three[...]]))
        gram = product(pieces, pieces, ((0,), (0,)))
        for i in range(8):
            sums[i * 120 + 80 : i * 120 + 112, :] = gram[i * 32 : i * 32 + 32]

    ranges = split(whole[...])
    right = product(split(weight[...]), ranges, LAST)
    gram = product(ranges, ranges, LAST)
    both = product(split(left[...]), ranges, LAST)
    for i in range(8):
        at = i * 120
        sums[at : at + 48, :] += right[i * 48 : i * 48 + 48]
        sums[at + 48 : at + 80, :] += gram[i * 32 : i * 32 + 32]
        sums[at + 112 : at + 114, :] += both[i * 2 : i * 2 + 2]


def right_products(whole, extra, weight, left):
    count, columns = weight.shape
    return call(
        right_kernel,
        array(960, R),
        grid=(columns // TILE,),
        in_specs=[pl.BlockSpec((R, TILE), lambda j: (0, j))]
        + [pl.BlockSpec((R, R), lambda j: (0, 0))] * 3
        + [
            pl.BlockSpec((count, TILE), lambda j: (0, j)),
            pl.BlockSpec((16, TILE), lambda j: (0, j)),
        ],
        out_specs=pl.BlockSpec((960, R), lambda j: (0, 0)),
        name="right_products",
    )(whole, *extra, weight, left)


def pack_kernel(right, out):
    for d in range(16):
        for i in range(8):
            at = 16 * d + 2 * i
            out[at : at + 2, :] = right[i * 192 + 112 : i * 192 + 114, :]


def pack(right):
    whole = pl.BlockSpec(memory_space=pltpu.VMEM)
    return call(pack_kernel, array(R, R), in_specs=[whole], out_specs=whole, name="pack")(right)


def exact(left, right, dims):
    return lax.dot_general(
        left,
        right,
        (dims, ((), ())),
        precision=lax.Precision.HIGHEST,
        preferred_element_type=jnp.float32,
    )


def spread(value):
    return jnp.broadcast_to(value, (8, 2 * BLOCK))


def eliminate(matrices):
    sub = lax.broadcasted_iota(jnp.int32, (8, 2 * BLOCK), 0)
    count = BLOCK // 8
    groups = [[m[8 * i : 8 * i + 8] for i in range(count)] for m in matrices]
    for at in range(count):
        k = 8 * at
        for group in groups:
            tile = group[at]
            lines = [spread(tile[j : j + 1]) for j in range(8)]
            pivot = {
                (j, l): spread(lines[j][:, k + l : k + l + 1])
                for j in range(8)
                for l in range(j, 8)
            }
            scaled, factor = [], {}
            for j in range(8):
                inverse = 1.0 / pivot[j, j]
                scaled.append(lines[j] * inverse)
                for l in range(j + 1, 8):
                    factor[j, l] = pivot[j, l] * inverse
                    for m in range(l, 8):
                        pivot[l, m] = pivot[l, m] - factor[j, l] * pivot[j, m]
                    lines[l] = lines[l] - factor[j, l] * lines[j]
            for i in range(at + 1, count):
                value, sums, columns = group[i], None, []
                for j in range(8):
                    column = spread(value[:, k + j : k + j + 1])
                    for q in range(j):
                        column = column - columns[q] * factor[q, j]
                    columns.append(column)
                    term = column * scaled[j]
                    sums = term if sums is None else sums + term
                group[i] = value - sums
            for j in range(8):
                tile = jnp.where(sub == j, lines[j] * lax.rsqrt(pivot[j, j]), tile)
            group[at] = tile
    return [jnp.concatenate(group, axis=0) for group in groups]


def lower_inverses(work, outs):
    row = lax.broadcasted_iota(jnp.int32, (BLOCK, BLOCK), 0)
    column = lax.broadcasted_iota(jnp.int32, (BLOCK, BLOCK), 1)
    identity = jnp.where(row == column, 1.0, 0.0)
    for low in range(0, R, BLOCK):
        high = low + BLOCK
        done = eliminate(
            [jnp.concatenate([w[low:high, low:high], identity], axis=1) for w in work]
        )
        for w, corner, out in zip(work, done, outs):
            corner = jnp.where(row >= column, corner[:, BLOCK:], 0.0)
            line = exact(corner, w[low:high, :], INNER)
            out[low:high, :] = line[:, R:]
            if high < R:
                w[high:, :] -= exact(line[:, high:R], line, ((0,), (0,)))


def factor_kernel(counts, right, inverse_act, inverse_grad, scale, *work):
    trace_grad, trace_act = jnp.zeros((1, 1)), jnp.zeros((1, 1))
    for i in range(8):
        at = i * 192 + 184
        trace_grad += right[at : at + 1, 64:65]
        trace_act += right[at : at + 1, 65:66]
    damp_grad = DAMPING * trace_grad / counts[0]
    damp_act = DAMPING * trace_act / counts[1]
    scale[...] = jnp.broadcast_to(1.0 / (damp_act * damp_grad), (8, 128))
    row = lax.broadcasted_iota(jnp.int32, (R, R), 0)
    column = lax.broadcasted_iota(jnp.int32, (R, R), 1)
    identity = jnp.where(row == column, 1.0, 0.0)
    for w in work:
        w[:, R:] = identity
    for i in range(8):
        at, here = slice(i * 32, i * 32 + 32), i * 192
        work[0][at, :R] = damp_act * right[here + 152 : here + 184, :] + right[here + 80 : here + 112, :]
        work[1][at, :R] = damp_grad * right[here + 120 : here + 152, :] + right[here + 48 : here + 80, :]
    lower_inverses(work, (inverse_act, inverse_grad))


def factors(right, counts):
    whole = pl.BlockSpec(memory_space=pltpu.VMEM)
    return call(
        functools.partial(factor_kernel, counts),
        [array(R, R), array(R, R), array(8, 128)],
        in_specs=[whole],
        out_specs=[whole] * 3,
        scratch_shapes=[pltpu.VMEM((R, 2 * R), jnp.float32)] * 2,
        name="factors",
    )(right)


def applied(value, inverse):
    pieces = split(inverse)
    value = product(split(value), pieces, LAST)
    return product(split(value), pieces, INNER)


def last_kernel(
    left_sums, weight, range_grad, right, both, rows_act, inverse_act, inverse_grad, scale, out, sums, *pieces
):
    @pl.when(pl.program_id(0) == 0)
    def _():
        for i in range(8):
            sums[i * 48 : i * 48 + 48, :] = right[i * 192 : i * 192 + 48, :]
        solved = applied(rows_act[...], inverse_act[...])
        pieces[0][...], pieces[1][...] = split(solved)
        rest = sums[...] - product(split(solved), split(both[...]), INNER)
        pieces[2][...], pieces[3][...] = split(applied(rest, inverse_grad[...]))

    left = product((pieces[0][...], pieces[1][...]), split(left_sums[...]), INNER)
    range_pieces = split(range_grad[...])
    update = left + product((pieces[2][...], pieces[3][...]), range_pieces, INNER)
    out[...] = (weight[...] - update) * scale[0:1, 0:1]


def last_update(left_sums, weight, range_grad, *rest):
    count, columns = weight.shape
    return call(
        last_kernel,
        array(count, columns),
        grid=(columns // TILE,),
        in_specs=[
            pl.BlockSpec((R, TILE), lambda j: (0, j)),
            pl.BlockSpec((count, TILE), lambda j: (0, j)),
            pl.BlockSpec((R, TILE), lambda j: (0, j)),
        ]
        + [pl.BlockSpec(value.shape, lambda j: (0, 0)) for value in rest],
        out_specs=pl.BlockSpec((count, TILE), lambda j: (0, j)),
        scratch_shapes=[pltpu.VMEM((count, R), jnp.float32)]
        + [pltpu.VMEM((count, R), jnp.bfloat16)] * 4,
        name="last_update",
    )(left_sums, weight, range_grad, *rest)


def hand_over_dp(value):
    return lax.all_to_all(value, "dp", 0, 0, tiled=True)


def body(acts, grads_out, sketch_in, sketch_out, weight_grad):
    tokens_all = acts.shape[0] * lax.axis_size("dp")
    columns = weight_grad.shape[1]
    core_id = lax.axis_index("tensor") % 2
    places = jnp.stack([tensor_chunk(), core_id]).astype(jnp.int32)
    width = R // 8

    part, sq_one = sketches(1 - core_id, grads_out, acts, sketch_out, sketch_in)
    other = swap_cores(part)
    part, sq_two = sketches(core_id, grads_out, acts, sketch_out, sketch_in)
    own = gather_four(scatter_four(part + other, "x"), "x")
    other = swap_cores(own)

    piece = scatter_dp(
        *ranges(places, own, other, grads_out, acts, sq_one, sq_two, tokens_all)
    )
    gathered = lax.all_gather(piece, "dp", axis=0, tiled=True)

    at = columns + 128
    piece = jnp.concatenate([piece[:, at + i * R : at + i * R + R] for i in range(3)])
    moves = []
    for d in range(16):
        for t in range(8):
            k = d % 8
            moves.append((d * 8 + t, (2 * t + d // 8) * 8 + 2 * (k % 4) + k // 4))
    rows_act = gather_tensor(lax.ppermute(piece, ("dp", "tensor"), moves))

    piece = scatter_dp(*left_products(rows_act, weight_grad))
    left_sums = lax.all_gather(piece, "dp", axis=0, tiled=True)

    blocks = [gathered[:, at + i * R : at + i * R + R] for i in range(3)]
    part = scatter_tensor(right_products(gathered, blocks, weight_grad, piece))
    extra = gathered[:, columns:at]
    cores = extra[:, : 2 * width].T
    rest = jnp.pad(extra[:8], ((0, 0), (0, R - 128)))
    right = gather_tensor(jnp.concatenate([part, cores, rest]))
    both = lax.all_to_all(pack(right), "dp", 0, 0, tiled=True)

    counts = (float(tokens_all * FF), float(tokens_all * D))
    inverse_act, inverse_grad, scale = factors(right, counts)
    return last_update(
        left_sums, weight_grad, gathered, right, both, rows_act, inverse_act, inverse_grad, scale
    )


def solution(mesh):
    return jax.shard_map(
        body,
        mesh=mesh,
        in_specs=(
            P("dp", "tensor"),
            P("dp", "tensor"),
            P("tensor", None),
            P("tensor", None),
            P("dp", "tensor"),
        ),
        out_specs=P("dp", "tensor"),
        check_vma=False,
    )
```

```python
import functools

import jax
import jax.numpy as jnp
from jax import lax
from jax.experimental import pallas as pl
from jax.experimental.pallas import tpu as pltpu
from jax.sharding import PartitionSpec as P

D = 6144
FF = 24576
R = 256
TILE = 512
BLOCK = 64
VMEM_LIMIT = 48 * 1024 * 1024

DAMPING = 0.1


def ring(kind, step):
    if kind == "y":
        return [(i, i // 4 * 4 + (i % 4 + step) % 4) for i in range(16)]
    if kind == "z":
        return [(i, (i // 4 + step) % 4 * 4 + i % 4) for i in range(16)]
    return [(i, (i // 2 + step) % 4 * 2 + i % 2) for i in range(8)]


def send(value, kind, step):
    return lax.ppermute(value, "tensor" if kind == "x" else "dp", ring(kind, step))


def swap_cores(value):
    return lax.ppermute(value, "tensor", [(i, i ^ 1) for i in range(8)])


def place(kind):
    if kind == "y":
        return lax.axis_index("dp") % 4
    if kind == "z":
        return lax.axis_index("dp") // 4
    return lax.axis_index("tensor") // 2


def rows(value, index, count):
    return lax.dynamic_slice_in_dim(value, index * count, count, 0)


def scatter_four(value, kind):
    here, count = place(kind), value.shape[0] // 4
    two, one, three = (
        send(rows(value, (here + step) % 4, count), kind, step) for step in (2, 1, 3)
    )
    return (rows(value, here, count) + two) + (one + three)


def gather_four(value, kind):
    here, count = place(kind), value.shape[0]
    two, one, three = (send(value, kind, step) for step in (2, 1, 3))
    whole = jnp.zeros((4 * count,) + value.shape[1:], value.dtype)
    for step, part in enumerate((value, one, two, three)):
        whole = lax.dynamic_update_slice_in_dim(whole, part, (here - step) % 4 * count, 0)
    return whole


def scatter_dp(first, second):
    first, second = scatter_four(first, "y"), scatter_four(second, "z")
    both = [scatter_four(first, "z"), scatter_four(second, "y")]
    return jnp.concatenate(both), second


def store_groups(first, second, columns, value):
    for d in range(16):
        to = d % 4 * 4 + d // 4
        first[8 * to : 8 * to + 8, columns] = value[16 * d : 16 * d + 8]
        second[8 * d : 8 * d + 8, columns] = value[16 * d + 8 : 16 * d + 16]


def tensor_chunk():
    index = lax.axis_index("tensor")
    return index % 2 * 4 + index // 2


def scatter_tensor(value):
    core, half = lax.axis_index("tensor") % 2, value.shape[0] // 2
    other = swap_cores(rows(value, 1 - core, half))
    return scatter_four(rows(value, core, half) + other, "x")


def exchange_x(value):
    groups = [[2 * x + core for x in range(4)] for core in range(2)]
    return lax.all_to_all(value, "tensor", 0, 0, axis_index_groups=groups, tiled=True)


def gather_tensor(value):
    core = lax.axis_index("tensor") % 2
    value = gather_four(value, "x")
    other = swap_cores(value)
    low = jnp.where(core == 0, value, other)
    high = jnp.where(core == 0, other, value)
    return jnp.concatenate([low, high])


def split(value):
    high = value.astype(jnp.bfloat16)
    return high, (value - high.astype(jnp.float32)).astype(jnp.bfloat16)


def product(left, right, dims):
    (lh, ll), (rh, rl) = left, right
    (along_left,), (along_right,) = dims
    return lax.dot_general(
        jnp.concatenate([lh, lh, ll], axis=along_left),
        jnp.concatenate([rh, rl, rh], axis=along_right),
        (dims, ((), ())),
        preferred_element_type=jnp.float32,
    )


def call(kernel, out_shape, vmem=VMEM_LIMIT, **options):
    return pl.pallas_call(
        kernel,
        out_shape=out_shape,
        compiler_params=pltpu.CompilerParams(vmem_limit_bytes=vmem),
        **options,
    )


def array(*shape):
    return jax.ShapeDtypeStruct(shape, jnp.float32)


def sketch_kernel(core, grads, acts, sketch_out, sketch_in, out, squares, total_grad, total_act):
    step = pl.program_id(0)
    some = zip((grads, acts), (sketch_out, sketch_in), (total_grad, total_act))
    for i, (value, sketch, total) in enumerate(some):

        @pl.when(step == 0)
        def _():
            total[...] = jnp.zeros_like(total)

        tile = value[...]
        out[:, i * R : i * R + R] = jnp.dot(
            tile, sketch[...], preferred_element_type=jnp.float32
        )
        tile = tile.astype(jnp.float32)
        total[...] += jnp.sum(jnp.square(tile).reshape(-1, 8, tile.shape[1]), axis=0)

        @pl.when(step == pl.num_programs(0) - 1)
        def _():
            whole = jnp.sum(total[...], keepdims=True)
            squares[8 * i : 8 * i + 8, :] = jnp.broadcast_to(whole, (8, 128))


def sketches(half, grads, acts, sketch_out, sketch_in):
    count = grads.shape[0] // 2
    step = 384
    steps = count // step
    tile = lambda columns: pl.BlockSpec((step, columns), lambda i, h: (h[0] * steps + i, 0))
    whole = lambda value: pl.BlockSpec(value.shape, lambda i, h: (0, 0))
    grid_spec = pltpu.PrefetchScalarGridSpec(
        num_scalar_prefetch=1,
        grid=(steps,),
        in_specs=[
            tile(grads.shape[1]),
            tile(acts.shape[1]),
            whole(sketch_out),
            whole(sketch_in),
        ],
        out_specs=[
            pl.BlockSpec((step, 2 * R), lambda i, h: (i, 0)),
            pl.BlockSpec((16, 128), lambda i, h: (0, 0)),
        ],
        scratch_shapes=[
            pltpu.VMEM((8, grads.shape[1]), jnp.float32),
            pltpu.VMEM((8, acts.shape[1]), jnp.float32),
        ],
    )
    return call(
        sketch_kernel,
        [array(count, 2 * R), array(16, 128)],
        vmem=60 * 1024 * 1024,
        grid_spec=grid_spec,
        name="sketches",
    )(half.astype(jnp.int32).reshape(1), grads, acts, sketch_out, sketch_in)


LAST = ((1,), (1,))
INNER = ((1,), (0,))


def flip_halves(core, own, other, flipped):
    half = own.shape[0]
    flipped[:, pl.ds(pl.multiple_of(core * half, 128), half)] = own[...].T
    flipped[:, pl.ds(pl.multiple_of((1 - core) * half, 128), half)] = other[...].T


def ranges_kernel(
    tokens_all, places, own, other, grads, acts, sq_one, sq_two, first, second, flipped, rounded, range_act
):
    step = pl.program_id(0)
    columns = grads.shape[1]
    whole = pl.num_programs(0) * columns

    @pl.when(step == 0)
    def _():
        half = own.shape[0]
        flipped[:, pl.ds(pl.multiple_of(places[1] * half, 128), half)] = own[...].T
        flipped[:, pl.ds(pl.multiple_of((1 - places[1]) * half, 128), half)] = other[...].T
        rounded[...] = flipped[...].astype(jnp.bfloat16)

    part = jnp.dot(rounded[:R, :], grads[...], preferred_element_type=jnp.float32)
    to = pl.ds(pl.multiple_of(step * columns, 128), columns)
    store_groups(first, second, to, part / tokens_all)

    @pl.when(step == pl.num_programs(0) - 1)
    def _():
        cores = []
        for low in (0, R):
            some = flipped[pl.ds(pl.multiple_of(low + places[0] * 32, 32), 32), :]
            core = product(split(flipped[low : low + R, :]), split(some), LAST)
            cores.append(core / tokens_all)
        lane = lax.broadcasted_iota(jnp.int32, (R, 64), 1)
        squares = sq_one[...] + sq_two[...]
        traces = jnp.where(lane == 0, squares[0:1, 0:1], 0.0)
        traces = jnp.where(lane == 1, squares[8:9, 0:1], traces)
        rest = jnp.concatenate(cores + [traces], axis=1)
        store_groups(first, second, pl.ds(whole, 128), rest)
        part = jnp.dot(rounded[R:, :], acts[...], preferred_element_type=jnp.float32)
        range_act[...] = part.T / tokens_all
        for d in range(16):
            for i in range(3):
                to = pl.ds(whole + 128 + i * R, R)
                at, here = d % 4 * 4 + d // 4, 48 * d + 16 * i
                first[8 * at : 8 * at + 8, to] = range_act[here : here + 8, :]
                second[8 * d : 8 * d + 8, to] = range_act[here + 8 : here + 16, :]


def ranges(places, own, other, grads, acts, sq_one, sq_two, tokens_all):
    count, columns = grads.shape
    fixed = lambda shape: pl.BlockSpec(shape, lambda j, c: (0, 0))
    total = columns + 128 + 3 * R
    grid_spec = pltpu.PrefetchScalarGridSpec(
        num_scalar_prefetch=1,
        grid=(columns // TILE,),
        in_specs=[
            fixed(own.shape),
            fixed(other.shape),
            pl.BlockSpec((count, TILE), lambda j, c: (0, j)),
            fixed(acts.shape),
            fixed((16, 128)),
            fixed((16, 128)),
        ],
        out_specs=[fixed((R // 2, total))] * 2,
        scratch_shapes=[
            pltpu.VMEM((2 * R, count), jnp.float32),
            pltpu.VMEM((2 * R, count), jnp.bfloat16),
            pltpu.VMEM((acts.shape[1], R), jnp.float32),
        ],
    )
    return call(
        functools.partial(ranges_kernel, tokens_all),
        [array(R // 2, total)] * 2,
        grid_spec=grid_spec,
        name="ranges",
    )(places, own, other, grads, acts, sq_one, sq_two)


def left_kernel(rows_act, weight, first, second, high, low):
    step = pl.program_id(0)
    columns = weight.shape[1]

    @pl.when(step == 0)
    def _():
        high[...], low[...] = split(rows_act[...].T)

    part = product((high[...], low[...]), split(weight[...]), INNER)
    store_groups(first, second, pl.ds(pl.multiple_of(step * columns, 128), columns), part)


def left_products(rows_act, weight):
    count, columns = weight.shape
    return call(
        left_kernel,
        [array(R // 2, columns)] * 2,
        grid=(columns // TILE,),
        in_specs=[
            pl.BlockSpec((count, R), lambda j: (0, 0)),
            pl.BlockSpec((count, TILE), lambda j: (0, j)),
        ],
        out_specs=[pl.BlockSpec((R // 2, columns), lambda j: (0, 0))] * 2,
        scratch_shapes=[pltpu.VMEM((R, count), jnp.bfloat16)] * 2,
        name="left_products",
    )(rows_act, weight)


def right_kernel(whole, *refs):
    extra, (weight, after, sums) = refs[:6], refs[6:]

    @pl.when(pl.program_id(0) == 0)
    def _():
        sums[...] = jnp.zeros_like(sums)
        blocks = [jnp.concatenate([extra[i][...], extra[i + 1][...]], axis=1) for i in (0, 2, 4)]
        pieces = split(jnp.concatenate(blocks))
        gram = product(pieces, pieces, ((0,), (0,)))
        for i in range(8):
            sums[i * 112 + 80 : i * 112 + 112, :] = gram[i * 32 : i * 32 + 32]

    ranges = split(whole[...])
    right = product(split(weight[...]), ranges, LAST)
    gram = product(ranges, ranges, LAST)
    for i in range(8):
        at = i * 112
        sums[at : at + 48, :] += right[i * 48 : i * 48 + 48]
        sums[at + 48 : at + 80, :] += gram[i * 32 : i * 32 + 32]


def right_products(gathered, weight, after):
    count, columns = weight.shape
    extra = lambda i: pl.BlockSpec((R, 128), lambda j: (0, columns // 128 + 1 + i))
    return call(
        right_kernel,
        array(896, R),
        grid=(columns // TILE,),
        in_specs=[pl.BlockSpec((R, TILE), lambda j: (0, j))]
        + [extra(i) for i in range(6)]
        + [
            pl.BlockSpec((count, TILE), lambda j: (0, j)),
            pl.BlockSpec(memory_space=pl.ANY),
        ],
        out_specs=pl.BlockSpec((896, R), lambda j: (0, 0)),
        name="right_products",
    )(*[gathered] * 7, weight, after)


def both_kernel(whole, left, out):
    @pl.when(pl.program_id(0) == 0)
    def _():
        out[...] = jnp.zeros_like(out)

    out[...] += product(split(left[...]), split(whole[...]), LAST)


def both_products(gathered, left):
    count, columns = left.shape
    return call(
        both_kernel,
        array(count, R),
        grid=(columns // 1024,),
        in_specs=[
            pl.BlockSpec((R, 1024), lambda j: (0, j)),
            pl.BlockSpec((count, 1024), lambda j: (0, j)),
        ],
        out_specs=pl.BlockSpec((count, R), lambda j: (0, 0)),
        name="both_products",
    )(gathered, left)


def pack_kernel(right, out):
    total = right[184:200, :]
    for i in range(1, 8):
        total += right[i * 200 + 184 : i * 200 + 200, :]
    for d in range(16):
        out[16 * d : 16 * d + 16, :] = total


def pack(right):
    whole = pl.BlockSpec(memory_space=pltpu.VMEM)
    return call(pack_kernel, array(R, R), in_specs=[whole], out_specs=whole, name="pack")(right)


def exact(left, right, dims):
    return lax.dot_general(
        left,
        right,
        (dims, ((), ())),
        precision=lax.Precision.HIGHEST,
        preferred_element_type=jnp.float32,
    )


def spread(value):
    return jnp.broadcast_to(value, (8, 2 * BLOCK))


def eliminate(matrices):
    sub = lax.broadcasted_iota(jnp.int32, (8, 2 * BLOCK), 0)
    count = BLOCK // 8
    groups = [[m[8 * i : 8 * i + 8] for i in range(count)] for m in matrices]
    for at in range(count):
        k = 8 * at
        for group in groups:
            tile = group[at]
            lines = [spread(tile[j : j + 1]) for j in range(8)]
            pivot = {
                (j, l): spread(lines[j][:, k + l : k + l + 1])
                for j in range(8)
                for l in range(j, 8)
            }
            scaled, factor = [], {}
            for j in range(8):
                inverse = 1.0 / pivot[j, j]
                scaled.append(lines[j] * inverse)
                for l in range(j + 1, 8):
                    factor[j, l] = pivot[j, l] * inverse
                    for m in range(l, 8):
                        pivot[l, m] = pivot[l, m] - factor[j, l] * pivot[j, m]
                    lines[l] = lines[l] - factor[j, l] * lines[j]
            for i in range(at + 1, count):
                value, sums, columns = group[i], None, []
                for j in range(8):
                    column = spread(value[:, k + j : k + j + 1])
                    for q in range(j):
                        column = column - columns[q] * factor[q, j]
                    columns.append(column)
                    term = column * scaled[j]
                    sums = term if sums is None else sums + term
                group[i] = value - sums
            for j in range(8):
                tile = jnp.where(sub == j, lines[j] * lax.rsqrt(pivot[j, j]), tile)
            group[at] = tile
    return [jnp.concatenate(group, axis=0) for group in groups]


def lower_inverses(work, outs):
    row = lax.broadcasted_iota(jnp.int32, (BLOCK, BLOCK), 0)
    column = lax.broadcasted_iota(jnp.int32, (BLOCK, BLOCK), 1)
    identity = jnp.where(row == column, 1.0, 0.0)
    for low in range(0, R, BLOCK):
        high = low + BLOCK
        done = eliminate(
            [jnp.concatenate([w[low:high, low:high], identity], axis=1) for w in work]
        )
        for w, corner, out in zip(work, done, outs):
            corner = jnp.where(row >= column, corner[:, BLOCK:], 0.0)
            line = exact(corner, w[low:high, :], INNER)
            out[low:high, :] = line[:, R:]
            if high < R:
                w[high:, :] -= exact(line[:, high:R], line, ((0,), (0,)))


def factor_kernel(counts, right, inverse_act, inverse_grad, scale, *work):
    trace_grad, trace_act = jnp.zeros((1, 1)), jnp.zeros((1, 1))
    for i in range(8):
        at = i * 200 + 176
        trace_grad += right[at : at + 1, 64:65]
        trace_act += right[at : at + 1, 65:66]
    damp_grad = DAMPING * trace_grad / counts[0]
    damp_act = DAMPING * trace_act / counts[1]
    scale[...] = jnp.broadcast_to(1.0 / (damp_act * damp_grad), (8, 128))
    row = lax.broadcasted_iota(jnp.int32, (R, R), 0)
    column = lax.broadcasted_iota(jnp.int32, (R, R), 1)
    identity = jnp.where(row == column, 1.0, 0.0)
    for w in work:
        w[:, R:] = identity
    for i in range(8):
        at, here = slice(i * 32, i * 32 + 32), i * 200
        work[0][at, :R] = damp_act * right[here + 144 : here + 176, :] + right[here + 80 : here + 112, :]
        work[1][at, :R] = damp_grad * right[here + 112 : here + 144, :] + right[here + 48 : here + 80, :]
    lower_inverses(work, (inverse_act, inverse_grad))


def factors(right, counts):
    whole = pl.BlockSpec(memory_space=pltpu.VMEM)
    return call(
        functools.partial(factor_kernel, counts),
        [array(R, R), array(R, R), array(8, 128)],
        in_specs=[whole],
        out_specs=[whole] * 3,
        scratch_shapes=[pltpu.VMEM((R, 2 * R), jnp.float32)] * 2,
        name="factors",
    )(right)


def applied(value, inverse):
    pieces = split(inverse)
    value = product(split(value), pieces, LAST)
    return product(split(value), pieces, INNER)


def last_kernel(
    left_sums, weight, range_grad, right, both, rows_act, inverse_act, inverse_grad, scale, out, sums, *pieces
):
    @pl.when(pl.program_id(0) == 0)
    def _():
        for i in range(8):
            sums[i * 48 : i * 48 + 48, :] = right[i * 200 : i * 200 + 48, :]
        solved = applied(rows_act[...], inverse_act[...])
        pieces[0][...], pieces[1][...] = split(solved)
        rest = sums[...] - product(split(solved), split(both[...]), INNER)
        pieces[2][...], pieces[3][...] = split(applied(rest, inverse_grad[...]))

    left = product((pieces[0][...], pieces[1][...]), split(left_sums[...]), INNER)
    range_pieces = split(range_grad[...])
    update = left + product((pieces[2][...], pieces[3][...]), range_pieces, INNER)
    out[...] = (weight[...] - update) * scale[0:1, 0:1]


def last_update(left_sums, weight, range_grad, *rest):
    count, columns = weight.shape
    return call(
        last_kernel,
        array(count, columns),
        grid=(columns // TILE,),
        in_specs=[
            pl.BlockSpec((R, TILE), lambda j: (0, j)),
            pl.BlockSpec((count, TILE), lambda j: (0, j)),
            pl.BlockSpec((R, TILE), lambda j: (0, j)),
        ]
        + [pl.BlockSpec(value.shape, lambda j: (0, 0)) for value in rest],
        out_specs=pl.BlockSpec((count, TILE), lambda j: (0, j)),
        scratch_shapes=[pltpu.VMEM((count, R), jnp.float32)]
        + [pltpu.VMEM((count, R), jnp.bfloat16)] * 4,
        name="last_update",
    )(left_sums, weight, range_grad, *rest)


def hand_over_dp(value):
    return lax.all_to_all(value, "dp", 0, 0, tiled=True)


def body(acts, grads_out, sketch_in, sketch_out, weight_grad):
    tokens_all = acts.shape[0] * lax.axis_size("dp")
    columns = weight_grad.shape[1]
    core_id = lax.axis_index("tensor") % 2
    places = jnp.stack([tensor_chunk(), core_id]).astype(jnp.int32)
    width = R // 8

    part, sq_one = sketches(1 - core_id, grads_out, acts, sketch_out, sketch_in)
    other = swap_cores(part)
    part, sq_two = sketches(core_id, grads_out, acts, sketch_out, sketch_in)
    part = exchange_x(part + other)
    part = jnp.sum(part.reshape(4, -1, 2 * R), axis=0)
    own = exchange_x(jnp.tile(part, (4, 1)))
    other = swap_cores(own)

    piece, _ = scatter_dp(
        *ranges(places, own, other, grads_out, acts, sq_one, sq_two, tokens_all)
    )
    gathered = lax.all_gather(piece, "dp", axis=0, tiled=True)

    at = columns + 128
    piece = jnp.concatenate([piece[:, at + i * R : at + i * R + R] for i in range(3)])
    moves = []
    for d in range(16):
        for t in range(8):
            k = d % 8
            moves.append((d * 8 + t, (2 * t + d // 8) * 8 + 2 * (k % 4) + k // 4))
    rows_act = gather_tensor(lax.ppermute(piece, ("dp", "tensor"), moves))

    piece, after = scatter_dp(*left_products(rows_act, weight_grad))
    left_sums = lax.all_gather(piece, "dp", axis=0, tiled=True)

    part = scatter_tensor(right_products(gathered, weight_grad, after))
    extra = gathered[:, columns:at]
    cores = extra[:, : 2 * width].T
    rest = jnp.pad(extra[:8], ((0, 0), (0, R - 128)))
    part = jnp.concatenate([part, cores, rest, both_products(gathered, piece)])
    right = gather_tensor(part)
    both = lax.all_to_all(pack(right), "dp", 0, 0, tiled=True)

    counts = (float(tokens_all * FF), float(tokens_all * D))
    inverse_act, inverse_grad, scale = factors(right, counts)
    return last_update(
        left_sums, weight_grad, gathered, right, both, rows_act, inverse_act, inverse_grad, scale
    )


def solution(mesh):
    return jax.shard_map(
        body,
        mesh=mesh,
        in_specs=(
            P("dp", "tensor"),
            P("dp", "tensor"),
            P("tensor", None),
            P("tensor", None),
            P("dp", "tensor"),
        ),
        out_specs=P("dp", "tensor"),
        check_vma=False,
    )
```

```python
import functools

import jax
import jax.numpy as jnp
from jax import lax
from jax.experimental import pallas as pl
from jax.experimental.pallas import tpu as pltpu
from jax.sharding import PartitionSpec as P

D = 6144
FF = 24576
R = 256
TILE = 512
BLOCK = 64
VMEM_LIMIT = 48 * 1024 * 1024
VMEM_MOST = 60 * 1024 * 1024

DAMPING = 0.1


def ring(kind, step):
    if kind == "y":
        return [(i, i // 4 * 4 + (i % 4 + step) % 4) for i in range(16)]
    if kind == "z":
        return [(i, (i // 4 + step) % 4 * 4 + i % 4) for i in range(16)]
    return [(i, (i // 2 + step) % 4 * 2 + i % 2) for i in range(8)]


def send(value, kind, step):
    return lax.ppermute(value, "tensor" if kind == "x" else "dp", ring(kind, step))


def swap_cores(value):
    return lax.ppermute(value, "tensor", [(i, i ^ 1) for i in range(8)])


def place(kind):
    if kind == "y":
        return lax.axis_index("dp") % 4
    if kind == "z":
        return lax.axis_index("dp") // 4
    return lax.axis_index("tensor") // 2


def rows(value, index, count):
    return lax.dynamic_slice_in_dim(value, index * count, count, 0)


def scatter_four(value, kind):
    here, count = place(kind), value.shape[0] // 4
    two, one, three = (
        send(rows(value, (here + step) % 4, count), kind, step) for step in (2, 1, 3)
    )
    return (rows(value, here, count) + two) + (one + three)


def gather_four(value, kind):
    two, one, three = (send(value, kind, step) for step in (2, 1, 3))
    return assemble((value, one, two, three), place(kind))


def assemble(parts, here):
    count = parts[0].shape[0]
    whole = jnp.zeros((4 * count,) + parts[0].shape[1:], parts[0].dtype)
    for step, part in enumerate(parts):
        whole = lax.dynamic_update_slice_in_dim(whole, part, (here - step) % 4 * count, 0)
    return whole


def scatter_dp(first, second):
    first, second = scatter_four(first, "y"), scatter_four(second, "z")
    both = [scatter_four(first, "z"), scatter_four(second, "y")]
    return jnp.concatenate(both), second


def store_groups(first, second, columns, value):
    for d in range(16):
        to = d % 4 * 4 + d // 4
        first[8 * to : 8 * to + 8, columns] = value[16 * d : 16 * d + 8]
        second[8 * d : 8 * d + 8, columns] = value[16 * d + 8 : 16 * d + 16]


def tensor_chunk():
    index = lax.axis_index("tensor")
    return index % 2 * 4 + index // 2


def scatter_tensor(value):
    core, half = lax.axis_index("tensor") % 2, value.shape[0] // 2
    other = swap_cores(rows(value, 1 - core, half))
    return scatter_four(rows(value, core, half) + other, "x")


def gather_cores(value):
    core = lax.axis_index("tensor") % 2
    other = swap_cores(value)
    low = jnp.where(core == 0, value, other)
    high = jnp.where(core == 0, other, value)
    return jnp.concatenate([low, high])


def gather_tensor(value):
    return gather_cores(gather_four(value, "x"))


def gather_rows(piece):
    parts = []
    for step in range(4):
        moves = []
        for d in range(16):
            for t in range(8):
                x, core = (d % 4 + step) % 4, d % 8 // 4
                moves.append((d * 8 + t, (2 * t + d // 8) * 8 + 2 * x + core))
        parts.append(lax.ppermute(piece, ("dp", "tensor"), moves))
    return gather_cores(assemble(parts, place("x")))


def split(value):
    high = value.astype(jnp.bfloat16)
    return high, (value - high.astype(jnp.float32)).astype(jnp.bfloat16)


def product(left, right, dims):
    (lh, ll), (rh, rl) = left, right
    (along_left,), (along_right,) = dims
    return lax.dot_general(
        jnp.concatenate([lh, lh, ll], axis=along_left),
        jnp.concatenate([rh, rl, rh], axis=along_right),
        (dims, ((), ())),
        preferred_element_type=jnp.float32,
    )


def call(kernel, out_shape, vmem=VMEM_LIMIT, **options):
    return pl.pallas_call(
        kernel,
        out_shape=out_shape,
        compiler_params=pltpu.CompilerParams(vmem_limit_bytes=vmem),
        **options,
    )


def array(*shape):
    return jax.ShapeDtypeStruct(shape, jnp.float32)


def sketch_kernel(core, grads, acts, sketch_out, sketch_in, out, squares, total_grad, total_act):
    step = pl.program_id(0)
    some = zip((grads, acts), (sketch_out, sketch_in), (total_grad, total_act))
    for i, (value, sketch, total) in enumerate(some):

        @pl.when(step == 0)
        def _():
            total[...] = jnp.zeros_like(total)

        out[:, i * R : i * R + R] = jnp.dot(
            value[...], sketch[...], preferred_element_type=jnp.float32
        )
        count, columns = value.shape
        for low in range(0, columns, 256):
            sums = jnp.zeros((16, 256), jnp.float32)
            for row in range(0, count, 16):
                sums += jnp.square(value[row : row + 16, low : low + 256].astype(jnp.float32))
            total[:, low : low + 256] += sums

        @pl.when(step == pl.num_programs(0) - 1)
        def _():
            whole = jnp.sum(total[...], keepdims=True)
            squares[8 * i : 8 * i + 8, :] = jnp.broadcast_to(whole, (8, 128))


def sketches(half, grads, acts, sketch_out, sketch_in):
    count = grads.shape[0] // 2
    step = 384
    steps = count // step
    tile = lambda columns: pl.BlockSpec((step, columns), lambda i, h: (h[0] * steps + i, 0))
    whole = lambda value: pl.BlockSpec(value.shape, lambda i, h: (0, 0))
    grid_spec = pltpu.PrefetchScalarGridSpec(
        num_scalar_prefetch=1,
        grid=(steps,),
        in_specs=[
            tile(grads.shape[1]),
            tile(acts.shape[1]),
            whole(sketch_out),
            whole(sketch_in),
        ],
        out_specs=[
            pl.BlockSpec((step, 2 * R), lambda i, h: (i, 0)),
            pl.BlockSpec((16, 128), lambda i, h: (0, 0)),
        ],
        scratch_shapes=[
            pltpu.VMEM((16, grads.shape[1]), jnp.float32),
            pltpu.VMEM((16, acts.shape[1]), jnp.float32),
        ],
    )
    return call(
        sketch_kernel,
        [array(count, 2 * R), array(16, 128)],
        vmem=VMEM_MOST,
        grid_spec=grid_spec,
        name="sketches",
    )(half.astype(jnp.int32).reshape(1), grads, acts, sketch_out, sketch_in)


LAST = ((1,), (1,))
INNER = ((1,), (0,))


def flip_halves(core, own, other, flipped):
    half = own.shape[0]
    flipped[:, pl.ds(pl.multiple_of(core * half, 128), half)] = own[...].T
    flipped[:, pl.ds(pl.multiple_of((1 - core) * half, 128), half)] = other[...].T


def ranges_kernel(
    tokens_all, places, own, other, grads, acts, sq_one, sq_two, first, second, flipped, rounded, range_act
):
    step = pl.program_id(0)
    columns = grads.shape[1]
    whole = pl.num_programs(0) * columns

    @pl.when(step == 0)
    def _():
        half = own.shape[0]
        flipped[:, pl.ds(pl.multiple_of(places[1] * half, 128), half)] = own[...].T
        flipped[:, pl.ds(pl.multiple_of((1 - places[1]) * half, 128), half)] = other[...].T
        rounded[...] = flipped[...].astype(jnp.bfloat16)

    part = jnp.dot(rounded[:R, :], grads[...], preferred_element_type=jnp.float32)
    to = pl.ds(pl.multiple_of(step * columns, 128), columns)
    store_groups(first, second, to, part * (1.0 / tokens_all))

    @pl.when(step == pl.num_programs(0) - 1)
    def _():
        cores = []
        for low in (0, R):
            some = flipped[pl.ds(pl.multiple_of(low + places[0] * 32, 32), 32), :]
            core = product(split(flipped[low : low + R, :]), split(some), LAST)
            cores.append(core * (1.0 / tokens_all))
        lane = lax.broadcasted_iota(jnp.int32, (R, 64), 1)
        squares = sq_one[...] + sq_two[...]
        traces = jnp.where(lane == 0, squares[0:1, 0:1], 0.0)
        traces = jnp.where(lane == 1, squares[8:9, 0:1], traces)
        rest = jnp.concatenate(cores + [traces], axis=1)
        store_groups(first, second, pl.ds(whole, 128), rest)
        part = jnp.dot(rounded[R:, :], acts[...], preferred_element_type=jnp.float32)
        range_act[...] = part.T * (1.0 / tokens_all)
        for d in range(16):
            for i in range(3):
                to = pl.ds(whole + 128 + i * R, R)
                at, here = d % 4 * 4 + d // 4, 48 * d + 16 * i
                first[8 * at : 8 * at + 8, to] = range_act[here : here + 8, :]
                second[8 * d : 8 * d + 8, to] = range_act[here + 8 : here + 16, :]


def ranges(places, own, other, grads, acts, sq_one, sq_two, tokens_all):
    count, columns = grads.shape
    fixed = lambda shape: pl.BlockSpec(shape, lambda j, c: (0, 0))
    total = columns + 128 + 3 * R
    grid_spec = pltpu.PrefetchScalarGridSpec(
        num_scalar_prefetch=1,
        grid=(columns // TILE,),
        in_specs=[
            fixed(own.shape),
            fixed(other.shape),
            pl.BlockSpec((count, TILE), lambda j, c: (0, j)),
            fixed(acts.shape),
            fixed((16, 128)),
            fixed((16, 128)),
        ],
        out_specs=[fixed((R // 2, total))] * 2,
        scratch_shapes=[
            pltpu.VMEM((2 * R, count), jnp.float32),
            pltpu.VMEM((2 * R, count), jnp.bfloat16),
            pltpu.VMEM((acts.shape[1], R), jnp.float32),
        ],
    )
    return call(
        functools.partial(ranges_kernel, tokens_all),
        [array(R // 2, total)] * 2,
        grid_spec=grid_spec,
        name="ranges",
    )(places, own, other, grads, acts, sq_one, sq_two)


def left_kernel(rows_act, weight, first, second, high, low):
    step = pl.program_id(0)
    columns = weight.shape[1]

    @pl.when(step == 0)
    def _():
        high[...], low[...] = split(rows_act[...].T)

    part = product((high[...], low[...]), split(weight[...]), INNER)
    store_groups(first, second, pl.ds(pl.multiple_of(step * columns, 128), columns), part)


def left_products(rows_act, weight):
    count, columns = weight.shape
    return call(
        left_kernel,
        [array(R // 2, columns)] * 2,
        grid=(columns // TILE,),
        in_specs=[
            pl.BlockSpec((count, R), lambda j: (0, 0)),
            pl.BlockSpec((count, TILE), lambda j: (0, j)),
        ],
        out_specs=[pl.BlockSpec((R // 2, columns), lambda j: (0, 0))] * 2,
        scratch_shapes=[pltpu.VMEM((R, count), jnp.bfloat16)] * 2,
        name="left_products",
    )(rows_act, weight)


def right_kernel(whole, *refs):
    extra, (weight, after, sums) = refs[:6], refs[6:]

    @pl.when(pl.program_id(0) == 0)
    def _():
        sums[...] = jnp.zeros_like(sums)
        blocks = [jnp.concatenate([extra[i][...], extra[i + 1][...]], axis=1) for i in (0, 2, 4)]
        pieces = split(jnp.concatenate(blocks))
        gram = product(pieces, pieces, ((0,), (0,)))
        for i in range(8):
            sums[i * 112 + 80 : i * 112 + 112, :] = gram[i * 32 : i * 32 + 32]

    ranges = split(whole[...])
    right = product(split(weight[...]), ranges, LAST)
    gram = product(ranges, ranges, LAST)
    for i in range(8):
        at = i * 112
        sums[at : at + 48, :] += right[i * 48 : i * 48 + 48]
        sums[at + 48 : at + 80, :] += gram[i * 32 : i * 32 + 32]


def right_products(gathered, weight, after):
    count, columns = weight.shape
    extra = lambda i: pl.BlockSpec((R, 128), lambda j: (0, columns // 128 + 1 + i))
    return call(
        right_kernel,
        array(896, R),
        grid=(columns // TILE,),
        in_specs=[pl.BlockSpec((R, TILE), lambda j: (0, j))]
        + [extra(i) for i in range(6)]
        + [
            pl.BlockSpec((count, TILE), lambda j: (0, j)),
            pl.BlockSpec(memory_space=pl.ANY),
        ],
        out_specs=pl.BlockSpec((896, R), lambda j: (0, 0)),
        vmem=VMEM_MOST,
        name="right_products",
    )(*[gathered] * 7, weight, after)


def both_kernel(whole, left, out):
    @pl.when(pl.program_id(0) == 0)
    def _():
        out[...] = jnp.zeros_like(out)

    out[...] += product(split(left[...]), split(whole[...]), LAST)


def both_products(gathered, left):
    count, columns = left.shape
    return call(
        both_kernel,
        array(count, R),
        grid=(columns // 1024,),
        in_specs=[
            pl.BlockSpec((R, 1024), lambda j: (0, j)),
            pl.BlockSpec((count, 1024), lambda j: (0, j)),
        ],
        out_specs=pl.BlockSpec((count, R), lambda j: (0, 0)),
        vmem=VMEM_MOST,
        name="both_products",
    )(gathered, left)


def pack_kernel(right, out):
    total = right[184:200, :]
    for i in range(1, 8):
        total += right[i * 200 + 184 : i * 200 + 200, :]
    for d in range(16):
        out[16 * d : 16 * d + 16, :] = total


def pack(right):
    whole = pl.BlockSpec(memory_space=pltpu.VMEM)
    return call(pack_kernel, array(R, R), in_specs=[whole], out_specs=whole, name="pack")(right)


def exact(left, right, dims):
    return lax.dot_general(
        left,
        right,
        (dims, ((), ())),
        precision=lax.Precision.HIGHEST,
        preferred_element_type=jnp.float32,
    )


def spread(value):
    return jnp.broadcast_to(value, (8, 2 * BLOCK))


def eliminate(matrices):
    sub = lax.broadcasted_iota(jnp.int32, (8, 2 * BLOCK), 0)
    count = BLOCK // 8
    groups = [[m[8 * i : 8 * i + 8] for i in range(count)] for m in matrices]
    for at in range(count):
        k = 8 * at
        for group in groups:
            tile = group[at]
            lines = [spread(tile[j : j + 1]) for j in range(8)]
            pivot = {
                (j, l): spread(lines[j][:, k + l : k + l + 1])
                for j in range(8)
                for l in range(j, 8)
            }
            scaled, factor = [], {}
            for j in range(8):
                inverse = 1.0 / pivot[j, j]
                scaled.append(lines[j] * inverse)
                for l in range(j + 1, 8):
                    factor[j, l] = pivot[j, l] * inverse
                    for m in range(l, 8):
                        pivot[l, m] = pivot[l, m] - factor[j, l] * pivot[j, m]
                    lines[l] = lines[l] - factor[j, l] * lines[j]
            for i in range(at + 1, count):
                value, sums, columns = group[i], None, []
                for j in range(8):
                    column = spread(value[:, k + j : k + j + 1])
                    for q in range(j):
                        column = column - columns[q] * factor[q, j]
                    columns.append(column)
                    term = column * scaled[j]
                    sums = term if sums is None else sums + term
                group[i] = value - sums
            for j in range(8):
                tile = jnp.where(sub == j, lines[j] * lax.rsqrt(pivot[j, j]), tile)
            group[at] = tile
    return [jnp.concatenate(group, axis=0) for group in groups]


def lower_inverses(work, outs):
    row = lax.broadcasted_iota(jnp.int32, (BLOCK, BLOCK), 0)
    column = lax.broadcasted_iota(jnp.int32, (BLOCK, BLOCK), 1)
    identity = jnp.where(row == column, 1.0, 0.0)
    for low in range(0, R, BLOCK):
        high = low + BLOCK
        done = eliminate(
            [jnp.concatenate([w[low:high, low:high], identity], axis=1) for w in work]
        )
        for w, corner, out in zip(work, done, outs):
            corner = jnp.where(row >= column, corner[:, BLOCK:], 0.0)
            line = exact(corner, w[low:high, :], INNER)
            out[low:high, :] = line[:, R:]
            if high < R:
                w[high:, :] -= exact(line[:, high:R], line, ((0,), (0,)))


def factor_kernel(counts, right, inverse_act, inverse_grad, scale, *work):
    trace_grad, trace_act = jnp.zeros((1, 1)), jnp.zeros((1, 1))
    for i in range(8):
        at = i * 200 + 176
        trace_grad += right[at : at + 1, 64:65]
        trace_act += right[at : at + 1, 65:66]
    damp_grad = DAMPING * trace_grad / counts[0]
    damp_act = DAMPING * trace_act / counts[1]
    scale[...] = jnp.broadcast_to(1.0 / (damp_act * damp_grad), (8, 128))
    row = lax.broadcasted_iota(jnp.int32, (R, R), 0)
    column = lax.broadcasted_iota(jnp.int32, (R, R), 1)
    identity = jnp.where(row == column, 1.0, 0.0)
    for w in work:
        w[:, R:] = identity
    for i in range(8):
        at, here = slice(i * 32, i * 32 + 32), i * 200
        work[0][at, :R] = damp_act * right[here + 144 : here + 176, :] + right[here + 80 : here + 112, :]
        work[1][at, :R] = damp_grad * right[here + 112 : here + 144, :] + right[here + 48 : here + 80, :]
    lower_inverses(work, (inverse_act, inverse_grad))


def factors(right, counts):
    whole = pl.BlockSpec(memory_space=pltpu.VMEM)
    return call(
        functools.partial(factor_kernel, counts),
        [array(R, R), array(R, R), array(8, 128)],
        in_specs=[whole],
        out_specs=[whole] * 3,
        scratch_shapes=[pltpu.VMEM((R, 2 * R), jnp.float32)] * 2,
        name="factors",
    )(right)


def applied(value, inverse):
    pieces = split(inverse)
    value = product(split(value), pieces, LAST)
    return product(split(value), pieces, INNER)


def last_kernel(
    left_sums, weight, range_grad, right, both, rows_act, inverse_act, inverse_grad, scale, out, sums, *pieces
):
    @pl.when(pl.program_id(0) == 0)
    def _():
        for i in range(8):
            sums[i * 48 : i * 48 + 48, :] = right[i * 200 : i * 200 + 48, :]
        solved = applied(rows_act[...], inverse_act[...])
        pieces[0][...], pieces[1][...] = split(solved)
        rest = sums[...] - product(split(solved), split(both[...]), INNER)
        pieces[2][...], pieces[3][...] = split(applied(rest, inverse_grad[...]))

    left = product((pieces[0][...], pieces[1][...]), split(left_sums[...]), INNER)
    range_pieces = split(range_grad[...])
    update = left + product((pieces[2][...], pieces[3][...]), range_pieces, INNER)
    out[...] = (weight[...] - update) * scale[0:1, 0:1]


def last_update(left_sums, weight, range_grad, *rest):
    count, columns = weight.shape
    return call(
        last_kernel,
        array(count, columns),
        grid=(columns // TILE,),
        in_specs=[
            pl.BlockSpec((R, TILE), lambda j: (0, j)),
            pl.BlockSpec((count, TILE), lambda j: (0, j)),
            pl.BlockSpec((R, TILE), lambda j: (0, j)),
        ]
        + [pl.BlockSpec(value.shape, lambda j: (0, 0)) for value in rest],
        out_specs=pl.BlockSpec((count, TILE), lambda j: (0, j)),
        scratch_shapes=[pltpu.VMEM((count, R), jnp.float32)]
        + [pltpu.VMEM((count, R), jnp.bfloat16)] * 4,
        vmem=VMEM_MOST,
        name="last_update",
    )(left_sums, weight, range_grad, *rest)


def hand_over_dp(value):
    return lax.all_to_all(value, "dp", 0, 0, tiled=True)


def body(acts, grads_out, sketch_in, sketch_out, weight_grad):
    tokens_all = acts.shape[0] * lax.axis_size("dp")
    columns = weight_grad.shape[1]
    core_id = lax.axis_index("tensor") % 2
    places = jnp.stack([tensor_chunk(), core_id]).astype(jnp.int32)
    width = R // 8

    part, sq_one = sketches(1 - core_id, grads_out, acts, sketch_out, sketch_in)
    other = swap_cores(part)
    part, sq_two = sketches(core_id, grads_out, acts, sketch_out, sketch_in)
    own = gather_four(scatter_four(part + other, "x"), "x")
    other = swap_cores(own)

    piece, _ = scatter_dp(
        *ranges(places, own, other, grads_out, acts, sq_one, sq_two, tokens_all)
    )
    gathered = lax.all_gather(piece, "dp", axis=0, tiled=True)

    at = columns + 128
    piece = jnp.concatenate([piece[:, at + i * R : at + i * R + R] for i in range(3)])
    rows_act = gather_rows(piece)

    piece, after = scatter_dp(*left_products(rows_act, weight_grad))
    left_sums = lax.all_gather(piece, "dp", axis=0, tiled=True)

    part = scatter_tensor(right_products(gathered, weight_grad, after))
    extra = gathered[:, columns:at]
    cores = extra[:, : 2 * width].T
    rest = jnp.pad(extra[:8], ((0, 0), (0, R - 128)))
    part = jnp.concatenate([part, cores, rest, both_products(gathered, piece)])
    right = gather_tensor(part)
    both = lax.all_to_all(pack(right), "dp", 0, 0, tiled=True)

    counts = (float(tokens_all * FF), float(tokens_all * D))
    inverse_act, inverse_grad, scale = factors(right, counts)
    return last_update(
        left_sums, weight_grad, gathered, right, both, rows_act, inverse_act, inverse_grad, scale
    )


def solution(mesh):
    return jax.shard_map(
        body,
        mesh=mesh,
        in_specs=(
            P("dp", "tensor"),
            P("dp", "tensor"),
            P("tensor", None),
            P("tensor", None),
            P("dp", "tensor"),
        ),
        out_specs=P("dp", "tensor"),
        check_vma=False,
    )
```

```python
import functools

import jax
import jax.numpy as jnp
from jax import lax
from jax.experimental import pallas as pl
from jax.experimental.pallas import tpu as pltpu
from jax.sharding import PartitionSpec as P

D = 6144
FF = 24576
R = 256
TILE = 1024
BLOCK = 64
VMEM_LIMIT = 48 * 1024 * 1024
VMEM_MOST = 60 * 1024 * 1024

DAMPING = 0.1


def ring(kind, step):
    if kind == "y":
        return [(i, i // 4 * 4 + (i % 4 + step) % 4) for i in range(16)]
    if kind == "z":
        return [(i, (i // 4 + step) % 4 * 4 + i % 4) for i in range(16)]
    return [(i, (i // 2 + step) % 4 * 2 + i % 2) for i in range(8)]


def send(value, kind, step):
    return lax.ppermute(value, "tensor" if kind == "x" else "dp", ring(kind, step))


def swap_cores(value):
    return lax.ppermute(value, "tensor", [(i, i ^ 1) for i in range(8)])


def place(kind):
    if kind == "y":
        return lax.axis_index("dp") % 4
    if kind == "z":
        return lax.axis_index("dp") // 4
    return lax.axis_index("tensor") // 2


def rows(value, index, count):
    return lax.dynamic_slice_in_dim(value, index * count, count, 0)


def scatter_blocks(blocks, kind):
    two, one, three = (send(blocks[step], kind, step) for step in (2, 1, 3))
    return (blocks[0] + two) + (one + three)


def scatter_four(value, kind):
    here, count = place(kind), value.shape[0] // 4
    return scatter_blocks([rows(value, (here + step) % 4, count) for step in range(4)], kind)


def gather_four(value, kind):
    two, one, three = (send(value, kind, step) for step in (2, 1, 3))
    return assemble((value, one, two, three), place(kind))


def assemble(parts, here):
    count = parts[0].shape[0]
    whole = jnp.zeros((4 * count,) + parts[0].shape[1:], parts[0].dtype)
    for step, part in enumerate(parts):
        whole = lax.dynamic_update_slice_in_dim(whole, part, (here - step) % 4 * count, 0)
    return whole


def scatter_dp(blocks):
    first, second = scatter_blocks(blocks[:4], "y"), scatter_blocks(blocks[4:], "z")
    return jnp.concatenate([scatter_four(first, "z"), scatter_four(second, "y")])


def store_blocks(blocks, places, columns, value, stride=16):
    y, z = places[2], places[3]
    for step in range(4):
        for other in range(4):
            to = slice(8 * other, 8 * other + 8)
            at = (4 * other + lax.rem(y + step, 4)) * stride
            blocks[step][to, columns] = value[pl.ds(pl.multiple_of(at, 8), 8), :]
            at = (4 * lax.rem(z + step, 4) + other) * stride + 8
            blocks[4 + step][to, columns] = value[pl.ds(pl.multiple_of(at, 8), 8), :]


def tensor_chunk():
    index = lax.axis_index("tensor")
    return index % 2 * 4 + index // 2


def scatter_tensor(value):
    core, half = lax.axis_index("tensor") % 2, value.shape[0] // 2
    other = swap_cores(rows(value, 1 - core, half))
    return scatter_four(rows(value, core, half) + other, "x")


def gather_cores(value):
    core = lax.axis_index("tensor") % 2
    other = swap_cores(value)
    low = jnp.where(core == 0, value, other)
    high = jnp.where(core == 0, other, value)
    return jnp.concatenate([low, high])


def gather_tensor(value):
    return gather_cores(gather_four(value, "x"))


def gather_rows(piece):
    moves = []
    for d in range(16):
        for t in range(8):
            moves.append((d * 8 + t, (2 * t + d // 8) * 8 + 2 * (d % 4) + d % 8 // 4))
    return gather_tensor(lax.ppermute(piece, ("dp", "tensor"), moves))


def split(value):
    high = value.astype(jnp.bfloat16)
    return high, (value - high.astype(jnp.float32)).astype(jnp.bfloat16)


def product(left, right, dims):
    (lh, ll), (rh, rl) = left, right
    (along_left,), (along_right,) = dims
    return lax.dot_general(
        jnp.concatenate([lh, lh, ll], axis=along_left),
        jnp.concatenate([rh, rl, rh], axis=along_right),
        (dims, ((), ())),
        preferred_element_type=jnp.float32,
    )


def call(kernel, out_shape, vmem=VMEM_LIMIT, **options):
    return pl.pallas_call(
        kernel,
        out_shape=out_shape,
        compiler_params=pltpu.CompilerParams(vmem_limit_bytes=vmem),
        **options,
    )


def array(*shape):
    return jax.ShapeDtypeStruct(shape, jnp.float32)


def sketch_kernel(core, grads, acts, sketch_out, sketch_in, out, squares, total_grad, total_act):
    step = pl.program_id(0)
    some = zip((grads, acts), (sketch_out, sketch_in), (total_grad, total_act))
    for i, (value, sketch, total) in enumerate(some):

        @pl.when(step == 0)
        def _():
            total[...] = jnp.zeros_like(total)

        out[:, i * R : i * R + R] = jnp.dot(
            value[...], sketch[...], preferred_element_type=jnp.float32
        )
        count, columns = value.shape
        for low in range(0, columns, 256):
            sums = jnp.zeros((16, 256), jnp.float32)
            for row in range(0, count, 16):
                sums += jnp.square(value[row : row + 16, low : low + 256].astype(jnp.float32))
            total[:, low : low + 256] += sums

        @pl.when(step == pl.num_programs(0) - 1)
        def _():
            whole = jnp.sum(total[...], keepdims=True)
            squares[8 * i : 8 * i + 8, :] = jnp.broadcast_to(whole, (8, 128))


def sketches(half, grads, acts, sketch_out, sketch_in):
    count = grads.shape[0] // 2
    step = 384
    steps = count // step
    tile = lambda columns: pl.BlockSpec((step, columns), lambda i, h: (h[0] * steps + i, 0))
    whole = lambda value: pl.BlockSpec(value.shape, lambda i, h: (0, 0))
    grid_spec = pltpu.PrefetchScalarGridSpec(
        num_scalar_prefetch=1,
        grid=(steps,),
        in_specs=[
            tile(grads.shape[1]),
            tile(acts.shape[1]),
            whole(sketch_out),
            whole(sketch_in),
        ],
        out_specs=[
            pl.BlockSpec((step, 2 * R), lambda i, h: (i, 0)),
            pl.BlockSpec((16, 128), lambda i, h: (0, 0)),
        ],
        scratch_shapes=[
            pltpu.VMEM((16, grads.shape[1]), jnp.float32),
            pltpu.VMEM((16, acts.shape[1]), jnp.float32),
        ],
    )
    return call(
        sketch_kernel,
        [array(count, 2 * R), array(16, 128)],
        vmem=VMEM_MOST,
        grid_spec=grid_spec,
        name="sketches",
    )(half.astype(jnp.int32).reshape(1), grads, acts, sketch_out, sketch_in)


LAST = ((1,), (1,))
INNER = ((1,), (0,))


def flip_halves(core, own, other, flipped):
    half = own.shape[0]
    flipped[:, pl.ds(pl.multiple_of(core * half, 128), half)] = own[...].T
    flipped[:, pl.ds(pl.multiple_of((1 - core) * half, 128), half)] = other[...].T


def ranges_kernel(
    tokens_all, places, own, other, grads, acts, sq_one, sq_two, *refs
):
    blocks, (flipped, rounded, range_act, work) = refs[:8], refs[8:]
    step = pl.program_id(0)
    columns = grads.shape[1]
    whole = pl.num_programs(0) * columns

    @pl.when(step == 0)
    def _():
        half = own.shape[0]
        flipped[:, pl.ds(pl.multiple_of(places[1] * half, 128), half)] = own[...].T
        flipped[:, pl.ds(pl.multiple_of((1 - places[1]) * half, 128), half)] = other[...].T
        rounded[...] = flipped[...].astype(jnp.bfloat16)

    part = jnp.dot(rounded[:R, :], grads[...], preferred_element_type=jnp.float32)
    work[...] = part * (1.0 / tokens_all)
    store_blocks(blocks, places, pl.ds(pl.multiple_of(step * columns, 128), columns), work)

    @pl.when(step == pl.num_programs(0) - 1)
    def _():
        cores = []
        for low in (0, R):
            some = flipped[pl.ds(pl.multiple_of(low + places[0] * 32, 32), 32), :]
            core = product(split(flipped[low : low + R, :]), split(some), LAST)
            cores.append(core * (1.0 / tokens_all))
        lane = lax.broadcasted_iota(jnp.int32, (R, 64), 1)
        squares = sq_one[...] + sq_two[...]
        traces = jnp.where(lane == 0, squares[0:1, 0:1], 0.0)
        traces = jnp.where(lane == 1, squares[8:9, 0:1], traces)
        rest = jnp.concatenate(cores + [traces], axis=1)
        work[:, :128] = rest
        store_blocks(blocks, places, pl.ds(whole, 128), work.at[:, :128])
        part = jnp.dot(rounded[R:, :], acts[...], preferred_element_type=jnp.float32)
        range_act[...] = part.T * (1.0 / tokens_all)
        for i in range(3):
            to = pl.ds(whole + 128 + i * R, R)
            store_blocks(blocks, places, to, range_act.at[16 * i :, :], 48)


def ranges(places, own, other, grads, acts, sq_one, sq_two, tokens_all):
    count, columns = grads.shape
    fixed = lambda shape: pl.BlockSpec(shape, lambda j, c: (0, 0))
    total = columns + 128 + 3 * R
    grid_spec = pltpu.PrefetchScalarGridSpec(
        num_scalar_prefetch=1,
        grid=(columns // TILE,),
        in_specs=[
            fixed(own.shape),
            fixed(other.shape),
            pl.BlockSpec((count, TILE), lambda j, c: (0, j)),
            fixed(acts.shape),
            fixed((16, 128)),
            fixed((16, 128)),
        ],
        out_specs=[fixed((R // 8, total))] * 8,
        scratch_shapes=[
            pltpu.VMEM((2 * R, count), jnp.float32),
            pltpu.VMEM((2 * R, count), jnp.bfloat16),
            pltpu.VMEM((acts.shape[1], R), jnp.float32),
            pltpu.VMEM((R, TILE), jnp.float32),
        ],
    )
    return call(
        functools.partial(ranges_kernel, tokens_all),
        [array(R // 8, total)] * 8,
        grid_spec=grid_spec,
        name="ranges",
    )(places, own, other, grads, acts, sq_one, sq_two)


def left_kernel(places, rows_act, weight, *refs):
    blocks, (high, low, work) = refs[:8], refs[8:]
    step = pl.program_id(0)
    columns = weight.shape[1]

    @pl.when(step == 0)
    def _():
        high[...], low[...] = split(rows_act[...].T)

    work[...] = product((high[...], low[...]), split(weight[...]), INNER)
    store_blocks(blocks, places, pl.ds(pl.multiple_of(step * columns, 128), columns), work)


def left_products(places, rows_act, weight):
    count, columns = weight.shape
    grid_spec = pltpu.PrefetchScalarGridSpec(
        num_scalar_prefetch=1,
        grid=(columns // TILE,),
        in_specs=[
            pl.BlockSpec((count, R), lambda j, c: (0, 0)),
            pl.BlockSpec((count, TILE), lambda j, c: (0, j)),
        ],
        out_specs=[pl.BlockSpec((R // 8, columns), lambda j, c: (0, 0))] * 8,
        scratch_shapes=[pltpu.VMEM((R, count), jnp.bfloat16)] * 2
        + [pltpu.VMEM((R, TILE), jnp.float32)],
    )
    return call(
        left_kernel, [array(R // 8, columns)] * 8, grid_spec=grid_spec, name="left_products"
    )(places, rows_act, weight)


def right_kernel(whole, *refs):
    extra, (weight, left, sums, both) = refs[:6], refs[6:]

    @pl.when(pl.program_id(0) == 0)
    def _():
        sums[...] = jnp.zeros_like(sums)
        both[...] = jnp.zeros_like(both)
        blocks = [jnp.concatenate([extra[i][...], extra[i + 1][...]], axis=1) for i in (0, 2, 4)]
        pieces = split(jnp.concatenate(blocks))
        gram = product(pieces, pieces, ((0,), (0,)))
        for i in range(8):
            sums[i * 112 + 80 : i * 112 + 112, :] = gram[i * 32 : i * 32 + 32]

    ranges = split(whole[...])
    right = product(split(weight[...]), ranges, LAST)
    gram = product(ranges, ranges, LAST)
    for i in range(8):
        at = i * 112
        sums[at : at + 48, :] += right[i * 48 : i * 48 + 48]
        sums[at + 48 : at + 80, :] += gram[i * 32 : i * 32 + 32]
    both[...] += product(split(left[...]), ranges, LAST)


def right_products(gathered, weight, left):
    count, columns = weight.shape
    extra = lambda i: pl.BlockSpec((R, 128), lambda j: (0, columns // 128 + 1 + i))
    return call(
        right_kernel,
        [array(896, R), array(16, R)],
        grid=(columns // TILE,),
        in_specs=[pl.BlockSpec((R, TILE), lambda j: (0, j))]
        + [extra(i) for i in range(6)]
        + [
            pl.BlockSpec((count, TILE), lambda j: (0, j)),
            pl.BlockSpec((16, TILE), lambda j: (0, j)),
        ],
        out_specs=[
            pl.BlockSpec((896, R), lambda j: (0, 0)),
            pl.BlockSpec((16, R), lambda j: (0, 0)),
        ],
        vmem=VMEM_MOST,
        name="right_products",
    )(*[gathered] * 7, weight, left)


def pack_kernel(right, out):
    total = right[184:200, :]
    for i in range(1, 8):
        total += right[i * 200 + 184 : i * 200 + 200, :]
    for d in range(16):
        out[16 * d : 16 * d + 16, :] = total


def pack(right):
    whole = pl.BlockSpec(memory_space=pltpu.VMEM)
    return call(pack_kernel, array(R, R), in_specs=[whole], out_specs=whole, name="pack")(right)


def exact(left, right, dims):
    return lax.dot_general(
        left,
        right,
        (dims, ((), ())),
        precision=lax.Precision.HIGHEST,
        preferred_element_type=jnp.float32,
    )


def spread(value):
    return jnp.broadcast_to(value, (8, 2 * BLOCK))


def eliminate(matrices):
    sub = lax.broadcasted_iota(jnp.int32, (8, 2 * BLOCK), 0)
    count = BLOCK // 8
    groups = [[m[8 * i : 8 * i + 8] for i in range(count)] for m in matrices]
    for at in range(count):
        k = 8 * at
        for group in groups:
            tile = group[at]
            lines = [spread(tile[j : j + 1]) for j in range(8)]
            pivot = {
                (j, l): spread(lines[j][:, k + l : k + l + 1])
                for j in range(8)
                for l in range(j, 8)
            }
            scaled, factor = [], {}
            for j in range(8):
                inverse = 1.0 / pivot[j, j]
                scaled.append(lines[j] * inverse)
                for l in range(j + 1, 8):
                    factor[j, l] = pivot[j, l] * inverse
                    for m in range(l, 8):
                        pivot[l, m] = pivot[l, m] - factor[j, l] * pivot[j, m]
                    lines[l] = lines[l] - factor[j, l] * lines[j]
            for i in range(at + 1, count):
                value, sums, columns = group[i], None, []
                for j in range(8):
                    column = spread(value[:, k + j : k + j + 1])
                    for q in range(j):
                        column = column - columns[q] * factor[q, j]
                    columns.append(column)
                    term = column * scaled[j]
                    sums = term if sums is None else sums + term
                group[i] = value - sums
            for j in range(8):
                tile = jnp.where(sub == j, lines[j] * lax.rsqrt(pivot[j, j]), tile)
            group[at] = tile
    return [jnp.concatenate(group, axis=0) for group in groups]


def lower_inverses(work, outs):
    row = lax.broadcasted_iota(jnp.int32, (BLOCK, BLOCK), 0)
    column = lax.broadcasted_iota(jnp.int32, (BLOCK, BLOCK), 1)
    identity = jnp.where(row == column, 1.0, 0.0)
    for low in range(0, R, BLOCK):
        high = low + BLOCK
        done = eliminate(
            [jnp.concatenate([w[low:high, low:high], identity], axis=1) for w in work]
        )
        for w, corner, out in zip(work, done, outs):
            corner = jnp.where(row >= column, corner[:, BLOCK:], 0.0)
            line = exact(corner, w[low:high, :], INNER)
            out[low:high, :] = line[:, R:]
            if high < R:
                w[high:, :] -= exact(line[:, high:R], line, ((0,), (0,)))


def factor_kernel(counts, right, inverse_act, inverse_grad, scale, *work):
    trace_grad, trace_act = jnp.zeros((1, 1)), jnp.zeros((1, 1))
    for i in range(8):
        at = i * 200 + 176
        trace_grad += right[at : at + 1, 64:65]
        trace_act += right[at : at + 1, 65:66]
    damp_grad = DAMPING * trace_grad / counts[0]
    damp_act = DAMPING * trace_act / counts[1]
    scale[...] = jnp.broadcast_to(1.0 / (damp_act * damp_grad), (8, 128))
    row = lax.broadcasted_iota(jnp.int32, (R, R), 0)
    column = lax.broadcasted_iota(jnp.int32, (R, R), 1)
    identity = jnp.where(row == column, 1.0, 0.0)
    for w in work:
        w[:, R:] = identity
    for i in range(8):
        at, here = slice(i * 32, i * 32 + 32), i * 200
        work[0][at, :R] = damp_act * right[here + 144 : here + 176, :] + right[here + 80 : here + 112, :]
        work[1][at, :R] = damp_grad * right[here + 112 : here + 144, :] + right[here + 48 : here + 80, :]
    lower_inverses(work, (inverse_act, inverse_grad))


def factors(right, counts):
    whole = pl.BlockSpec(memory_space=pltpu.VMEM)
    return call(
        functools.partial(factor_kernel, counts),
        [array(R, R), array(R, R), array(8, 128)],
        in_specs=[whole],
        out_specs=[whole] * 3,
        scratch_shapes=[pltpu.VMEM((R, 2 * R), jnp.float32)] * 2,
        name="factors",
    )(right)


def applied(value, inverse):
    pieces = split(inverse)
    value = product(split(value), pieces, LAST)
    return product(split(value), pieces, INNER)


def last_kernel(
    left_sums, weight, range_grad, right, both, rows_act, inverse_act, inverse_grad, scale, out, sums, *pieces
):
    @pl.when(pl.program_id(0) == 0)
    def _():
        for i in range(8):
            sums[i * 48 : i * 48 + 48, :] = right[i * 200 : i * 200 + 48, :]
        solved = applied(rows_act[...], inverse_act[...])
        pieces[0][...], pieces[1][...] = split(solved)
        rest = sums[...] - product(split(solved), split(both[...]), INNER)
        pieces[2][...], pieces[3][...] = split(applied(rest, inverse_grad[...]))

    left = product((pieces[0][...], pieces[1][...]), split(left_sums[...]), INNER)
    range_pieces = split(range_grad[...])
    update = left + product((pieces[2][...], pieces[3][...]), range_pieces, INNER)
    out[...] = (weight[...] - update) * scale[0:1, 0:1]


def last_update(left_sums, weight, range_grad, *rest):
    count, columns = weight.shape
    return call(
        last_kernel,
        array(count, columns),
        grid=(columns // TILE,),
        in_specs=[
            pl.BlockSpec((R, TILE), lambda j: (0, j)),
            pl.BlockSpec((count, TILE), lambda j: (0, j)),
            pl.BlockSpec((R, TILE), lambda j: (0, j)),
        ]
        + [pl.BlockSpec(value.shape, lambda j: (0, 0)) for value in rest],
        out_specs=pl.BlockSpec((count, TILE), lambda j: (0, j)),
        scratch_shapes=[pltpu.VMEM((count, R), jnp.float32)]
        + [pltpu.VMEM((count, R), jnp.bfloat16)] * 4,
        name="last_update",
    )(left_sums, weight, range_grad, *rest)


def hand_over_dp(value):
    return lax.all_to_all(value, "dp", 0, 0, tiled=True)


def body(acts, grads_out, sketch_in, sketch_out, weight_grad):
    tokens_all = acts.shape[0] * lax.axis_size("dp")
    columns = weight_grad.shape[1]
    core_id = lax.axis_index("tensor") % 2
    places = jnp.stack([tensor_chunk(), core_id, place("y"), place("z")]).astype(jnp.int32)
    width = R // 8

    part, sq_one = sketches(1 - core_id, grads_out, acts, sketch_out, sketch_in)
    other = swap_cores(part)
    part, sq_two = sketches(core_id, grads_out, acts, sketch_out, sketch_in)
    own = gather_four(scatter_four(part + other, "x"), "x")
    other = swap_cores(own)

    piece = scatter_dp(
        ranges(places, own, other, grads_out, acts, sq_one, sq_two, tokens_all)
    )
    gathered = lax.all_gather(piece, "dp", axis=0, tiled=True)

    at = columns + 128
    piece = jnp.concatenate([piece[:, at + i * R : at + i * R + R] for i in range(3)])
    rows_act = gather_rows(piece)

    piece = scatter_dp(left_products(places, rows_act, weight_grad))
    left_sums = lax.all_gather(piece, "dp", axis=0, tiled=True)

    part, both = right_products(gathered, weight_grad, piece)
    part = scatter_tensor(part)
    extra = gathered[:, columns:at]
    cores = extra[:, : 2 * width].T
    rest = jnp.pad(extra[:8], ((0, 0), (0, R - 128)))
    part = jnp.concatenate([part, cores, rest, both])
    right = gather_tensor(part)
    both = lax.all_to_all(pack(right), "dp", 0, 0, tiled=True)

    counts = (float(tokens_all * FF), float(tokens_all * D))
    inverse_act, inverse_grad, scale = factors(right, counts)
    return last_update(
        left_sums, weight_grad, gathered, right, both, rows_act, inverse_act, inverse_grad, scale
    )


def solution(mesh):
    return jax.shard_map(
        body,
        mesh=mesh,
        in_specs=(
            P("dp", "tensor"),
            P("dp", "tensor"),
            P("tensor", None),
            P("tensor", None),
            P("dp", "tensor"),
        ),
        out_specs=P("dp", "tensor"),
        check_vma=False,
    )
```

```python
import functools

import jax
import jax.numpy as jnp
from jax import lax
from jax.experimental import pallas as pl
from jax.experimental.pallas import tpu as pltpu
from jax.sharding import PartitionSpec as P

D = 6144
FF = 24576
R = 256
TILE = 1024
BLOCK = 64
VMEM_LIMIT = 48 * 1024 * 1024
VMEM_MOST = 60 * 1024 * 1024

DAMPING = 0.1


def ring(kind, step):
    if kind == "y":
        return [(i, i // 4 * 4 + (i % 4 + step) % 4) for i in range(16)]
    if kind == "z":
        return [(i, (i // 4 + step) % 4 * 4 + i % 4) for i in range(16)]
    return [(i, (i // 2 + step) % 4 * 2 + i % 2) for i in range(8)]


def send(value, kind, step):
    return lax.ppermute(value, "tensor" if kind == "x" else "dp", ring(kind, step))


def swap_cores(value):
    return lax.ppermute(value, "tensor", [(i, i ^ 1) for i in range(8)])


def place(kind):
    if kind == "y":
        return lax.axis_index("dp") % 4
    if kind == "z":
        return lax.axis_index("dp") // 4
    return lax.axis_index("tensor") // 2


def rows(value, index, count):
    return lax.dynamic_slice_in_dim(value, index * count, count, 0)


def scatter_blocks(blocks, kind):
    two, one, three = (send(blocks[step], kind, step) for step in (2, 1, 3))
    return (blocks[0] + two) + (one + three)


def scatter_four(value, kind):
    here, count = place(kind), value.shape[0] // 4
    return scatter_blocks([rows(value, (here + step) % 4, count) for step in range(4)], kind)


def gather_four(value, kind):
    two, one, three = (send(value, kind, step) for step in (2, 1, 3))
    return assemble((value, one, two, three), place(kind))


def assemble(parts, here):
    count = parts[0].shape[0]
    whole = jnp.zeros((4 * count,) + parts[0].shape[1:], parts[0].dtype)
    for step, part in enumerate(parts):
        whole = lax.dynamic_update_slice_in_dim(whole, part, (here - step) % 4 * count, 0)
    return whole


def scatter_dp(blocks):
    first, second = scatter_blocks(blocks[:4], "y"), scatter_blocks(blocks[4:], "z")
    return jnp.concatenate([scatter_four(first, "z"), scatter_four(second, "y")])


def store_blocks(blocks, places, columns, value, stride=16):
    y, z = places[2], places[3]
    for step in range(4):
        for other in range(4):
            to = slice(8 * other, 8 * other + 8)
            at = (4 * other + lax.rem(y + step, 4)) * stride
            blocks[step][to, columns] = value[pl.ds(pl.multiple_of(at, 8), 8), :]
            at = (4 * lax.rem(z + step, 4) + other) * stride + 8
            blocks[4 + step][to, columns] = value[pl.ds(pl.multiple_of(at, 8), 8), :]


def tensor_chunk():
    index = lax.axis_index("tensor")
    return index % 2 * 4 + index // 2


def scatter_tensor(value):
    core, half = lax.axis_index("tensor") % 2, value.shape[0] // 2
    other = swap_cores(rows(value, 1 - core, half))
    return scatter_four(rows(value, core, half) + other, "x")


def gather_cores(value):
    core = lax.axis_index("tensor") % 2
    other = swap_cores(value)
    low = jnp.where(core == 0, value, other)
    high = jnp.where(core == 0, other, value)
    return jnp.concatenate([low, high])


def gather_tensor(value):
    return gather_cores(gather_four(value, "x"))


def gather_rows(piece):
    moves = []
    for d in range(16):
        for t in range(8):
            moves.append((d * 8 + t, (2 * t + d // 8) * 8 + 2 * (d % 4) + d % 8 // 4))
    return gather_tensor(lax.ppermute(piece, ("dp", "tensor"), moves))


def split(value):
    high = value.astype(jnp.bfloat16)
    return high, (value - high.astype(jnp.float32)).astype(jnp.bfloat16)


def product(left, right, dims):
    (lh, ll), (rh, rl) = left, right
    (along_left,), (along_right,) = dims
    return lax.dot_general(
        jnp.concatenate([lh, lh, ll], axis=along_left),
        jnp.concatenate([rh, rl, rh], axis=along_right),
        (dims, ((), ())),
        preferred_element_type=jnp.float32,
    )


def stacked_product(left, right, dims):
    (lh, ll), (rh, rl) = left, right
    count = lh.shape[0]
    dot = functools.partial(
        lax.dot_general, dimension_numbers=(dims, ((), ())), preferred_element_type=jnp.float32
    )
    both = dot(jnp.concatenate([lh, ll]), rh)
    return both[:count] + (both[count:] + dot(lh, rl))


def call(kernel, out_shape, vmem=VMEM_LIMIT, **options):
    return pl.pallas_call(
        kernel,
        out_shape=out_shape,
        compiler_params=pltpu.CompilerParams(vmem_limit_bytes=vmem),
        **options,
    )


def array(*shape):
    return jax.ShapeDtypeStruct(shape, jnp.float32)


def sketch_kernel(core, grads, acts, sketch_out, sketch_in, out, squares, total_grad, total_act):
    step = pl.program_id(0)
    some = zip((grads, acts), (sketch_out, sketch_in), (total_grad, total_act))
    for i, (value, sketch, total) in enumerate(some):

        @pl.when(step == 0)
        def _():
            total[...] = jnp.zeros_like(total)

        half = value.shape[0] // 2
        for at in (0, half):
            out[at : at + half, i * R : i * R + R] = jnp.dot(
                value[at : at + half, :], sketch[...], preferred_element_type=jnp.float32
            )
        count, columns = value.shape
        for low in range(0, columns, 256):
            sums = jnp.zeros((16, 256), jnp.float32)
            for row in range(0, count, 16):
                sums += jnp.square(value[row : row + 16, low : low + 256].astype(jnp.float32))
            total[:, low : low + 256] += sums

        @pl.when(step == pl.num_programs(0) - 1)
        def _():
            whole = jnp.sum(total[...], keepdims=True)
            squares[8 * i : 8 * i + 8, :] = jnp.broadcast_to(whole, (8, 128))


def sketches(half, grads, acts, sketch_out, sketch_in):
    count = grads.shape[0] // 2
    step = 384
    steps = count // step
    tile = lambda columns: pl.BlockSpec((step, columns), lambda i, h: (h[0] * steps + i, 0))
    whole = lambda value: pl.BlockSpec(value.shape, lambda i, h: (0, 0))
    grid_spec = pltpu.PrefetchScalarGridSpec(
        num_scalar_prefetch=1,
        grid=(steps,),
        in_specs=[
            tile(grads.shape[1]),
            tile(acts.shape[1]),
            whole(sketch_out),
            whole(sketch_in),
        ],
        out_specs=[
            pl.BlockSpec((step, 2 * R), lambda i, h: (i, 0)),
            pl.BlockSpec((16, 128), lambda i, h: (0, 0)),
        ],
        scratch_shapes=[
            pltpu.VMEM((16, grads.shape[1]), jnp.float32),
            pltpu.VMEM((16, acts.shape[1]), jnp.float32),
        ],
    )
    return call(
        sketch_kernel,
        [array(count, 2 * R), array(16, 128)],
        vmem=VMEM_MOST,
        grid_spec=grid_spec,
        name="sketches",
    )(half.astype(jnp.int32).reshape(1), grads, acts, sketch_out, sketch_in)


LAST = ((1,), (1,))
INNER = ((1,), (0,))


def flip_halves(core, own, other, flipped):
    half = own.shape[0]
    flipped[:, pl.ds(pl.multiple_of(core * half, 128), half)] = own[...].T
    flipped[:, pl.ds(pl.multiple_of((1 - core) * half, 128), half)] = other[...].T


def ranges_kernel(
    tokens_all, places, own, other, grads, acts, sq_one, sq_two, *refs
):
    blocks, (flipped, rounded, range_act, work) = refs[:8], refs[8:]
    step = pl.program_id(0)
    columns = grads.shape[1]
    whole = pl.num_programs(0) * columns

    @pl.when(step == 0)
    def _():
        half = own.shape[0]
        flipped[:, pl.ds(pl.multiple_of(places[1] * half, 128), half)] = own[...].T
        flipped[:, pl.ds(pl.multiple_of((1 - places[1]) * half, 128), half)] = other[...].T
        rounded[...] = flipped[...].astype(jnp.bfloat16)

    part = jnp.dot(rounded[:R, :], grads[...], preferred_element_type=jnp.float32)
    work[...] = part * (1.0 / tokens_all)
    store_blocks(blocks, places, pl.ds(pl.multiple_of(step * columns, 128), columns), work)

    @pl.when(step == pl.num_programs(0) - 1)
    def _():
        cores = []
        for low in (0, R):
            some = flipped[pl.ds(pl.multiple_of(low + places[0] * 32, 32), 32), :]
            core = product(split(flipped[low : low + R, :]), split(some), LAST)
            cores.append(core * (1.0 / tokens_all))
        lane = lax.broadcasted_iota(jnp.int32, (R, 64), 1)
        squares = sq_one[...] + sq_two[...]
        traces = jnp.where(lane == 0, squares[0:1, 0:1], 0.0)
        traces = jnp.where(lane == 1, squares[8:9, 0:1], traces)
        rest = jnp.concatenate(cores + [traces], axis=1)
        work[:, :128] = rest
        store_blocks(blocks, places, pl.ds(whole, 128), work.at[:, :128])
        part = jnp.dot(rounded[R:, :], acts[...], preferred_element_type=jnp.float32)
        range_act[...] = part.T * (1.0 / tokens_all)
        for i in range(3):
            to = pl.ds(whole + 128 + i * R, R)
            store_blocks(blocks, places, to, range_act.at[16 * i :, :], 48)


def ranges(places, own, other, grads, acts, sq_one, sq_two, tokens_all):
    count, columns = grads.shape
    fixed = lambda shape: pl.BlockSpec(shape, lambda j, c: (0, 0))
    total = columns + 128 + 3 * R
    grid_spec = pltpu.PrefetchScalarGridSpec(
        num_scalar_prefetch=1,
        grid=(columns // TILE,),
        in_specs=[
            fixed(own.shape),
            fixed(other.shape),
            pl.BlockSpec((count, TILE), lambda j, c: (0, j)),
            fixed(acts.shape),
            fixed((16, 128)),
            fixed((16, 128)),
        ],
        out_specs=[fixed((R // 8, total))] * 8,
        scratch_shapes=[
            pltpu.VMEM((2 * R, count), jnp.float32),
            pltpu.VMEM((2 * R, count), jnp.bfloat16),
            pltpu.VMEM((acts.shape[1], R), jnp.float32),
            pltpu.VMEM((R, TILE), jnp.float32),
        ],
    )
    return call(
        functools.partial(ranges_kernel, tokens_all),
        [array(R // 8, total)] * 8,
        grid_spec=grid_spec,
        name="ranges",
    )(places, own, other, grads, acts, sq_one, sq_two)


def left_kernel(places, rows_act, weight, *refs):
    blocks, (high, low, work) = refs[:8], refs[8:]
    step = pl.program_id(0)
    columns = weight.shape[1]

    @pl.when(step == 0)
    def _():
        high[...], low[...] = split(rows_act[...].T)

    work[...] = product((high[...], low[...]), split(weight[...]), INNER)
    store_blocks(blocks, places, pl.ds(pl.multiple_of(step * columns, 128), columns), work)


def left_products(places, rows_act, weight):
    count, columns = weight.shape
    grid_spec = pltpu.PrefetchScalarGridSpec(
        num_scalar_prefetch=1,
        grid=(columns // TILE,),
        in_specs=[
            pl.BlockSpec((count, R), lambda j, c: (0, 0)),
            pl.BlockSpec((count, TILE), lambda j, c: (0, j)),
        ],
        out_specs=[pl.BlockSpec((R // 8, columns), lambda j, c: (0, 0))] * 8,
        scratch_shapes=[pltpu.VMEM((R, count), jnp.bfloat16)] * 2
        + [pltpu.VMEM((R, TILE), jnp.float32)],
    )
    return call(
        left_kernel, [array(R // 8, columns)] * 8, grid_spec=grid_spec, name="left_products"
    )(places, rows_act, weight)


def right_kernel(whole, *refs):
    extra, (weight, left, sums, cores, both) = refs[:7], refs[7:]

    @pl.when(pl.program_id(0) == 0)
    def _():
        sums[...] = jnp.zeros_like(sums)
        both[...] = jnp.zeros_like(both)
        cores[...] = extra[0][...].T[:64]
        blocks = [jnp.concatenate([extra[i][...], extra[i + 1][...]], axis=1) for i in (1, 3, 5)]
        pieces = split(jnp.concatenate(blocks))
        gram = product(pieces, pieces, ((0,), (0,)))
        for i in range(8):
            sums[i * 120 + 80 : i * 120 + 112, :] = gram[i * 32 : i * 32 + 32]
            sums[i * 120 + 112 : i * 120 + 120, :128] = extra[0][:8, :]

    ranges = split(whole[...])
    lines = [split(weight[...]), ranges, split(left[...])]
    lines = [jnp.concatenate([line[i] for line in lines]) for i in range(2)]
    total = stacked_product(lines, ranges, LAST)
    count = weight.shape[0]
    for i in range(8):
        at, gram = i * 120, count + i * 32
        sums[at : at + 48, :] += total[i * 48 : i * 48 + 48]
        sums[at + 48 : at + 80, :] += total[gram : gram + 32]
    both[...] += total[count + R :]


def right_products(gathered, weight, left):
    count, columns = weight.shape
    extra = lambda i: pl.BlockSpec((R, 128), lambda j: (0, columns // 128 + i))
    fixed = lambda shape: pl.BlockSpec(shape, lambda j: (0, 0))
    return call(
        right_kernel,
        [array(960, R), array(64, R), array(16, R)],
        grid=(columns // TILE,),
        in_specs=[pl.BlockSpec((R, TILE), lambda j: (0, j))]
        + [extra(i) for i in range(7)]
        + [
            pl.BlockSpec((count, TILE), lambda j: (0, j)),
            pl.BlockSpec((16, TILE), lambda j: (0, j)),
        ],
        out_specs=[fixed((960, R)), fixed((64, R)), fixed((16, R))],
        vmem=VMEM_MOST,
        name="right_products",
    )(*[gathered] * 8, weight, left)


def combine_kernel(counts, sums, cores, both, out, scale):
    damp_grad = DAMPING * sums[112:113, 64:65] / counts[0]
    damp_act = DAMPING * sums[112:113, 65:66] / counts[1]
    scale[...] = jnp.broadcast_to(1.0 / (damp_act * damp_grad), (8, 128))
    out[0:48, :] = sums[0:48, :]
    out[48:80, :] = damp_grad * cores[0:32, :] + sums[48:80, :]
    out[80:112, :] = damp_act * cores[32:64, :] + sums[80:112, :]
    out[112:128, :] = both[...]


def combine(sums, cores, both, counts):
    whole = pl.BlockSpec(memory_space=pltpu.VMEM)
    return call(
        functools.partial(combine_kernel, counts),
        [array(128, R), array(8, 128)],
        in_specs=[whole] * 3,
        out_specs=[whole] * 2,
        name="combine",
    )(sums, cores, both)


def pack_kernel(right, out):
    total = right[112:128, :]
    for i in range(1, 8):
        total += right[i * 128 + 112 : i * 128 + 128, :]
    for d in range(16):
        out[16 * d : 16 * d + 16, :] = total


def pack(right):
    whole = pl.BlockSpec(memory_space=pltpu.VMEM)
    return call(pack_kernel, array(R, R), in_specs=[whole], out_specs=whole, name="pack")(right)


def exact(left, right, dims):
    return lax.dot_general(
        left,
        right,
        (dims, ((), ())),
        precision=lax.Precision.HIGHEST,
        preferred_element_type=jnp.float32,
    )


def spread(value):
    return jnp.broadcast_to(value, (8, 2 * BLOCK))


def eliminate(matrices):
    sub = lax.broadcasted_iota(jnp.int32, (8, 2 * BLOCK), 0)
    count = BLOCK // 8
    groups = [[m[8 * i : 8 * i + 8] for i in range(count)] for m in matrices]
    for at in range(count):
        k = 8 * at
        for group in groups:
            tile = group[at]
            lines = [spread(tile[j : j + 1]) for j in range(8)]
            pivot = {
                (j, l): spread(lines[j][:, k + l : k + l + 1])
                for j in range(8)
                for l in range(j, 8)
            }
            scaled, factor = [], {}
            for j in range(8):
                inverse = 1.0 / pivot[j, j]
                scaled.append(lines[j] * inverse)
                for l in range(j + 1, 8):
                    factor[j, l] = pivot[j, l] * inverse
                    for m in range(l, 8):
                        pivot[l, m] = pivot[l, m] - factor[j, l] * pivot[j, m]
                    lines[l] = lines[l] - factor[j, l] * lines[j]
            for i in range(at + 1, count):
                value, sums, columns = group[i], None, []
                for j in range(8):
                    column = spread(value[:, k + j : k + j + 1])
                    for q in range(j):
                        column = column - columns[q] * factor[q, j]
                    columns.append(column)
                    term = column * scaled[j]
                    sums = term if sums is None else sums + term
                group[i] = value - sums
            for j in range(8):
                tile = jnp.where(sub == j, lines[j] * lax.rsqrt(pivot[j, j]), tile)
            group[at] = tile
    return [jnp.concatenate(group, axis=0) for group in groups]


def lower_inverses(work, outs):
    row = lax.broadcasted_iota(jnp.int32, (BLOCK, BLOCK), 0)
    column = lax.broadcasted_iota(jnp.int32, (BLOCK, BLOCK), 1)
    identity = jnp.where(row == column, 1.0, 0.0)
    for low in range(0, R, BLOCK):
        high = low + BLOCK
        done = eliminate(
            [jnp.concatenate([w[low:high, low:high], identity], axis=1) for w in work]
        )
        for w, corner, out in zip(work, done, outs):
            corner = jnp.where(row >= column, corner[:, BLOCK:], 0.0)
            line = exact(corner, w[low:high, :], INNER)
            out[low:high, :] = line[:, R:]
            if high < R:
                w[high:, :] -= exact(line[:, high:R], line, ((0,), (0,)))


def factor_kernel(right, inverse_act, inverse_grad, *work):
    row = lax.broadcasted_iota(jnp.int32, (R, R), 0)
    column = lax.broadcasted_iota(jnp.int32, (R, R), 1)
    identity = jnp.where(row == column, 1.0, 0.0)
    for w in work:
        w[:, R:] = identity
    for i in range(8):
        at, here = slice(i * 32, i * 32 + 32), i * 128
        work[0][at, :R] = right[here + 80 : here + 112, :]
        work[1][at, :R] = right[here + 48 : here + 80, :]
    lower_inverses(work, (inverse_act, inverse_grad))


def factors(right):
    whole = pl.BlockSpec(memory_space=pltpu.VMEM)
    return call(
        factor_kernel,
        [array(R, R), array(R, R)],
        in_specs=[whole],
        out_specs=[whole] * 2,
        scratch_shapes=[pltpu.VMEM((R, 2 * R), jnp.float32)] * 2,
        name="factors",
    )(right)


def applied(value, inverse):
    pieces = split(inverse)
    value = product(split(value), pieces, LAST)
    return product(split(value), pieces, INNER)


def last_kernel(
    left_sums, weight, range_grad, right, both, rows_act, inverse_act, inverse_grad, scale, out, sums, *pieces
):
    @pl.when(pl.program_id(0) == 0)
    def _():
        for i in range(8):
            sums[i * 48 : i * 48 + 48, :] = right[i * 128 : i * 128 + 48, :]
        solved = applied(rows_act[...], inverse_act[...])
        pieces[0][...], pieces[1][...] = split(solved)
        rest = sums[...] - product(split(solved), split(both[...]), INNER)
        pieces[2][...], pieces[3][...] = split(applied(rest, inverse_grad[...]))

    left = product((pieces[0][...], pieces[1][...]), split(left_sums[...]), INNER)
    range_pieces = split(range_grad[...])
    update = left + product((pieces[2][...], pieces[3][...]), range_pieces, INNER)
    out[...] = (weight[...] - update) * scale[0:1, 0:1]


def last_update(left_sums, weight, range_grad, *rest):
    count, columns = weight.shape
    return call(
        last_kernel,
        array(count, columns),
        grid=(columns // TILE,),
        in_specs=[
            pl.BlockSpec((R, TILE), lambda j: (0, j)),
            pl.BlockSpec((count, TILE), lambda j: (0, j)),
            pl.BlockSpec((R, TILE), lambda j: (0, j)),
        ]
        + [pl.BlockSpec(value.shape, lambda j: (0, 0)) for value in rest],
        out_specs=pl.BlockSpec((count, TILE), lambda j: (0, j)),
        scratch_shapes=[pltpu.VMEM((count, R), jnp.float32)]
        + [pltpu.VMEM((count, R), jnp.bfloat16)] * 4,
        name="last_update",
    )(left_sums, weight, range_grad, *rest)


def hand_over_dp(value):
    return lax.all_to_all(value, "dp", 0, 0, tiled=True)


def body(acts, grads_out, sketch_in, sketch_out, weight_grad):
    tokens_all = acts.shape[0] * lax.axis_size("dp")
    columns = weight_grad.shape[1]
    core_id = lax.axis_index("tensor") % 2
    places = jnp.stack([tensor_chunk(), core_id, place("y"), place("z")]).astype(jnp.int32)

    part, sq_one = sketches(1 - core_id, grads_out, acts, sketch_out, sketch_in)
    other = swap_cores(part)
    part, sq_two = sketches(core_id, grads_out, acts, sketch_out, sketch_in)
    own = gather_four(scatter_four(part + other, "x"), "x")
    other = swap_cores(own)

    piece = scatter_dp(
        ranges(places, own, other, grads_out, acts, sq_one, sq_two, tokens_all)
    )
    gathered = lax.all_gather(piece, "dp", axis=0, tiled=True)

    at = columns + 128
    piece = jnp.concatenate([piece[:, at + i * R : at + i * R + R] for i in range(3)])
    rows_act = gather_rows(piece)

    piece = scatter_dp(left_products(places, rows_act, weight_grad))
    left_sums = lax.all_gather(piece, "dp", axis=0, tiled=True)

    counts = (float(tokens_all * FF), float(tokens_all * D))
    part, cores, both = right_products(gathered, weight_grad, piece)
    part, scale = combine(scatter_tensor(part), cores, both, counts)
    right = gather_tensor(part)
    both = lax.all_to_all(pack(right), "dp", 0, 0, tiled=True)

    inverse_act, inverse_grad = factors(right)
    return last_update(
        left_sums, weight_grad, gathered, right, both, rows_act, inverse_act, inverse_grad, scale
    )


def solution(mesh):
    return jax.shard_map(
        body,
        mesh=mesh,
        in_specs=(
            P("dp", "tensor"),
            P("dp", "tensor"),
            P("tensor", None),
            P("tensor", None),
            P("dp", "tensor"),
        ),
        out_specs=P("dp", "tensor"),
        check_vma=False,
    )
```

```python
import functools

import jax
import jax.numpy as jnp
from jax import lax
from jax.experimental import pallas as pl
from jax.experimental.pallas import tpu as pltpu
from jax.sharding import PartitionSpec as P

D = 6144
FF = 24576
R = 256
TILE = 1024
BLOCK = 64
VMEM_LIMIT = 48 * 1024 * 1024
VMEM_MOST = 60 * 1024 * 1024
VMEM_LAST = 58 * 1024 * 1024

DAMPING = 0.1


def ring(kind, step):
    if kind == "y":
        return [(i, i // 4 * 4 + (i % 4 + step) % 4) for i in range(16)]
    if kind == "z":
        return [(i, (i // 4 + step) % 4 * 4 + i % 4) for i in range(16)]
    return [(i, (i // 2 + step) % 4 * 2 + i % 2) for i in range(8)]


def send(value, kind, step):
    return lax.ppermute(value, "tensor" if kind == "x" else "dp", ring(kind, step))


def swap_cores(value):
    return lax.ppermute(value, "tensor", [(i, i ^ 1) for i in range(8)])


def place(kind):
    if kind == "y":
        return lax.axis_index("dp") % 4
    if kind == "z":
        return lax.axis_index("dp") // 4
    return lax.axis_index("tensor") // 2


def rows(value, index, count):
    return lax.dynamic_slice_in_dim(value, index * count, count, 0)


def scatter_blocks(blocks, kind):
    two, one, three = (send(blocks[step], kind, step) for step in (2, 1, 3))
    return (blocks[0] + two) + (one + three)


def scatter_four(value, kind):
    here, count = place(kind), value.shape[0] // 4
    return scatter_blocks([rows(value, (here + step) % 4, count) for step in range(4)], kind)


def gather_four(value, kind):
    two, one, three = (send(value, kind, step) for step in (2, 1, 3))
    return assemble((value, one, two, three), place(kind))


def assemble(parts, here):
    count = parts[0].shape[0]
    whole = jnp.zeros((4 * count,) + parts[0].shape[1:], parts[0].dtype)
    for step, part in enumerate(parts):
        whole = lax.dynamic_update_slice_in_dim(whole, part, (here - step) % 4 * count, 0)
    return whole


def scatter_dp(blocks):
    first, second = scatter_blocks(blocks[:4], "y"), scatter_blocks(blocks[4:], "z")
    return jnp.concatenate([scatter_four(first, "z"), scatter_four(second, "y")])


def store_blocks(blocks, places, columns, value, stride=16):
    y, z = places[2], places[3]
    for step in range(4):
        for other in range(4):
            to = slice(8 * other, 8 * other + 8)
            at = (4 * other + lax.rem(y + step, 4)) * stride
            blocks[step][to, columns] = value[pl.ds(pl.multiple_of(at, 8), 8), :]
            at = (4 * lax.rem(z + step, 4) + other) * stride + 8
            blocks[4 + step][to, columns] = value[pl.ds(pl.multiple_of(at, 8), 8), :]


def tensor_chunk():
    index = lax.axis_index("tensor")
    return index % 2 * 4 + index // 2


def scatter_tensor(value):
    core, half = lax.axis_index("tensor") % 2, value.shape[0] // 2
    other = swap_cores(rows(value, 1 - core, half))
    return scatter_four(rows(value, core, half) + other, "x")


def gather_cores(value):
    core = lax.axis_index("tensor") % 2
    other = swap_cores(value)
    low = jnp.where(core == 0, value, other)
    high = jnp.where(core == 0, other, value)
    return jnp.concatenate([low, high])


def gather_tensor(value):
    return gather_cores(gather_four(value, "x"))


def gather_rows(piece):
    moves = []
    for d in range(16):
        for t in range(8):
            moves.append((d * 8 + t, (2 * t + d // 8) * 8 + 2 * (d % 4) + d % 8 // 4))
    return gather_tensor(lax.ppermute(piece, ("dp", "tensor"), moves))


def split(value):
    high = value.astype(jnp.bfloat16)
    return high, (value - high.astype(jnp.float32)).astype(jnp.bfloat16)


def product(left, right, dims):
    (lh, ll), (rh, rl) = left, right
    (along_left,), (along_right,) = dims
    return lax.dot_general(
        jnp.concatenate([lh, lh, ll], axis=along_left),
        jnp.concatenate([rh, rl, rh], axis=along_right),
        (dims, ((), ())),
        preferred_element_type=jnp.float32,
    )


def stacked_product(left, right, dims):
    (lh, ll), (rh, rl) = left, right
    count = lh.shape[0]
    dot = functools.partial(
        lax.dot_general, dimension_numbers=(dims, ((), ())), preferred_element_type=jnp.float32
    )
    both = dot(jnp.concatenate([lh, ll]), rh)
    return both[:count] + (both[count:] + dot(lh, rl))


def call(kernel, out_shape, vmem=VMEM_LIMIT, **options):
    return pl.pallas_call(
        kernel,
        out_shape=out_shape,
        compiler_params=pltpu.CompilerParams(vmem_limit_bytes=vmem),
        **options,
    )


def array(*shape):
    return jax.ShapeDtypeStruct(shape, jnp.float32)


def sketch_kernel(core, grads, acts, sketch_out, sketch_in, out, squares, total_grad, total_act):
    step = pl.program_id(0)
    some = zip((grads, acts), (sketch_out, sketch_in), (total_grad, total_act))
    for i, (value, sketch, total) in enumerate(some):

        @pl.when(step == 0)
        def _():
            total[...] = jnp.zeros_like(total)

        half = value.shape[0] // 2
        for at in (0, half):
            out[at : at + half, i * R : i * R + R] = jnp.dot(
                value[at : at + half, :], sketch[...], preferred_element_type=jnp.float32
            )
        count, columns = value.shape
        for low in range(0, columns, 256):
            sums = jnp.zeros((16, 256), jnp.float32)
            for row in range(0, count, 16):
                sums += jnp.square(value[row : row + 16, low : low + 256].astype(jnp.float32))
            total[:, low : low + 256] += sums

        @pl.when(step == pl.num_programs(0) - 1)
        def _():
            whole = jnp.sum(total[...], keepdims=True)
            squares[8 * i : 8 * i + 8, :] = jnp.broadcast_to(whole, (8, 128))


def sketches(half, grads, acts, sketch_out, sketch_in):
    count = grads.shape[0] // 2
    step = 384
    steps = count // step
    tile = lambda columns: pl.BlockSpec((step, columns), lambda i, h: (h[0] * steps + i, 0))
    whole = lambda value: pl.BlockSpec(value.shape, lambda i, h: (0, 0))
    grid_spec = pltpu.PrefetchScalarGridSpec(
        num_scalar_prefetch=1,
        grid=(steps,),
        in_specs=[
            tile(grads.shape[1]),
            tile(acts.shape[1]),
            whole(sketch_out),
            whole(sketch_in),
        ],
        out_specs=[
            pl.BlockSpec((step, 2 * R), lambda i, h: (i, 0)),
            pl.BlockSpec((16, 128), lambda i, h: (0, 0)),
        ],
        scratch_shapes=[
            pltpu.VMEM((16, grads.shape[1]), jnp.float32),
            pltpu.VMEM((16, acts.shape[1]), jnp.float32),
        ],
    )
    return call(
        sketch_kernel,
        [array(count, 2 * R), array(16, 128)],
        vmem=VMEM_MOST,
        grid_spec=grid_spec,
        name="sketches",
    )(half.astype(jnp.int32).reshape(1), grads, acts, sketch_out, sketch_in)


LAST = ((1,), (1,))
INNER = ((1,), (0,))


def flip_halves(core, own, other, flipped):
    half = own.shape[0]
    flipped[:, pl.ds(pl.multiple_of(core * half, 128), half)] = own[...].T
    flipped[:, pl.ds(pl.multiple_of((1 - core) * half, 128), half)] = other[...].T


def ranges_kernel(
    tokens_all, places, own, other, grads, acts, sq_one, sq_two, *refs
):
    blocks, (flipped, rounded, range_act, work) = refs[:8], refs[8:]
    step = pl.program_id(0)
    columns = grads.shape[1]
    whole = pl.num_programs(0) * columns

    @pl.when(step == 0)
    def _():
        half = own.shape[0]
        flipped[:, pl.ds(pl.multiple_of(places[1] * half, 128), half)] = own[...].T
        flipped[:, pl.ds(pl.multiple_of((1 - places[1]) * half, 128), half)] = other[...].T
        rounded[...] = flipped[...].astype(jnp.bfloat16)

    part = jnp.dot(rounded[:R, :], grads[...], preferred_element_type=jnp.float32)
    work[...] = part * (1.0 / tokens_all)
    store_blocks(blocks, places, pl.ds(pl.multiple_of(step * columns, 128), columns), work)

    @pl.when(step == pl.num_programs(0) - 1)
    def _():
        cores = []
        for low in (0, R):
            some = flipped[pl.ds(pl.multiple_of(low + places[0] * 32, 32), 32), :]
            core = product(split(flipped[low : low + R, :]), split(some), LAST)
            cores.append(core * (1.0 / tokens_all))
        lane = lax.broadcasted_iota(jnp.int32, (R, 64), 1)
        squares = sq_one[...] + sq_two[...]
        traces = jnp.where(lane == 0, squares[0:1, 0:1], 0.0)
        traces = jnp.where(lane == 1, squares[8:9, 0:1], traces)
        rest = jnp.concatenate(cores + [traces], axis=1)
        work[:, :128] = rest
        store_blocks(blocks, places, pl.ds(whole, 128), work.at[:, :128])
        part = jnp.dot(rounded[R:, :], acts[...], preferred_element_type=jnp.float32)
        range_act[...] = part.T * (1.0 / tokens_all)
        for i in range(3):
            to = pl.ds(whole + 128 + i * R, R)
            store_blocks(blocks, places, to, range_act.at[16 * i :, :], 48)


def ranges(places, own, other, grads, acts, sq_one, sq_two, tokens_all):
    count, columns = grads.shape
    fixed = lambda shape: pl.BlockSpec(shape, lambda j, c: (0, 0))
    total = columns + 128 + 3 * R
    grid_spec = pltpu.PrefetchScalarGridSpec(
        num_scalar_prefetch=1,
        grid=(columns // TILE,),
        in_specs=[
            fixed(own.shape),
            fixed(other.shape),
            pl.BlockSpec((count, TILE), lambda j, c: (0, j)),
            fixed(acts.shape),
            fixed((16, 128)),
            fixed((16, 128)),
        ],
        out_specs=[fixed((R // 8, total))] * 8,
        scratch_shapes=[
            pltpu.VMEM((2 * R, count), jnp.float32),
            pltpu.VMEM((2 * R, count), jnp.bfloat16),
            pltpu.VMEM((acts.shape[1], R), jnp.float32),
            pltpu.VMEM((R, TILE), jnp.float32),
        ],
    )
    return call(
        functools.partial(ranges_kernel, tokens_all),
        [array(R // 8, total)] * 8,
        grid_spec=grid_spec,
        name="ranges",
    )(places, own, other, grads, acts, sq_one, sq_two)


def left_kernel(places, rows_act, weight, *refs):
    blocks, (high, low, work) = refs[:8], refs[8:]
    step = pl.program_id(0)
    columns = weight.shape[1]

    @pl.when(step == 0)
    def _():
        high[...], low[...] = split(rows_act[...].T)

    work[...] = product((high[...], low[...]), split(weight[...]), INNER)
    store_blocks(blocks, places, pl.ds(pl.multiple_of(step * columns, 128), columns), work)


def left_products(places, rows_act, weight):
    count, columns = weight.shape
    grid_spec = pltpu.PrefetchScalarGridSpec(
        num_scalar_prefetch=1,
        grid=(columns // TILE,),
        in_specs=[
            pl.BlockSpec((count, R), lambda j, c: (0, 0)),
            pl.BlockSpec((count, TILE), lambda j, c: (0, j)),
        ],
        out_specs=[pl.BlockSpec((R // 8, columns), lambda j, c: (0, 0))] * 8,
        scratch_shapes=[pltpu.VMEM((R, count), jnp.bfloat16)] * 2
        + [pltpu.VMEM((R, TILE), jnp.float32)],
    )
    return call(
        left_kernel, [array(R // 8, columns)] * 8, grid_spec=grid_spec, name="left_products"
    )(places, rows_act, weight)


def right_kernel(whole, *refs):
    extra, (weight, left, sums, cores, both) = refs[:7], refs[7:]

    @pl.when(pl.program_id(0) == 0)
    def _():
        sums[...] = jnp.zeros_like(sums)
        both[...] = jnp.zeros_like(both)
        cores[...] = extra[0][...].T[:64]
        blocks = [jnp.concatenate([extra[i][...], extra[i + 1][...]], axis=1) for i in (1, 3, 5)]
        pieces = split(jnp.concatenate(blocks))
        gram = product(pieces, pieces, ((0,), (0,)))
        for i in range(8):
            sums[i * 120 + 80 : i * 120 + 112, :] = gram[i * 32 : i * 32 + 32]
            sums[i * 120 + 112 : i * 120 + 120, :128] = extra[0][:8, :]

    ranges = split(whole[...])
    lines = [split(weight[...]), ranges, split(left[...])]
    lines = [jnp.concatenate([line[i] for line in lines]) for i in range(2)]
    total = stacked_product(lines, ranges, LAST)
    count = weight.shape[0]
    for i in range(8):
        at, gram = i * 120, count + i * 32
        sums[at : at + 48, :] += total[i * 48 : i * 48 + 48]
        sums[at + 48 : at + 80, :] += total[gram : gram + 32]
    both[...] += total[count + R :]


def right_products(gathered, weight, left):
    count, columns = weight.shape
    extra = lambda i: pl.BlockSpec((R, 128), lambda j: (0, columns // 128 + i))
    fixed = lambda shape: pl.BlockSpec(shape, lambda j: (0, 0))
    return call(
        right_kernel,
        [array(960, R), array(64, R), array(16, R)],
        grid=(columns // TILE,),
        in_specs=[pl.BlockSpec((R, TILE), lambda j: (0, j))]
        + [extra(i) for i in range(7)]
        + [
            pl.BlockSpec((count, TILE), lambda j: (0, j)),
            pl.BlockSpec((16, TILE), lambda j: (0, j)),
        ],
        out_specs=[fixed((960, R)), fixed((64, R)), fixed((16, R))],
        vmem=VMEM_MOST,
        name="right_products",
    )(*[gathered] * 8, weight, left)


def combine_kernel(counts, sums, cores, both, out, scale):
    damp_grad = DAMPING * sums[112:113, 64:65] / counts[0]
    damp_act = DAMPING * sums[112:113, 65:66] / counts[1]
    scale[...] = jnp.broadcast_to(1.0 / (damp_act * damp_grad), (8, 128))
    out[0:48, :] = sums[0:48, :]
    out[48:80, :] = damp_grad * cores[0:32, :] + sums[48:80, :]
    out[80:112, :] = damp_act * cores[32:64, :] + sums[80:112, :]
    out[112:128, :] = both[...]


def combine(sums, cores, both, counts):
    whole = pl.BlockSpec(memory_space=pltpu.VMEM)
    return call(
        functools.partial(combine_kernel, counts),
        [array(128, R), array(8, 128)],
        in_specs=[whole] * 3,
        out_specs=[whole] * 2,
        name="combine",
    )(sums, cores, both)


def pack_kernel(right, out):
    total = right[112:128, :]
    for i in range(1, 8):
        total += right[i * 128 + 112 : i * 128 + 128, :]
    for d in range(16):
        out[16 * d : 16 * d + 16, :] = total


def pack(right):
    whole = pl.BlockSpec(memory_space=pltpu.VMEM)
    return call(pack_kernel, array(R, R), in_specs=[whole], out_specs=whole, name="pack")(right)


def exact(left, right, dims):
    return lax.dot_general(
        left,
        right,
        (dims, ((), ())),
        precision=lax.Precision.HIGHEST,
        preferred_element_type=jnp.float32,
    )


def spread(value):
    return jnp.broadcast_to(value, (8, 2 * BLOCK))


def eliminate(matrices):
    sub = lax.broadcasted_iota(jnp.int32, (8, 2 * BLOCK), 0)
    count = BLOCK // 8
    groups = [[m[8 * i : 8 * i + 8] for i in range(count)] for m in matrices]
    for at in range(count):
        k = 8 * at
        for group in groups:
            tile = group[at]
            lines = [spread(tile[j : j + 1]) for j in range(8)]
            pivot = {
                (j, l): spread(lines[j][:, k + l : k + l + 1])
                for j in range(8)
                for l in range(j, 8)
            }
            scaled, factor = [], {}
            for j in range(8):
                inverse = 1.0 / pivot[j, j]
                scaled.append(lines[j] * inverse)
                for l in range(j + 1, 8):
                    factor[j, l] = pivot[j, l] * inverse
                    for m in range(l, 8):
                        pivot[l, m] = pivot[l, m] - factor[j, l] * pivot[j, m]
                    lines[l] = lines[l] - factor[j, l] * lines[j]
            for i in range(at + 1, count):
                value, sums, columns = group[i], None, []
                for j in range(8):
                    column = spread(value[:, k + j : k + j + 1])
                    for q in range(j):
                        column = column - columns[q] * factor[q, j]
                    columns.append(column)
                    term = column * scaled[j]
                    sums = term if sums is None else sums + term
                group[i] = value - sums
            for j in range(8):
                tile = jnp.where(sub == j, lines[j] * lax.rsqrt(pivot[j, j]), tile)
            group[at] = tile
    return [jnp.concatenate(group, axis=0) for group in groups]


def lower_inverses(work, outs):
    row = lax.broadcasted_iota(jnp.int32, (BLOCK, BLOCK), 0)
    column = lax.broadcasted_iota(jnp.int32, (BLOCK, BLOCK), 1)
    identity = jnp.where(row == column, 1.0, 0.0)
    for low in range(0, R, BLOCK):
        high = low + BLOCK
        done = eliminate(
            [jnp.concatenate([w[low:high, low:high], identity], axis=1) for w in work]
        )
        for w, corner, out in zip(work, done, outs):
            corner = jnp.where(row >= column, corner[:, BLOCK:], 0.0)
            line = exact(corner, w[low:high, :], INNER)
            out[low:high, :] = line[:, R:]
            if high < R:
                w[high:, :] -= exact(line[:, high:R], line, ((0,), (0,)))


def factor_kernel(right, inverse_act, inverse_grad, *work):
    row = lax.broadcasted_iota(jnp.int32, (R, R), 0)
    column = lax.broadcasted_iota(jnp.int32, (R, R), 1)
    identity = jnp.where(row == column, 1.0, 0.0)
    for w in work:
        w[:, R:] = identity
    for i in range(8):
        at, here = slice(i * 32, i * 32 + 32), i * 128
        work[0][at, :R] = right[here + 80 : here + 112, :]
        work[1][at, :R] = right[here + 48 : here + 80, :]
    lower_inverses(work, (inverse_act, inverse_grad))


def factors(right):
    whole = pl.BlockSpec(memory_space=pltpu.VMEM)
    return call(
        factor_kernel,
        [array(R, R), array(R, R)],
        in_specs=[whole],
        out_specs=[whole] * 2,
        scratch_shapes=[pltpu.VMEM((R, 2 * R), jnp.float32)] * 2,
        name="factors",
    )(right)


def applied(value, inverse):
    pieces = split(inverse)
    value = product(split(value), pieces, LAST)
    return product(split(value), pieces, INNER)


def last_kernel(
    left_sums, weight, range_grad, right, both, rows_act, inverse_act, inverse_grad, scale, out, sums, *pieces
):
    @pl.when(pl.program_id(0) == 0)
    def _():
        for i in range(8):
            sums[i * 48 : i * 48 + 48, :] = right[i * 128 : i * 128 + 48, :]
        solved = applied(rows_act[...], inverse_act[...])
        pieces[0][...], pieces[1][...] = split(solved)
        rest = sums[...] - product(split(solved), split(both[...]), INNER)
        pieces[2][...], pieces[3][...] = split(applied(rest, inverse_grad[...]))

    left = product((pieces[0][...], pieces[1][...]), split(left_sums[...]), INNER)
    range_pieces = split(range_grad[...])
    update = left + product((pieces[2][...], pieces[3][...]), range_pieces, INNER)
    out[...] = (weight[...] - update) * scale[0:1, 0:1]


def last_update(left_sums, weight, range_grad, *rest):
    count, columns = weight.shape
    return call(
        last_kernel,
        array(count, columns),
        grid=(columns // TILE,),
        in_specs=[
            pl.BlockSpec((R, TILE), lambda j: (0, j)),
            pl.BlockSpec((count, TILE), lambda j: (0, j)),
            pl.BlockSpec((R, TILE), lambda j: (0, j)),
        ]
        + [pl.BlockSpec(value.shape, lambda j: (0, 0)) for value in rest],
        out_specs=pl.BlockSpec((count, TILE), lambda j: (0, j)),
        scratch_shapes=[pltpu.VMEM((count, R), jnp.float32)]
        + [pltpu.VMEM((count, R), jnp.bfloat16)] * 4,
        vmem=VMEM_LAST,
        name="last_update",
    )(left_sums, weight, range_grad, *rest)


def hand_over_dp(value):
    return lax.all_to_all(value, "dp", 0, 0, tiled=True)


def body(acts, grads_out, sketch_in, sketch_out, weight_grad):
    tokens_all = acts.shape[0] * lax.axis_size("dp")
    columns = weight_grad.shape[1]
    core_id = lax.axis_index("tensor") % 2
    places = jnp.stack([tensor_chunk(), core_id, place("y"), place("z")]).astype(jnp.int32)

    part, sq_one = sketches(1 - core_id, grads_out, acts, sketch_out, sketch_in)
    other = swap_cores(part)
    part, sq_two = sketches(core_id, grads_out, acts, sketch_out, sketch_in)
    own = gather_four(scatter_four(part + other, "x"), "x")
    other = swap_cores(own)

    piece = scatter_dp(
        ranges(places, own, other, grads_out, acts, sq_one, sq_two, tokens_all)
    )
    gathered = lax.all_gather(piece, "dp", axis=0, tiled=True)

    at = columns + 128
    piece = jnp.concatenate([piece[:, at + i * R : at + i * R + R] for i in range(3)])
    rows_act = gather_rows(piece)

    piece = scatter_dp(left_products(places, rows_act, weight_grad))
    left_sums = lax.all_gather(piece, "dp", axis=0, tiled=True)

    counts = (float(tokens_all * FF), float(tokens_all * D))
    part, cores, both = right_products(gathered, weight_grad, piece)
    part, scale = combine(scatter_tensor(part), cores, both, counts)
    right = gather_tensor(part)
    both = lax.all_to_all(pack(right), "dp", 0, 0, tiled=True)

    inverse_act, inverse_grad = factors(right)
    return last_update(
        left_sums, weight_grad, gathered, right, both, rows_act, inverse_act, inverse_grad, scale
    )


def solution(mesh):
    return jax.shard_map(
        body,
        mesh=mesh,
        in_specs=(
            P("dp", "tensor"),
            P("dp", "tensor"),
            P("tensor", None),
            P("tensor", None),
            P("dp", "tensor"),
        ),
        out_specs=P("dp", "tensor"),
        check_vma=False,
    )
```
